32 devices in a mesh: dp: 8 (over z, core), seq: 4 (over y, x).
Axes of the slice: x: 2, y: 2, z: 4, core: 2. Of those that a mesh axis runs over, the one named last changes fastest.
Arguments:
- features: bfloat16 [8, 512, 1920], P('dp', 'seq'), may hold values from -48 to 48
- segment_ids: int32 [8, 512], P('dp'), may hold values from 0 to 7, never falling along the last dimension, each value on 1 to 128 neighbouring positions
- projections: bfloat16 [3, 1920, 1920], P(None, 'seq'), may hold values from -1 to 1
- cotangent: bfloat16 [8, 512, 1920], P('dp', 'seq'), may hold values from -6 to 6
Outputs:
- context: bfloat16 [8, 512, 1920], P('dp', 'seq')
- value_grad: float32 [1920, 1920], P('seq')
The draws below stay inside these ranges and needn't reach their ends.
Inputs may be any that keep to these rules, and one draw needn't show every extreme that they name: `segment_ids`: segment numbers never fall along a sequence; every utterance number appears, each utterance has 1 to 128 frames, and one has exactly 128.
All inputs are finite; a program needn't handle non-finite values.
Results may differ from the reference program's by a relative error of at most 0.011.
Values may be sent and summed in bfloat16 or wider, within the bound.
No kernel may reach another device: no remote copies, remote signals or barrier semaphores. Data moves between devices by JAX's collectives and lax.ppermute only.
A program may use at most 64 MiB of HBM per device.

```python
import math
import jax
import jax.numpy as jnp
import numpy as np
from jax import lax

D = 1920
HEADS = 16
HEAD = 120
FRAMES = 512
SEQS = 8
UTTS = 8
MOST = 128


def draw_features(key, part):
    base_key = jax.random.fold_in(key, 0)
    values = jnp.clip(jax.random.normal(base_key, (SEQS, FRAMES, D), jnp.float32), -6.0, 6.0)
    return values.astype(jnp.bfloat16)


def draw_projections(key, part):
    main_key = jax.random.fold_in(key, 0)
    draws = jax.random.normal(main_key, (3, D, D), jnp.float32) * D ** (-0.5)
    return jnp.clip(draws, -1.0, 1.0).astype(jnp.bfloat16)


def shard_levels(key, extent, cuts, smallest, high):
    loudness = 1.0
    for axis_at, parts in cuts:
        heights = jax.random.uniform(jax.random.fold_in(jax.random.fold_in(key, 6), axis_at), (parts,), jnp.float32, smallest / len(cuts), high / len(cuts))
        loudness = loudness * jnp.repeat(jnp.exp(heights), extent[axis_at] // parts).reshape((-1,) + (1,) * (len(extent) - 1 - axis_at))
    return loudness


def profile(count, total, most, skew):
    loads = [(1 << 20) // math.isqrt(standing ** skew) + 1 for standing in range(2, count + 1)]
    spare, given = total - most - (count - 1), [1] * (count - 1)
    while spare > 0:
        movable = [i for i in range(count - 1) if given[i] < most]
        pool, remaining = sum([loads[i] for i in movable]), spare
        for i in movable:
            more = min(most - given[i], max(1, remaining * loads[i] // pool), spare)
            given[i] = given[i] + more
            spare = spare - more
    return np.array([most] + given)


def uneven(key, count, total, most, slope):
    if count == 2:
        one = jax.random.randint(key, (), max(1, total - most), min(most, total - 1) + 1)
        return jnp.stack([one, total - one])
    sizes = jnp.asarray(profile(count, total, most, slope), jnp.int32)
    pairs = (count - 1) // 2
    giver, taker = sizes[1:1 + 2 * pairs:2], sizes[2:2 + 2 * pairs:2]
    slack = jnp.minimum(giver - 1, most - taker)
    passed = jax.random.randint(jax.random.fold_in(key, 1), (pairs,), 0, 1 << 20) % (slack + 1)
    sizes = sizes.at[1:1 + 2 * pairs:2].set(giver - passed).at[2:2 + 2 * pairs:2].set(taker + passed)
    return sizes[jax.random.permutation(jax.random.fold_in(key, 2), count)]


def noise(stream_key, shape, spread, reach, cuts=(), dtype=jnp.bfloat16):
    array = spread * jax.random.normal(stream_key, shape, jnp.float32)
    if cuts:
        array = array * shard_levels(stream_key, shape, cuts, -0.22, 0.18)
    return jnp.clip(array, -reach, reach).astype(dtype)


def setup_inputs(seed: int = 0) -> dict:
    splits = jax.random.split(jax.random.key(seed), 5)
    return {
        "features": draw_features(jax.random.fold_in(splits[4], 71), 0),
        "segment_ids": jax.vmap(lambda own: jnp.searchsorted(jnp.cumsum(uneven(own, UTTS, FRAMES, MOST, 2)), jnp.arange(FRAMES), side="right"))(jax.random.split(splits[1], SEQS)).reshape((SEQS, FRAMES)).astype(jnp.int32),
        "projections": draw_projections(jax.random.fold_in(splits[4], 71), 0),
        "cotangent": noise(splits[3], (SEQS, FRAMES, D), 1.0, 6.0, ((0, 8), (1, 4))),
    }


def reference(features, segment_ids, projections, cotangent):
    score_scale = HEAD ** -0.5

    def to_heads(matrix):
        return matrix.reshape(FRAMES, HEADS, HEAD).transpose(1, 0, 2)

    def from_heads(stacked):
        return stacked.transpose(1, 0, 2).reshape(FRAMES, D)

    def project(frames, matrix):
        return lax.dot_general(frames, matrix, (((1,), (1,)), ((), ())), preferred_element_type=jnp.float32).astype(jnp.bfloat16)

    def one_sequence(gradient_sum, sequence_item):
        frames, labels, upstream = sequence_item
        same_segment = labels[:, None] == labels[None, :]
        queries = project(frames, projections[0])
        key_rows = project(frames, projections[1])
        values = project(frames, projections[2])

        def single_head(head_item):
            head_queries, head_keys, head_values, head_upstream = head_item
            scores = jnp.dot(head_queries, head_keys.T, preferred_element_type=jnp.float32) * score_scale
            scores = jnp.where(same_segment, scores, -1e30)
            row_max = jnp.max(scores, axis=1, keepdims=True)
            exponent = jnp.exp(scores - row_max)
            attn_weights = (exponent / jnp.sum(exponent, axis=1, keepdims=True)).astype(jnp.bfloat16)
            context = jnp.dot(attn_weights, head_values, preferred_element_type=jnp.float32).astype(jnp.bfloat16)
            value_rows = jnp.dot(attn_weights.T, head_upstream, preferred_element_type=jnp.float32).astype(jnp.bfloat16)
            return context, value_rows

        context, value_rows = lax.map(single_head, (to_heads(queries), to_heads(key_rows), to_heads(values), to_heads(upstream)))
        context = from_heads(context)
        value_rows = from_heads(value_rows)
        gradient_sum = gradient_sum + jnp.dot(value_rows.T, frames, preferred_element_type=jnp.float32)
        return gradient_sum, context

    gradient_sum, context = lax.scan(one_sequence, jnp.zeros((D, D), jnp.float32), (features, segment_ids, cotangent))
    return context, gradient_sum / SEQS
```

```python
import jax
import jax.numpy as jnp
from jax import lax
from jax.sharding import PartitionSpec as P

HEAD = 120
BF16 = jnp.bfloat16
F32 = jnp.float32


def swap(array, axis, mask):
    return lax.ppermute(array, axis, [(i, i ^ mask) for i in range(lax.axis_size(axis))])


def gather_blocks(block, axis):
    n = lax.axis_size(axis)
    half = block.shape[0] // 2
    bits = [1 << b for b in range(n.bit_length() - 1)]
    held = [{0: block[:half]}, {0: block[half:]}]
    for step in range(len(bits)):
        for part, order in enumerate((bits, bits[::-1])):
            mask = order[step]
            for k in sorted(held[part]):
                held[part][k ^ mask] = swap(held[part][k], axis, mask)
    return [jnp.concatenate([held[0][k], held[1][k]], axis=0) for k in range(n)]


def line_sum(part, axis):
    n = lax.axis_size(axis)
    me = lax.axis_index(axis)
    core, place, length = me % 2, me // 2, n // 2
    rows = part.shape[0] // 2
    top, bottom = part[:rows], part[rows:]
    theirs = jnp.where(core == 0, bottom, top)
    mine = jnp.where(core == 0, top, bottom)
    total = (mine.astype(F32) + swap(theirs, axis, 1).astype(F32)).astype(BF16)
    middle = length // 2

    def hop(value, pairs):
        return lax.ppermute(value, axis, [(2 * a + c, 2 * b + c) for a, b in pairs for c in range(2)])

    for i in range(middle - 1):
        got = hop(total, [(i, i + 1), (length - 1 - i, length - 2 - i)])
        total = (total.astype(F32) + got.astype(F32)).astype(BF16)
    got = hop(total, [(middle - 1, middle), (middle, middle - 1)])
    total = (total.astype(F32) + got.astype(F32)).astype(BF16)
    for i in range(middle - 2, -1, -1):
        got = hop(total, [(i + 1, i), (length - 2 - i, length - 1 - i)])
        total = jnp.where((place == i) | (place == length - 1 - i), got, total)
    other = swap(total, axis, 1)
    return jnp.where(core == 0, total, other), jnp.where(core == 0, other, total)


def body(features, segment_ids, projections, cotangent):
    n = lax.axis_size("seq")
    me = lax.axis_index("seq")
    rows = features.shape[1]
    width = projections.shape[1]
    model = features.shape[2]
    heads = width // HEAD
    total = n * rows

    blocks = gather_blocks(features[0], "seq")
    shares = cotangent[0].reshape(rows, n, width).transpose(1, 0, 2)

    def share(k):
        return lax.dynamic_index_in_dim(shares, me ^ k, 0, keepdims=False)

    upstream = jnp.concatenate([share(0)] + [swap(share(k), "seq", k) for k in range(1, n)], axis=0)
    frames = jnp.concatenate(blocks, axis=0)
    ids = segment_ids[0].reshape(n, rows)
    labels = jnp.concatenate([lax.dynamic_index_in_dim(ids, me ^ k, 0, keepdims=False) for k in range(n)])
    same = labels[:, None] == labels[None, :]

    projected = jnp.einsum(
        "tf,cf->tc", frames, projections.reshape(3 * width, model), preferred_element_type=F32
    ).astype(BF16)

    def by_head(x):
        return x.reshape(total, heads, HEAD)

    queries, keys, values = (by_head(projected[:, i * width : (i + 1) * width]) for i in range(3))
    gradient = by_head(upstream)
    scores = jnp.einsum("qhe,khe->hqk", queries, keys, preferred_element_type=F32) * HEAD**-0.5
    scores = jnp.where(same[None], scores, -1e30)
    exponent = jnp.exp(scores - jnp.max(scores, axis=2, keepdims=True))
    weights = (exponent / jnp.sum(exponent, axis=2, keepdims=True)).astype(BF16)
    value_rows = jnp.einsum("hqk,qhe->khe", weights, gradient, preferred_element_type=F32).astype(BF16)

    sums = []
    for h in range(heads):
        piece = jnp.einsum("te,tf->ef", value_rows[:, h], frames, preferred_element_type=F32).astype(BF16)
        sums += line_sum(piece, "dp")
    value_grad = jnp.concatenate(sums, axis=0).astype(F32) / lax.axis_size("dp")

    context = jnp.einsum("hqk,khe->qhe", weights, values, preferred_element_type=F32).astype(BF16)
    context = context.reshape(n, rows, width)
    pieces = [context[0]] + [swap(context[k], "seq", k) for k in range(1, n)]
    stacked = jnp.stack(pieces)
    ordered = jnp.stack([lax.dynamic_index_in_dim(stacked, me ^ k, 0, keepdims=False) for k in range(n)])
    returned = ordered.transpose(1, 0, 2).reshape(rows, model)
    return returned[None], value_grad


def solution(mesh):
    in_specs = (P("dp", "seq", None), P("dp", None), P(None, "seq", None), P("dp", "seq", None))
    out_specs = (P("dp", "seq", None), P("seq", None))
    return jax.shard_map(body, mesh=mesh, in_specs=in_specs, out_specs=out_specs, check_vma=False)
```

```python
import functools

import jax
import jax.numpy as jnp
from jax import lax
from jax.experimental import pallas as pl
from jax.experimental.pallas import tpu as pltpu
from jax.sharding import PartitionSpec as P

HEAD = 120
PADDED = 128
BF16 = jnp.bfloat16
F32 = jnp.float32
VMEM = pl.BlockSpec(memory_space=pltpu.VMEM)
SMEM = pl.BlockSpec(memory_space=pltpu.SMEM)
LIMIT = pltpu.CompilerParams(vmem_limit_bytes=40 * 1024 * 1024)
CUTS = (1024, 896)


def swap(array, axis, mask):
    return lax.ppermute(array, axis, [(i, i ^ mask) for i in range(lax.axis_size(axis))])


def gather_blocks(block, axis):
    n = lax.axis_size(axis)
    if n != 4:
        return [block] + [swap(block, axis, k) for k in range(1, n)]
    half = block.shape[0] // 2
    by_x, by_y = swap(block, axis, 1), swap(block, axis, 2)
    top, bottom = swap(by_x[:half], axis, 2), swap(by_y[half:], axis, 1)
    return [block, by_x, by_y, jnp.concatenate([top, bottom], axis=0)]


def padded_head(rows, h):
    own = rows[h * HEAD : (h + 1) * HEAD]
    zeros = jnp.zeros((PADDED - HEAD, rows.shape[1]), F32)
    return jnp.concatenate([own, zeros], axis=0).astype(BF16)


def shares_kernel(me_ref, cot_ref, *refs):
    n = len(refs) - 1
    turned = refs[n]
    width = turned.shape[0] // n
    turned[...] = cot_ref[...].astype(F32).T
    for k in range(n):
        start = pl.multiple_of((me_ref[0] ^ k) * width, 8)
        refs[k][...] = turned[pl.ds(start, width), :].astype(BF16)


def cotangent_shares(me, cotangent, n):
    rows, model = cotangent.shape
    return pl.pallas_call(
        shares_kernel,
        out_shape=[jax.ShapeDtypeStruct((model // n, rows), BF16)] * n,
        in_specs=[SMEM, VMEM],
        out_specs=[VMEM] * n,
        scratch_shapes=[pltpu.VMEM((model, rows), F32)],
        compiler_params=LIMIT,
        name="cotangent_shares",
    )(me, cotangent)


def project_into(w_ref, frames, out_ref):
    heads = out_ref.shape[1]

    def one(t, carry):
        rows = lax.dot_general(w_ref[t], frames, (((1,), (1,)), ((), ())), preferred_element_type=F32)
        for h in range(heads):
            out_ref[t, h] = padded_head(rows, h)
        return carry

    lax.fori_loop(0, 3, one, 0)


def project_kernel(w_ref, *refs):
    project_into(w_ref, jnp.concatenate([r[...] for r in refs[:-1]], axis=0), refs[-1])


def project(weights, blocks):
    rows = sum(b.shape[0] for b in blocks)
    heads = weights.shape[1] // HEAD
    flops = 2 * 3 * weights.shape[1] * weights.shape[2] * rows
    return pl.pallas_call(
        project_kernel,
        out_shape=jax.ShapeDtypeStruct((3, heads, PADDED, rows), BF16),
        in_specs=[VMEM] * (1 + len(blocks)),
        out_specs=VMEM,
        compiler_params=LIMIT,
        cost_estimate=pl.CostEstimate(flops=flops, bytes_accessed=weights.size * 2, transcendentals=0),
        name="project",
    )(weights, *blocks)


def attend_kernel(members, n, parts, last, core_ref, row_ref, col_ref, *refs):
    refs = list(refs)

    def take(count):
        out = refs[:count]
        del refs[:count]
        return out

    pieces = take(parts)
    cots = take(n)
    blocks = take(n)
    earlier = take(1)[0] if last else None
    theirs = take(len(CUTS))
    mine = take(len(CUTS))
    contexts = take(n if last else 1)
    total = row_ref.shape[1]
    rows = blocks[0].shape[0]
    step = min(512, total)
    core = core_ref[0]
    upstream = jnp.concatenate([c[...] for c in cots], axis=1).astype(F32)
    results, sums = [], []
    for h in members:
        queries, keys, values = (
            jnp.concatenate([p[t, h] for p in pieces], axis=1) for t in range(3)
        )
        gradient = padded_head(upstream, h)
        columns, value_rows = [], None
        for at in range(0, total, step):
            scores = lax.dot_general(
                keys, queries[:, at : at + step], (((0,), (0,)), ((), ())), preferred_element_type=F32
            )
            same = jnp.concatenate(
                [col_ref[...] == row_ref[:, c : c + PADDED] for c in range(at, at + step, PADDED)], axis=1
            )
            scores = jnp.where(same, scores * HEAD**-0.5, -1e30)
            exponent = jnp.exp(scores - jnp.max(scores, axis=0, keepdims=True))
            inverse = 1.0 / jnp.sum(exponent, axis=0, keepdims=True)
            weights = (exponent * inverse).astype(BF16)
            columns.append(jnp.dot(values, weights, preferred_element_type=F32))
            term = lax.dot_general(
                gradient[:, at : at + step], weights, (((1,), (1,)), ((), ())), preferred_element_type=F32
            )
            value_rows = term if value_rows is None else value_rows + term
        sums.append(value_rows.astype(BF16))
        results.append(jnp.concatenate(columns, axis=1)[:HEAD])
    start = 0
    for i, cut in enumerate(CUTS):
        frames = jnp.concatenate([b[:, start : start + cut] for b in blocks], axis=0)
        start += cut
        grads = [jnp.dot(s, frames, preferred_element_type=F32)[:HEAD].astype(BF16) for s in sums]
        if len(grads) == 2:
            theirs[i][...] = jnp.where(core == 0, grads[1], grads[0])
            mine[i][...] = jnp.where(core == 0, grads[0], grads[1])
        else:
            theirs[i][...] = grads[0]
    if not last:
        for i, result in enumerate(results):
            contexts[0][i] = result
        return
    if earlier is None:
        ordered = results
    else:
        count = earlier.shape[0]
        ordered = [earlier[i] for i in range(count)] + results
        half = len(ordered) // 2
        ordered = [ordered[2 * (i % half) + i // half] for i in range(len(ordered))]
    stacked = jnp.concatenate(ordered, axis=0)
    for k in range(n):
        contexts[k][...] = stacked[:, k * rows : (k + 1) * rows].astype(BF16)


def attend(members, last, core, row, col, pieces, cots, blocks, earlier):
    n, width, rows = len(cots), cots[0].shape[0], cots[0].shape[1]
    total = n * rows
    chunks = [jax.ShapeDtypeStruct((HEAD, c), BF16) for c in CUTS]
    if last:
        contexts = [jax.ShapeDtypeStruct((width, rows), BF16)] * n
    else:
        contexts = [jax.ShapeDtypeStruct((len(members), HEAD, total), F32)]
    extra = [] if earlier is None else [earlier]
    model = blocks[0].shape[1]
    flops = 2 * len(members) * PADDED * total * (3 * total + model)
    outs = pl.pallas_call(
        functools.partial(
            attend_kernel, members, n, len(pieces), last
        ) if earlier is not None or not last else functools.partial(attend_alone, members, n, len(pieces)),
        out_shape=chunks * 2 + contexts,
        in_specs=[SMEM] + [VMEM] * (2 + len(pieces) + 2 * n + len(extra)),
        out_specs=[VMEM] * (2 * len(CUTS) + len(contexts)),
        compiler_params=LIMIT,
        cost_estimate=pl.CostEstimate(flops=flops, bytes_accessed=2 * total * model, transcendentals=0),
        name="attend",
    )(core, row, col, *pieces, *cots, *blocks, *extra)
    return outs[: len(CUTS)], outs[len(CUTS) : 2 * len(CUTS)], outs[2 * len(CUTS) :]


def attend_alone(members, n, parts, core_ref, row_ref, col_ref, *refs):
    inputs = parts + 2 * n
    attend_kernel(members, n, parts, True, core_ref, row_ref, col_ref, *refs[:inputs], None, *refs[inputs:])


def context_kernel(me_ref, *refs):
    n = len(refs) - 2
    out, turned = refs[n], refs[n + 1]
    width = refs[0].shape[0]
    for k in range(n):
        start = pl.multiple_of((me_ref[0] ^ k) * width, 8)
        turned[pl.ds(start, width), :] = refs[k][...].astype(F32)
    out[...] = turned[...].T.astype(BF16)


def assemble_context(me, pieces):
    n, (width, rows) = len(pieces), pieces[0].shape
    return pl.pallas_call(
        context_kernel,
        out_shape=jax.ShapeDtypeStruct((rows, n * width), BF16),
        in_specs=[SMEM] + [VMEM] * n,
        out_specs=VMEM,
        scratch_shapes=[pltpu.VMEM((n * width, rows), F32)],
        compiler_params=LIMIT,
        name="assemble_context",
    )(me, *pieces)


def final_kernel(groups, scale, core_ref, *refs):
    out = refs[-1]
    at = pl.program_id(0)
    for i in range(2 * groups):
        owner, group = i // groups, i % groups

        @pl.when(at == i)
        def _():
            start = 0
            for c, cut in enumerate(CUTS):
                own, other = refs[2 * (group * len(CUTS) + c)], refs[2 * (group * len(CUTS) + c) + 1]
                out[:, start : start + cut] = scale * jnp.where(
                    core_ref[0] == owner, own[...].astype(F32), other[...].astype(F32)
                )
                start += cut


def final(core, sums, scale, model):
    groups = len(sums) // len(CUTS)
    flat = [x for pair in sums for x in pair]
    return pl.pallas_call(
        functools.partial(final_kernel, groups, scale),
        grid=(2 * groups,),
        out_shape=jax.ShapeDtypeStruct((2 * groups * HEAD, model), F32),
        in_specs=[SMEM] + [VMEM] * len(flat),
        out_specs=pl.BlockSpec((HEAD, model), lambda i: (i, 0)),
        compiler_params=LIMIT,
        name="final",
    )(core, *flat)


def line_sum(theirs, mine, axis):
    n = lax.axis_size(axis)
    length = n // 2
    place = lax.axis_index(axis) // 2
    total = (mine.astype(F32) + swap(theirs, axis, 1).astype(F32)).astype(BF16)
    middle = length // 2

    def hop(value, pairs):
        return lax.ppermute(value, axis, [(2 * a + c, 2 * b + c) for a, b in pairs for c in range(2)])

    for i in range(middle - 1):
        got = hop(total, [(i, i + 1), (length - 1 - i, length - 2 - i)])
        total = (total.astype(F32) + got.astype(F32)).astype(BF16)
    got = hop(total, [(middle - 1, middle), (middle, middle - 1)])
    total = (total.astype(F32) + got.astype(F32)).astype(BF16)
    for i in range(middle - 2, -1, -1):
        got = hop(total, [(i + 1, i), (length - 2 - i, length - 1 - i)])
        total = jnp.where((place == i) | (place == length - 1 - i), got, total)
    return total, swap(total, axis, 1)


def body(features, segment_ids, projections, cotangent):
    n = lax.axis_size("seq")
    me = lax.axis_index("seq")
    core = lax.axis_index("dp") % 2
    me_ref, core_ref = me.reshape(1).astype(jnp.int32), core.reshape(1).astype(jnp.int32)
    rows, model = features.shape[1:]
    heads = projections.shape[1] // HEAD
    total = n * rows
    scale = 1.0 / lax.axis_size("dp")

    blocks = gather_blocks(features[0], "seq")
    shares = cotangent_shares(me_ref, cotangent[0], n)
    cots = [shares[0]] + [swap(shares[k], "seq", k) for k in range(1, n)]
    ids = segment_ids[0].reshape(n, rows)
    labels = jnp.concatenate([lax.dynamic_index_in_dim(ids, me ^ k, 0, keepdims=False) for k in range(n)])
    row = labels[None, :]
    col = jnp.broadcast_to(labels[:, None], (total, PADDED))
    pieces = [project(projections, blocks[:1])]
    if n > 2:
        pieces.append(project(projections, blocks[1 : n - 1]))
    pieces.append(project(projections, blocks[n - 1 :]))

    if heads % 2:
        groups = [(h,) for h in range(heads)]
    else:
        groups = [(g, g + heads // 2) for g in range(heads // 2)]
    earlier, sums = None, []
    for g, members in enumerate(groups):
        last = g == len(groups) - 1
        theirs, mine, contexts = attend(members, last, core_ref, row, col, pieces, cots, blocks, earlier)
        if not last:
            earlier = contexts[0] if earlier is None else jnp.concatenate([earlier, contexts[0]])
        for i in range(len(CUTS)):
            if heads % 2:
                half = HEAD // 2
                low, high = theirs[i][:half], theirs[i][half:]
                own, other = line_sum(jnp.where(core == 0, high, low), jnp.where(core == 0, low, high), "dp")
                sums.append(jnp.where(core == 0, jnp.concatenate([own, other]), jnp.concatenate([other, own])))
            else:
                sums.append(line_sum(theirs[i], mine[i], "dp"))
    if heads % 2:
        cuts = len(CUTS)
        value_grad = jnp.concatenate(
            [jnp.concatenate(sums[g * cuts : (g + 1) * cuts], axis=1) for g in range(heads)]
        ).astype(F32) * scale
    else:
        value_grad = final(core_ref, sums, scale, model)

    received = [contexts[0]] + [swap(contexts[k], "seq", k) for k in range(1, n)]
    return assemble_context(me_ref, received)[None], value_grad


def solution(mesh):
    in_specs = (P("dp", "seq", None), P("dp", None), P(None, "seq", None), P("dp", "seq", None))
    out_specs = (P("dp", "seq", None), P("seq", None))
    return jax.shard_map(body, mesh=mesh, in_specs=in_specs, out_specs=out_specs, check_vma=False)
```

```python
import functools

import jax
import jax.numpy as jnp
from jax import lax
from jax.experimental import pallas as pl
from jax.experimental.pallas import tpu as pltpu
from jax.sharding import PartitionSpec as P

HEAD = 120
PADDED = 128
BF16 = jnp.bfloat16
F32 = jnp.float32
VMEM = pl.BlockSpec(memory_space=pltpu.VMEM)
ANY = pl.BlockSpec(memory_space=pl.ANY)
SMEM = pl.BlockSpec(memory_space=pltpu.SMEM)
LIMIT = pltpu.CompilerParams(vmem_limit_bytes=16 * 1024 * 1024)
SMALL = pl.CostEstimate(flops=1000, bytes_accessed=1000, transcendentals=0)
CUTS = (1024, 896)


def swap(array, axis, mask):
    return lax.ppermute(array, axis, [(i, i ^ mask) for i in range(lax.axis_size(axis))])


def halves_kernel(x_ref, top_ref, bottom_ref, sems):
    half = top_ref.shape[0]
    copies = [
        pltpu.make_async_copy(x_ref.at[pl.ds(i * half, half)], out, sems.at[i])
        for i, out in enumerate((top_ref, bottom_ref))
    ]
    for copy in copies:
        copy.start()
    for copy in copies:
        copy.wait()


def halves(block):
    rows, model = block.shape
    return pl.pallas_call(
        halves_kernel,
        out_shape=[jax.ShapeDtypeStruct((rows // 2, model), BF16)] * 2,
        in_specs=[ANY],
        out_specs=[VMEM] * 2,
        scratch_shapes=[pltpu.SemaphoreType.DMA((2,))],
        compiler_params=LIMIT,
        name="halves",
    )(block)


def gather_blocks(block, axis):
    n = lax.axis_size(axis)
    if n != 4:
        return [[block]] + [[swap(block, axis, k)] for k in range(1, n)]
    top, bottom = halves(block)
    top_x, bottom_y = swap(top, axis, 1), swap(bottom, axis, 2)
    bottom_x, top_y = swap(bottom, axis, 1), swap(top, axis, 2)
    top_xy, bottom_xy = swap(top_x, axis, 2), swap(bottom_y, axis, 1)
    return [[block], [top_x, bottom_x], [top_y, bottom_y], [top_xy, bottom_xy]]


def padded_head(rows, h):
    own = rows[h * HEAD : (h + 1) * HEAD]
    zeros = jnp.zeros((PADDED - HEAD, rows.shape[1]), F32)
    return jnp.concatenate([own, zeros], axis=0).astype(BF16)


def shares_kernel(me_ref, cot_ref, *refs):
    n = len(refs) - 1
    turned = refs[n]
    width = turned.shape[0] // n
    turned[...] = cot_ref[...].astype(F32).T
    for k in range(n):
        start = pl.multiple_of((me_ref[0] ^ k) * width, 8)
        refs[k][...] = turned[pl.ds(start, width), :].astype(BF16)


def cotangent_shares(me, cotangent, n):
    rows, model = cotangent.shape
    return pl.pallas_call(
        shares_kernel,
        out_shape=[jax.ShapeDtypeStruct((model // n, rows), BF16)] * n,
        in_specs=[SMEM, VMEM],
        out_specs=[VMEM] * n,
        scratch_shapes=[pltpu.VMEM((model, rows), F32)],
        compiler_params=LIMIT,
        name="cotangent_shares",
    )(me, cotangent)


def project_kernel(first, w_ref, *refs):
    out_ref = refs[-1]
    count, heads = out_ref.shape[:2]
    frames = jnp.concatenate([r[...] for r in refs[:-1]], axis=0)

    def one(t, carry):
        rows = lax.dot_general(
            w_ref[first + t], frames, (((1,), (1,)), ((), ())), preferred_element_type=F32
        )
        for h in range(heads):
            out_ref[t, h] = padded_head(rows, h)
        return carry

    lax.fori_loop(0, count, one, 0)


def project(weights, first, count, blocks):
    rows = sum(b.shape[0] for b in blocks)
    heads = weights.shape[1] // HEAD
    flops = 2 * count * weights.shape[1] * weights.shape[2] * rows
    return pl.pallas_call(
        functools.partial(project_kernel, first),
        out_shape=jax.ShapeDtypeStruct((count, heads, PADDED, rows), BF16),
        in_specs=[VMEM] * (1 + len(blocks)),
        out_specs=VMEM,
        compiler_params=LIMIT,
        cost_estimate=pl.CostEstimate(flops=flops, bytes_accessed=weights.size * 2, transcendentals=0),
        name="project",
    )(weights, *blocks)


def weights_kernel(members, row_ref, col_ref, *refs):
    out_ref = refs[-1]
    total = row_ref.shape[1]
    step = max(PADDED, min(total, 512 * 512 // total))
    for place, h in enumerate(members):
        queries, keys = (jnp.concatenate([p[t, h] for p in refs[:-1]], axis=1) for t in range(2))
        for at in range(0, total, step):
            scores = lax.dot_general(
                keys, queries[:, at : at + step], (((0,), (0,)), ((), ())), preferred_element_type=F32
            )
            same = jnp.concatenate(
                [col_ref[...] == row_ref[:, c : c + PADDED] for c in range(at, at + step, PADDED)], axis=1
            )
            scores = jnp.where(same, scores * HEAD**-0.5, -1e30)
            exponent = jnp.exp(scores - jnp.max(scores, axis=0, keepdims=True))
            inverse = 1.0 / jnp.sum(exponent, axis=0, keepdims=True)
            out_ref[place, :, at : at + step] = (exponent * inverse).astype(BF16)


def attention_weights(members, row, col, pieces):
    total = row.shape[1]
    return pl.pallas_call(
        functools.partial(weights_kernel, members),
        out_shape=jax.ShapeDtypeStruct((len(members), total, total), BF16),
        in_specs=[VMEM] * (2 + len(pieces)),
        out_specs=VMEM,
        compiler_params=LIMIT,
        cost_estimate=pl.CostEstimate(
            flops=2 * len(members) * PADDED * total * total,
            bytes_accessed=2 * len(members) * total * total,
            transcendentals=len(members) * total * total,
        ),
        name="attention_weights",
    )(row, col, *pieces)


def gradient_kernel(members, n, core_ref, weights_ref, *refs):
    cots, blocks, (theirs, mine) = refs[:n], refs[n:-2], refs[-2:]
    upstream = jnp.concatenate([c[...] for c in cots], axis=1).astype(F32)
    sums = []
    for place, h in enumerate(members):
        rows = lax.dot_general(
            padded_head(upstream, h), weights_ref[place], (((1,), (1,)), ((), ())), preferred_element_type=F32
        )
        sums.append(rows.astype(BF16))
    start = 0
    for cut in CUTS:
        at = slice(start, start + cut)
        frames = jnp.concatenate([b[:, at] for b in blocks], axis=0)
        start += cut
        grads = [jnp.dot(s, frames, preferred_element_type=F32)[:HEAD].astype(BF16) for s in sums]
        if len(grads) == 2:
            theirs[:, at] = jnp.where(core_ref[0] == 0, grads[1], grads[0])
            mine[:, at] = jnp.where(core_ref[0] == 0, grads[0], grads[1])
        else:
            theirs[:, at] = grads[0]
            mine[:, at] = grads[0]


def gradient(members, core, weights, cots, blocks):
    total, model = weights.shape[1], blocks[0].shape[1]
    return pl.pallas_call(
        functools.partial(gradient_kernel, members, len(cots)),
        out_shape=[jax.ShapeDtypeStruct((HEAD, model), BF16)] * 2,
        in_specs=[SMEM] + [VMEM] * (1 + len(cots) + len(blocks)),
        out_specs=[VMEM] * 2,
        compiler_params=LIMIT,
        cost_estimate=pl.CostEstimate(
            flops=2 * len(members) * PADDED * total * (total + model),
            bytes_accessed=2 * total * model,
            transcendentals=0,
        ),
        name="gradient",
    )(core, weights, *cots, *blocks)


def context_kernel(groups, values_ref, *refs):
    weights, outs = refs[: len(groups)], refs[len(groups) :]
    rows = outs[0].shape[1]
    found = {}
    for members, ref in zip(groups, weights):
        for place, h in enumerate(members):
            found[h] = jnp.dot(values_ref[0, h], ref[place], preferred_element_type=F32)[:HEAD]
    stacked = jnp.concatenate([found[h] for h in sorted(found)], axis=0)
    for k, out in enumerate(outs):
        out[...] = stacked[:, k * rows : (k + 1) * rows].astype(BF16)


def contexts_of(groups, values, weights, n):
    heads, total = values.shape[1], values.shape[3]
    return pl.pallas_call(
        functools.partial(context_kernel, groups),
        out_shape=[jax.ShapeDtypeStruct((heads * HEAD, total // n), BF16)] * n,
        in_specs=[VMEM] * (1 + len(weights)),
        out_specs=[VMEM] * n,
        compiler_params=LIMIT,
        cost_estimate=pl.CostEstimate(
            flops=2 * heads * PADDED * total * total, bytes_accessed=2 * heads * total * total, transcendentals=0
        ),
        name="contexts",
    )(values, *weights)


def assemble_kernel(me_ref, *refs):
    n = len(refs) - 3
    out, token, turned = refs[n:]
    width = refs[0].shape[0]
    for k in range(n):
        start = pl.multiple_of((me_ref[0] ^ k) * width, 8)
        turned[pl.ds(start, width), :] = refs[k][...].astype(F32)
    out[...] = turned[...].T.astype(BF16)
    token[...] = jnp.zeros_like(token)


def assemble_context(me, pieces):
    n, (width, rows) = len(pieces), pieces[0].shape
    return pl.pallas_call(
        assemble_kernel,
        out_shape=[jax.ShapeDtypeStruct((rows, n * width), BF16), jax.ShapeDtypeStruct((8, PADDED), F32)],
        in_specs=[SMEM] + [VMEM] * n,
        out_specs=[VMEM] * 2,
        scratch_shapes=[pltpu.VMEM((n * width, rows), F32)],
        compiler_params=LIMIT,
        cost_estimate=SMALL,
        name="assemble_context",
    )(me, *pieces)


def final_kernel(groups, scale, core_ref, bit_ref, *refs):
    out = refs[-1]
    at = pl.program_id(0)
    half = refs[0].shape[1]
    for i in range(2 * groups):
        owner, group = i // groups, i % groups

        @pl.when(at == i)
        def _():
            kept, got, far_kept, far_got = refs[4 * group : 4 * group + 4]
            near = core_ref[0] == owner
            first = jnp.where(near, kept[...].astype(F32), far_kept[...].astype(F32)) * scale
            second = jnp.where(near, got[...].astype(F32), far_got[...].astype(F32)) * scale
            low = bit_ref[0] == 0
            out[:, :half] = jnp.where(low, first, second)
            out[:, half:] = jnp.where(low, second, first)


def final(core, bit, sums, scale, model):
    groups = len(sums)
    flat = [x for four in sums for x in four]
    return pl.pallas_call(
        functools.partial(final_kernel, groups, scale),
        grid=(2 * groups,),
        out_shape=jax.ShapeDtypeStruct((2 * groups * HEAD, model), F32),
        in_specs=[SMEM, SMEM] + [VMEM] * len(flat),
        out_specs=pl.BlockSpec((HEAD, model), lambda i: (i, 0)),
        compiler_params=LIMIT,
        cost_estimate=SMALL,
        name="final",
    )(core, bit, *flat)


def add_kernel(a_ref, b_ref, *refs):
    refs[-1][...] = (a_ref[...].astype(F32) + b_ref[...].astype(F32)).astype(BF16)


def add(a, b, *after):
    return pl.pallas_call(
        add_kernel,
        out_shape=jax.ShapeDtypeStruct(a.shape, BF16),
        in_specs=[VMEM, VMEM] + [ANY] * len(after),
        out_specs=VMEM,
        compiler_params=LIMIT,
        cost_estimate=SMALL,
        name="add",
    )(a, b, *after)


def split_sum_kernel(bit_ref, a_ref, b_ref, *refs):
    sent, kept = refs[-2:]
    total = a_ref[...].astype(F32) + b_ref[...].astype(F32)
    half = sent.shape[1]
    first, second = total[:, :half], total[:, half:]
    low = bit_ref[0] == 0
    sent[...] = jnp.where(low, second, first).astype(BF16)
    kept[...] = jnp.where(low, first, second).astype(BF16)


def split_sum(bit, a, b, *after):
    rows, columns = a.shape
    return pl.pallas_call(
        split_sum_kernel,
        out_shape=[jax.ShapeDtypeStruct((rows, columns // 2), BF16)] * 2,
        in_specs=[SMEM, VMEM, VMEM] + [ANY] * len(after),
        out_specs=[VMEM] * 2,
        compiler_params=LIMIT,
        cost_estimate=SMALL,
        name="split_sum",
    )(bit, a, b, *after)


def cube_sums(parts, bit, axis, after, late):
    n = lax.axis_size(axis)
    masks = [1 << b for b in range(2, n.bit_length() - 1)]
    split, previous = [], []
    for k, (theirs, mine) in enumerate(parts):
        previous = split_sum(bit, mine, swap(theirs, axis, 1), *previous)
        split.append(previous)
    kept = []
    for k, (sent, own) in enumerate(split):
        wait = [kept[-1]] if kept else list(after) + [split[-1][1]]
        kept.append(add(own, swap(sent, axis, 2), *wait))
    out = []
    for mask in masks[:-1]:
        kept = [add(own, swap(own, axis, mask)) for own in kept]
    for k, own in enumerate(kept):
        wait = out[-1][1:3] if out else ()
        total = add(own, swap(own, axis, masks[-1]), *wait, *(late if k == len(kept) - 1 else ()))
        got = swap(total, axis, 2)
        out.append((total, got, swap(total, axis, 1), swap(got, axis, 1)))
    return out


def body(features, segment_ids, projections, cotangent):
    n = lax.axis_size("seq")
    me = lax.axis_index("seq")
    core, bit = lax.axis_index("dp") % 2, lax.axis_index("dp") // 2 % 2
    me_ref, core_ref, bit_ref = (x.reshape(1).astype(jnp.int32) for x in (me, core, bit))
    rows, model = features.shape[1:]
    heads = projections.shape[1] // HEAD
    total = n * rows
    scale = 1.0 / lax.axis_size("dp")

    blocks = gather_blocks(features[0], "seq")
    shares = cotangent_shares(me_ref, cotangent[0], n)
    cots = [shares[0]] + [swap(shares[k], "seq", k) for k in range(1, n)]
    ids = segment_ids[0].reshape(n, rows)
    labels = jnp.concatenate([lax.dynamic_index_in_dim(ids, me ^ k, 0, keepdims=False) for k in range(n)])
    row = labels[None, :]
    col = jnp.broadcast_to(labels[:, None], (total, PADDED))

    def flat(some):
        return [part for block in some for part in block]

    pieces = [project(projections, 0, 2, flat(some)) for some in (blocks[:1], blocks[1 : n - 1], blocks[n - 1 :]) if some]
    frames = flat(blocks)
    if heads % 2:
        groups = [(h,) for h in range(heads)]
    else:
        groups = [(g, g + heads // 2) for g in range(heads // 2)]
    weights = [attention_weights(members, row, col, pieces) for members in groups]
    parts = []
    for members, ready in zip(groups, weights):
        theirs, mine = gradient(members, core_ref, ready, cots, frames)
        if heads % 2:
            half = HEAD // 2
            low, high = mine[:half], mine[half:]
            theirs, mine = jnp.where(core == 0, high, low), jnp.where(core == 0, low, high)
        parts.append((theirs, mine))
    contexts = contexts_of(groups, project(projections, 2, 1, frames), weights, n)
    received = [contexts[0]] + [swap(contexts[k], "seq", k) for k in range(1, n)]
    context, token = assemble_context(me_ref, received)
    sums = cube_sums(parts, bit_ref, "dp", contexts[:1], [token])
    if heads % 2:
        low = bit == 0
        whole = []
        for kept, got, far_kept, far_got in sums:
            near = jnp.where(low, jnp.concatenate([kept, got], axis=1), jnp.concatenate([got, kept], axis=1))
            far = jnp.where(
                low, jnp.concatenate([far_kept, far_got], axis=1), jnp.concatenate([far_got, far_kept], axis=1)
            )
            whole.append(jnp.where(core == 0, jnp.concatenate([near, far]), jnp.concatenate([far, near])))
        value_grad = jnp.concatenate(whole).astype(F32) * scale
    else:
        value_grad = final(core_ref, bit_ref, sums, scale, model)
    return context[None], value_grad


def solution(mesh):
    in_specs = (P("dp", "seq", None), P("dp", None), P(None, "seq", None), P("dp", "seq", None))
    out_specs = (P("dp", "seq", None), P("seq", None))
    return jax.shard_map(body, mesh=mesh, in_specs=in_specs, out_specs=out_specs, check_vma=False)
```

```python
import functools

import jax
import jax.numpy as jnp
from jax import lax
from jax.experimental import pallas as pl
from jax.experimental.pallas import tpu as pltpu
from jax.sharding import PartitionSpec as P

HEAD = 120
PADDED = 128
BF16 = jnp.bfloat16
F32 = jnp.float32
VMEM = pl.BlockSpec(memory_space=pltpu.VMEM)
ANY = pl.BlockSpec(memory_space=pl.ANY)
HBM = pl.BlockSpec(memory_space=pltpu.HBM)
SMEM = pl.BlockSpec(memory_space=pltpu.SMEM)
LIMIT = pltpu.CompilerParams(vmem_limit_bytes=16 * 1024 * 1024)
SMALL = pl.CostEstimate(flops=1000, bytes_accessed=1000, transcendentals=0)
CUTS = (512, 896, 512)


def swap(array, axis, mask):
    return lax.ppermute(array, axis, [(i, i ^ mask) for i in range(lax.axis_size(axis))])


def halves_kernel(x_ref, top_ref, bottom_ref, sems):
    half = top_ref.shape[0]
    copies = [
        pltpu.make_async_copy(x_ref.at[pl.ds(i * half, half)], out, sems.at[i])
        for i, out in enumerate((top_ref, bottom_ref))
    ]
    for copy in copies:
        copy.start()
    for copy in copies:
        copy.wait()


def halves(block):
    rows, model = block.shape
    return pl.pallas_call(
        halves_kernel,
        out_shape=[jax.ShapeDtypeStruct((rows // 2, model), BF16)] * 2,
        in_specs=[HBM],
        out_specs=[VMEM] * 2,
        scratch_shapes=[pltpu.SemaphoreType.DMA((2,))],
        compiler_params=LIMIT,
        name="halves",
    )(block)


def gather_blocks(block, axis):
    n = lax.axis_size(axis)
    if n != 4:
        return [[block]] + [[swap(block, axis, k)] for k in range(1, n)]
    top, bottom = halves(block)
    top_x, bottom_y = swap(top, axis, 1), swap(bottom, axis, 2)
    bottom_x, top_y = swap(bottom, axis, 1), swap(top, axis, 2)
    top_xy, bottom_xy = swap(top_x, axis, 2), swap(bottom_y, axis, 1)
    return [[block], [top_x, bottom_x], [top_y, bottom_y], [top_xy, bottom_xy]]


def padded_head(rows, h):
    own = rows[h * HEAD : (h + 1) * HEAD]
    zeros = jnp.zeros((PADDED - HEAD, rows.shape[1]), F32)
    return jnp.concatenate([own, zeros], axis=0).astype(BF16)


def shares_kernel(n, me_ref, cot_ref, *refs):
    outs, (loaded, turned, sem) = refs[-n - 3 : -3], refs[-3:]
    copy = pltpu.make_async_copy(cot_ref, loaded, sem)
    copy.start()
    copy.wait()
    turned[...] = loaded[...].astype(F32).T
    width = outs[0].shape[0]
    for k in range(n):
        start = pl.multiple_of((me_ref[0] ^ k) * width, 8)
        outs[k][...] = turned[pl.ds(start, width), :].astype(BF16)


def cotangent_shares(me, cotangent, n, after):
    rows, model = cotangent.shape
    return pl.pallas_call(
        functools.partial(shares_kernel, n),
        out_shape=[jax.ShapeDtypeStruct((model // n, rows), BF16)] * n,
        in_specs=[SMEM, HBM] + [ANY] * len(after),
        out_specs=[VMEM] * n,
        scratch_shapes=[
            pltpu.VMEM((rows, model), BF16),
            pltpu.VMEM((model, rows), F32),
            pltpu.SemaphoreType.DMA,
        ],
        compiler_params=LIMIT,
        name="cotangent_shares",
    )(me, cotangent, *after)


def project_into(w_ref, first, frames, out_ref):
    count, heads = out_ref.shape[:2]

    def one(t, carry):
        rows = lax.dot_general(
            w_ref[first + t], frames, (((1,), (1,)), ((), ())), preferred_element_type=F32
        )
        for h in range(heads):
            out_ref[t, h] = padded_head(rows, h)
        return carry

    lax.fori_loop(0, count, one, 0)


def project_kernel(w_ref, *refs):
    project_into(w_ref, 0, jnp.concatenate([r[...] for r in refs[:-1]], axis=0), refs[-1])


def project(weights, blocks):
    rows = sum(b.shape[0] for b in blocks)
    heads = weights.shape[1] // HEAD
    return pl.pallas_call(
        project_kernel,
        out_shape=jax.ShapeDtypeStruct((3, heads, PADDED, rows), BF16),
        in_specs=[VMEM] * (1 + len(blocks)),
        out_specs=VMEM,
        compiler_params=LIMIT,
        cost_estimate=SMALL,
        name="project",
    )(weights, *blocks)


def attention_kernel(parts, n, me_ref, ids_ref, w_ref, *refs):
    pieces, last, (out_ref, own) = refs[:parts], refs[parts:-2], refs[-2:]
    heads, total = out_ref.shape[:2]
    rows = total // n
    project_into(w_ref, 0, jnp.concatenate([r[...] for r in last], axis=0), own)
    labels = []
    for k in range(n):
        start = pl.multiple_of((me_ref[0] ^ k) * rows, PADDED)
        labels.append(ids_ref[:, pl.ds(start, rows)].astype(F32))
    down = [jnp.broadcast_to(row, (PADDED, rows)).T for row in labels]
    column = jnp.concatenate(down, axis=0)
    step = max(PADDED, min(total, 512 * 512 // total))
    for h in range(heads):
        queries, keys = (
            jnp.concatenate([p[t, h] for p in pieces] + [own[t, h]], axis=1) for t in range(2)
        )
        for at in range(0, total, step):
            scores = lax.dot_general(
                keys, queries[:, at : at + step], (((0,), (0,)), ((), ())), preferred_element_type=F32
            )
            same = jnp.concatenate(
                [column == labels[c // rows] for c in range(at, at + step, rows)], axis=1
            )
            scores = jnp.where(same, scores * HEAD**-0.5, -1e30)
            exponent = jnp.exp(scores - jnp.max(scores, axis=0, keepdims=True))
            inverse = 1.0 / jnp.sum(exponent, axis=0, keepdims=True)
            out_ref[h, :, at : at + step] = (exponent * inverse).astype(BF16)


def attention_weights(me, ids, weights, pieces, last, n):
    heads, total = weights.shape[1] // HEAD, ids.shape[1]
    rows = total // n
    return pl.pallas_call(
        functools.partial(attention_kernel, len(pieces), n),
        out_shape=jax.ShapeDtypeStruct((heads, total, total), BF16),
        in_specs=[SMEM] + [VMEM] * (2 + len(pieces) + len(last)),
        out_specs=VMEM,
        scratch_shapes=[pltpu.VMEM((2, heads, PADDED, rows), BF16)],
        compiler_params=LIMIT,
        cost_estimate=SMALL,
        name="attention_weights",
    )(me, ids, weights, *pieces, *last)


def gradient_into(core, values, blocks, outs, cuts):
    for (start, cut), theirs, mine in zip(cuts, outs[::2], outs[1::2]):
        frames = jnp.concatenate([b[:, start : start + cut] for b in blocks], axis=0)
        grads = jnp.dot(values, frames, preferred_element_type=F32)
        half = theirs.shape[0]
        theirs[...] = jnp.where(core == 0, grads[half:], grads[:half]).astype(BF16)
        mine[...] = jnp.where(core == 0, grads[:half], grads[half:]).astype(BF16)


def first_gradient_kernel(n, cuts, core_ref, weights_ref, *refs):
    cots, blocks, outs = refs[:n], refs[n : -1 - 2 * len(cuts)], refs[-1 - 2 * len(cuts) :]
    upstream = jnp.concatenate([c[...] for c in cots], axis=1).astype(F32)
    rows = []
    for h in range(weights_ref.shape[0]):
        rows.append(
            lax.dot_general(
                padded_head(upstream, h), weights_ref[h], (((1,), (1,)), ((), ())), preferred_element_type=F32
            )[:HEAD]
        )
    outs[0][...] = jnp.concatenate(rows, axis=0).astype(BF16)
    gradient_into(core_ref[0], outs[0][...], blocks, outs[1:], cuts)


def next_gradient_kernel(cuts, core_ref, values_ref, *refs):
    gradient_into(core_ref[0], values_ref[...], refs[: -2 * len(cuts) - 1], refs[-2 * len(cuts) :], cuts)


def gradient(core, bit, weights, cots, blocks, axis):
    width, total, model = cots[0].shape[0], weights.shape[1], blocks[0].shape[1]
    cuts = [(sum(CUTS[:i]), cut) for i, cut in enumerate(CUTS)]

    def shapes(some):
        return [jax.ShapeDtypeStruct((width // 2, cut), BF16) for _, cut in some for _ in range(2)]

    values, theirs, mine = pl.pallas_call(
        functools.partial(first_gradient_kernel, len(cots), cuts[:1]),
        out_shape=[jax.ShapeDtypeStruct((width, total), BF16)] + shapes(cuts[:1]),
        in_specs=[SMEM] + [VMEM] * (1 + len(cots) + len(blocks)),
        out_specs=[VMEM] * 3,
        compiler_params=LIMIT,
        cost_estimate=SMALL,
        name="first_gradient",
    )(core, weights, *cots, *blocks)
    split = [split_sum(bit, mine, swap(theirs, axis, 1))]
    outs = pl.pallas_call(
        functools.partial(next_gradient_kernel, cuts[1:]),
        out_shape=shapes(cuts[1:]),
        in_specs=[SMEM] + [VMEM] * (1 + len(blocks)) + [ANY],
        out_specs=[VMEM] * (2 * len(cuts) - 2),
        compiler_params=LIMIT,
        cost_estimate=pl.CostEstimate(
            flops=4 * width * total * model, bytes_accessed=2 * total * model, transcendentals=0
        ),
        name="next_gradient",
    )(core, values, *blocks, split[0][0])
    for theirs, mine in zip(outs[::2], outs[1::2]):
        split.append(split_sum(bit, mine, swap(theirs, axis, 1), split[-1][0]))
    return split


def context_kernel(parts, n, weights_ref, *refs):
    pieces, w_ref, last, outs = refs[:parts], refs[parts], refs[parts + 1 : -n - 3], refs[-n - 3 : -3]
    loaded, own, sem = refs[-3:]
    copy = pltpu.make_async_copy(w_ref.at[pl.ds(2, 1)], loaded, sem)
    copy.start()
    copy.wait()
    project_into(loaded, 0, jnp.concatenate([r[...] for r in last], axis=0), own)
    rows = outs[0].shape[1]
    found = []
    for h in range(weights_ref.shape[0]):
        values = jnp.concatenate([p[2, h] for p in pieces] + [own[0, h]], axis=1)
        found.append(jnp.dot(values, weights_ref[h], preferred_element_type=F32)[:HEAD])
    stacked = jnp.concatenate(found, axis=0)
    for k, out in enumerate(outs):
        out[...] = stacked[:, k * rows : (k + 1) * rows].astype(BF16)


def contexts_of(weights, projections, pieces, last, n):
    heads, total = weights.shape[:2]
    rows, width, model = total // n, projections.shape[1], projections.shape[2]
    return pl.pallas_call(
        functools.partial(context_kernel, len(pieces), n),
        out_shape=[jax.ShapeDtypeStruct((heads * HEAD, rows), BF16)] * n,
        in_specs=[VMEM] * (1 + len(pieces)) + [HBM] + [VMEM] * len(last),
        out_specs=[VMEM] * n,
        scratch_shapes=[
            pltpu.VMEM((1, width, model), BF16),
            pltpu.VMEM((1, heads, PADDED, rows), BF16),
            pltpu.SemaphoreType.DMA,
        ],
        compiler_params=LIMIT,
        cost_estimate=SMALL,
        name="contexts",
    )(weights, *pieces, projections, *last)


def assemble_kernel(me_ref, *refs):
    n = len(refs) - 3
    out, token, turned = refs[n:]
    width = refs[0].shape[0]
    for k in range(n):
        start = pl.multiple_of((me_ref[0] ^ k) * width, 8)
        turned[pl.ds(start, width), :] = refs[k][...].astype(F32)
    out[...] = turned[...].T.astype(BF16)
    token[...] = jnp.zeros_like(token)


def assemble_context(me, pieces):
    n, (width, rows) = len(pieces), pieces[0].shape
    return pl.pallas_call(
        assemble_kernel,
        out_shape=[jax.ShapeDtypeStruct((rows, n * width), BF16), jax.ShapeDtypeStruct((8, PADDED), F32)],
        in_specs=[SMEM] + [VMEM] * n,
        out_specs=[VMEM] * 2,
        scratch_shapes=[pltpu.VMEM((n * width, rows), F32)],
        compiler_params=LIMIT,
        cost_estimate=SMALL,
        name="assemble_context",
    )(me, *pieces)


def final_kernel(start, scale, place_ref, *refs):
    pieces, out_ref, scratch, sem = refs[:4], refs[-3], refs[-2], refs[-1]
    rows, cut = pieces[0].shape
    for k, piece in enumerate(pieces):
        at = pl.multiple_of((place_ref[0] ^ k) * rows, 8)
        scratch[pl.ds(at, rows), :] = piece[...].astype(F32) * scale
    copy = pltpu.make_async_copy(scratch, out_ref.at[:, pl.ds(start, cut)], sem)
    copy.start()
    copy.wait()


def final(place, pieces, start, scale, model, out):
    rows, cut = pieces[0].shape
    earlier = [] if out is None else [out]
    return pl.pallas_call(
        functools.partial(final_kernel, start, scale),
        out_shape=jax.ShapeDtypeStruct((4 * rows, model), F32),
        in_specs=[SMEM] + [VMEM] * 4 + [HBM] * len(earlier),
        out_specs=HBM,
        scratch_shapes=[pltpu.VMEM((4 * rows, cut), F32), pltpu.SemaphoreType.DMA],
        input_output_aliases={5: 0} if earlier else {},
        compiler_params=LIMIT,
        cost_estimate=SMALL,
        name="final",
    )(place, *pieces, *earlier)


def add_kernel(a_ref, b_ref, *refs):
    refs[-1][...] = (a_ref[...].astype(F32) + b_ref[...].astype(F32)).astype(BF16)


def add(a, b, *after):
    return pl.pallas_call(
        add_kernel,
        out_shape=jax.ShapeDtypeStruct(a.shape, BF16),
        in_specs=[VMEM, VMEM] + [ANY] * len(after),
        out_specs=VMEM,
        compiler_params=LIMIT,
        cost_estimate=SMALL,
        name="add",
    )(a, b, *after)


def split_sum_kernel(bit_ref, a_ref, b_ref, *refs):
    sent, kept = refs[-2:]
    total = a_ref[...].astype(F32) + b_ref[...].astype(F32)
    half = sent.shape[0]
    low = bit_ref[0] == 0
    sent[...] = jnp.where(low, total[half:], total[:half]).astype(BF16)
    kept[...] = jnp.where(low, total[:half], total[half:]).astype(BF16)


def split_sum(bit, a, b, *after):
    rows, columns = a.shape
    return pl.pallas_call(
        split_sum_kernel,
        out_shape=[jax.ShapeDtypeStruct((rows // 2, columns), BF16)] * 2,
        in_specs=[SMEM, VMEM, VMEM] + [ANY] * len(after),
        out_specs=[VMEM] * 2,
        compiler_params=LIMIT,
        cost_estimate=SMALL,
        name="split_sum",
    )(bit, a, b, *after)


def cube_sums(split, axis, after, late):
    n = lax.axis_size(axis)
    masks = [1 << b for b in range(2, n.bit_length() - 1)]
    out = []
    for k, (sent, own) in enumerate(split):
        total = add(own, swap(sent, axis, 2), *([out[-1][0]] if out else after))
        for mask in masks:
            wait = []
            if mask == masks[-1]:
                wait += out[-1][1:3] if out else ()
                wait += out[-2][3:] if len(out) > 1 else ()
                wait += late if k == 1 else ()
            total = add(total, swap(total, axis, mask), *wait)
        got = swap(total, axis, 2)
        out.append((total, got, swap(total, axis, 1), swap(got, axis, 1)))
    return out


def body(features, segment_ids, projections, cotangent):
    n = lax.axis_size("seq")
    me = lax.axis_index("seq")
    core, bit = lax.axis_index("dp") % 2, lax.axis_index("dp") // 2 % 2
    me_ref, core_ref, bit_ref, place_ref = (
        x.reshape(1).astype(jnp.int32) for x in (me, core, bit, 2 * core + bit)
    )
    model, width = features.shape[2], projections.shape[1]
    scale = 1.0 / lax.axis_size("dp")

    blocks = gather_blocks(features[0], "seq")

    def flat(some):
        return [part for block in some for part in block]

    first = [blocks[1][0], blocks[2][1]] if n == 4 else []
    shares = cotangent_shares(me_ref, cotangent[0], n, first)
    cots = [shares[0]] + [swap(shares[k], "seq", k) for k in range(1, n)]
    pieces = [project(projections, flat(some)) for some in (blocks[:1], blocks[1 : n - 1]) if some]
    weights = attention_weights(me_ref, segment_ids, projections, pieces, flat(blocks[n - 1 :]), n)
    split = gradient(core_ref, bit_ref, weights, cots, flat(blocks), "dp")
    contexts = contexts_of(weights, projections, pieces, flat(blocks[n - 1 :]), n)
    received = [contexts[0]] + [swap(contexts[k], "seq", k) for k in range(1, n)]
    context, token = assemble_context(me_ref, received)
    sums = cube_sums(split, "dp", contexts[:1], [token])
    if width % 32:
        chunks = []
        for kept, got, far_kept, far_got in sums:
            low = bit == 0
            near = jnp.where(low, jnp.concatenate([kept, got]), jnp.concatenate([got, kept]))
            far = jnp.where(low, jnp.concatenate([far_kept, far_got]), jnp.concatenate([far_got, far_kept]))
            chunks.append(jnp.where(core == 0, jnp.concatenate([near, far]), jnp.concatenate([far, near])))
        value_grad = jnp.concatenate(chunks, axis=1).astype(F32) * scale
    else:
        value_grad, start = None, 0
        for pieces in sums:
            value_grad = final(place_ref, pieces, start, scale, model, value_grad)
            start += pieces[0].shape[1]
    return context[None], value_grad


def solution(mesh):
    in_specs = (P("dp", "seq", None), P("dp", None), P(None, "seq", None), P("dp", "seq", None))
    out_specs = (P("dp", "seq", None), P("seq", None))
    return jax.shard_map(body, mesh=mesh, in_specs=in_specs, out_specs=out_specs, check_vma=False)
```

```python
import functools

import jax
import jax.numpy as jnp
from jax import lax
from jax.experimental import pallas as pl
from jax.experimental.pallas import tpu as pltpu
from jax.sharding import PartitionSpec as P

HEAD = 120
PADDED = 128
BF16 = jnp.bfloat16
F32 = jnp.float32
VMEM = pl.BlockSpec(memory_space=pltpu.VMEM)
ANY = pl.BlockSpec(memory_space=pl.ANY)
HBM = pl.BlockSpec(memory_space=pltpu.HBM)
LIMIT = pltpu.CompilerParams(vmem_limit_bytes=12 * 1024 * 1024)
SMALL = pl.CostEstimate(flops=1000, bytes_accessed=1000, transcendentals=0)
CUTS = (512, 896, 512)


def core_index():
    return lax.axis_index("dp") % 2


def line_bit():
    return lax.axis_index("dp") // 2 % 2


def swap(array, axis, mask):
    return lax.ppermute(array, axis, [(i, i ^ mask) for i in range(lax.axis_size(axis))])


def halves_kernel(x_ref, top_ref, bottom_ref, sems):
    half = top_ref.shape[0]
    copies = [
        pltpu.make_async_copy(x_ref.at[pl.ds(i * half, half)], out, sems.at[i])
        for i, out in enumerate((top_ref, bottom_ref))
    ]
    for copy in copies:
        copy.start()
    for copy in copies:
        copy.wait()


def halves(block):
    rows, model = block.shape
    return pl.pallas_call(
        halves_kernel,
        out_shape=[jax.ShapeDtypeStruct((rows // 2, model), BF16)] * 2,
        in_specs=[HBM],
        out_specs=[VMEM] * 2,
        scratch_shapes=[pltpu.SemaphoreType.DMA((2,))],
        compiler_params=LIMIT,
        name="halves",
    )(block)


def gather_blocks(block, axis):
    n = lax.axis_size(axis)
    if n != 4:
        return [[block]] + [[swap(block, axis, k)] for k in range(1, n)]
    top, bottom = halves(block)
    top_x, bottom_y = swap(top, axis, 1), swap(bottom, axis, 2)
    bottom_x, top_y = swap(bottom, axis, 1), swap(top, axis, 2)
    top_xy, bottom_xy = swap(top_x, axis, 2), swap(bottom_y, axis, 1)
    return [[block], [top_x, bottom_x], [top_y, bottom_y], [top_xy, bottom_xy]]


def padded_head(rows, h):
    own = rows[h * HEAD : (h + 1) * HEAD]
    zeros = jnp.zeros((PADDED - HEAD, rows.shape[1]), F32)
    return jnp.concatenate([own, zeros], axis=0).astype(BF16)


def shares_kernel(n, cot_ref, *refs):
    outs, (loaded, turned, sem) = refs[-n - 3 : -3], refs[-3:]
    copy = pltpu.make_async_copy(cot_ref, loaded, sem)
    copy.start()
    copy.wait()
    turned[...] = loaded[...].astype(F32).T
    width, me = outs[0].shape[0], lax.axis_index("seq")
    for k in range(n):
        start = pl.multiple_of((me ^ k) * width, 8)
        outs[k][...] = turned[pl.ds(start, width), :].astype(BF16)


def cotangent_shares(cotangent, n, after):
    rows, model = cotangent.shape
    return pl.pallas_call(
        functools.partial(shares_kernel, n),
        out_shape=[jax.ShapeDtypeStruct((model // n, rows), BF16)] * n,
        in_specs=[HBM] + [ANY] * len(after),
        out_specs=[VMEM] * n,
        scratch_shapes=[
            pltpu.VMEM((rows, model), BF16),
            pltpu.VMEM((model, rows), F32),
            pltpu.SemaphoreType.DMA,
        ],
        compiler_params=LIMIT,
        name="cotangent_shares",
    )(cotangent, *after)


def project_into(w_ref, first, frames, out_ref):
    count, heads = out_ref.shape[:2]

    def one(t, carry):
        rows = lax.dot_general(
            w_ref[first + t], frames, (((1,), (1,)), ((), ())), preferred_element_type=F32
        )
        for h in range(heads):
            out_ref[t, h] = padded_head(rows, h)
        return carry

    lax.fori_loop(0, count, one, 0)


def project_kernel(w_ref, *refs):
    project_into(w_ref, 0, jnp.concatenate([r[...] for r in refs[:-1]], axis=0), refs[-1])


def project(weights, blocks):
    rows = sum(b.shape[0] for b in blocks)
    heads = weights.shape[1] // HEAD
    return pl.pallas_call(
        project_kernel,
        out_shape=jax.ShapeDtypeStruct((3, heads, PADDED, rows), BF16),
        in_specs=[VMEM] * (1 + len(blocks)),
        out_specs=VMEM,
        compiler_params=LIMIT,
        cost_estimate=SMALL,
        name="project",
    )(weights, *blocks)


def attention_kernel(parts, n, ids_ref, w_ref, *refs):
    pieces, last, (out_ref, own) = refs[:parts], refs[parts:-2], refs[-2:]
    heads, total = out_ref.shape[:2]
    rows = total // n
    project_into(w_ref, 0, jnp.concatenate([r[...] for r in last], axis=0), own)
    labels, me = [], lax.axis_index("seq")
    for k in range(n):
        start = pl.multiple_of((me ^ k) * rows, PADDED)
        labels.append(ids_ref[:, pl.ds(start, rows)].astype(F32))
    down = [jnp.broadcast_to(row, (PADDED, rows)).T for row in labels]
    column = jnp.concatenate(down, axis=0)
    step = max(PADDED, min(total, 512 * 512 // total))
    for h in range(heads):
        queries, keys = (
            jnp.concatenate([p[t, h] for p in pieces] + [own[t, h]], axis=1) for t in range(2)
        )
        for at in range(0, total, step):
            scores = lax.dot_general(
                keys, queries[:, at : at + step], (((0,), (0,)), ((), ())), preferred_element_type=F32
            )
            same = jnp.concatenate(
                [column == labels[c // rows] for c in range(at, at + step, rows)], axis=1
            )
            scores = jnp.where(same, scores * HEAD**-0.5, -1e30)
            exponent = jnp.exp(scores - jnp.max(scores, axis=0, keepdims=True))
            inverse = 1.0 / jnp.sum(exponent, axis=0, keepdims=True)
            out_ref[h, :, at : at + step] = (exponent * inverse).astype(BF16)


def attention_weights(ids, weights, pieces, last, n):
    heads, total = weights.shape[1] // HEAD, ids.shape[1]
    rows = total // n
    return pl.pallas_call(
        functools.partial(attention_kernel, len(pieces), n),
        out_shape=jax.ShapeDtypeStruct((heads, total, total), BF16),
        in_specs=[VMEM] * (2 + len(pieces) + len(last)),
        out_specs=VMEM,
        scratch_shapes=[pltpu.VMEM((2, heads, PADDED, rows), BF16)],
        compiler_params=LIMIT,
        cost_estimate=SMALL,
        name="attention_weights",
    )(ids, weights, *pieces, *last)


def gradient_into(values, blocks, outs, cuts):
    core = core_index()
    for (start, cut), theirs, mine in zip(cuts, outs[::2], outs[1::2]):
        frames = jnp.concatenate([b[:, start : start + cut] for b in blocks], axis=0)
        grads = jnp.dot(values, frames, preferred_element_type=F32)
        half = theirs.shape[0]
        theirs[...] = jnp.where(core == 0, grads[half:], grads[:half]).astype(BF16)
        mine[...] = jnp.where(core == 0, grads[:half], grads[half:]).astype(BF16)


def first_gradient_kernel(n, cuts, weights_ref, *refs):
    cots, blocks, outs = refs[:n], refs[n : -1 - 2 * len(cuts)], refs[-1 - 2 * len(cuts) :]
    upstream = jnp.concatenate([c[...] for c in cots], axis=1).astype(F32)
    rows = []
    for h in range(weights_ref.shape[0]):
        rows.append(
            lax.dot_general(
                padded_head(upstream, h), weights_ref[h], (((1,), (1,)), ((), ())), preferred_element_type=F32
            )[:HEAD]
        )
    outs[0][...] = jnp.concatenate(rows, axis=0).astype(BF16)
    gradient_into(outs[0][...], blocks, outs[1:], cuts)


def next_gradient_kernel(cuts, values_ref, *refs):
    gradient_into(values_ref[...], refs[: -2 * len(cuts) - 1], refs[-2 * len(cuts) :], cuts)


def gradient(weights, cots, blocks, axis):
    width, total, model = cots[0].shape[0], weights.shape[1], blocks[0].shape[1]
    cuts = [(sum(CUTS[:i]), cut) for i, cut in enumerate(CUTS)]

    def shapes(some):
        return [jax.ShapeDtypeStruct((width // 2, cut), BF16) for _, cut in some for _ in range(2)]

    values, theirs, mine = pl.pallas_call(
        functools.partial(first_gradient_kernel, len(cots), cuts[:1]),
        out_shape=[jax.ShapeDtypeStruct((width, total), BF16)] + shapes(cuts[:1]),
        in_specs=[VMEM] * (1 + len(cots) + len(blocks)),
        out_specs=[VMEM] * 3,
        compiler_params=LIMIT,
        cost_estimate=SMALL,
        name="first_gradient",
    )(weights, *cots, *blocks)
    split = [split_sum(mine, swap(theirs, axis, 1))]
    outs = pl.pallas_call(
        functools.partial(next_gradient_kernel, cuts[1:]),
        out_shape=shapes(cuts[1:]),
        in_specs=[VMEM] * (1 + len(blocks)) + [ANY],
        out_specs=[VMEM] * (2 * len(cuts) - 2),
        compiler_params=LIMIT,
        cost_estimate=pl.CostEstimate(
            flops=4 * width * total * model, bytes_accessed=2 * total * model, transcendentals=0
        ),
        name="next_gradient",
    )(values, *blocks, split[0][0])
    for theirs, mine in zip(outs[::2], outs[1::2]):
        split.append(split_sum(mine, swap(theirs, axis, 1), split[-1][0]))
    return split


def context_kernel(parts, n, weights_ref, *refs):
    pieces, w_ref, last, outs = refs[:parts], refs[parts], refs[parts + 1 : -n - 3], refs[-n - 3 : -3]
    loaded, own, sem = refs[-3:]
    copy = pltpu.make_async_copy(w_ref.at[pl.ds(2, 1)], loaded, sem)
    copy.start()
    copy.wait()
    project_into(loaded, 0, jnp.concatenate([r[...] for r in last], axis=0), own)
    rows = outs[0].shape[1]
    found = []
    for h in range(weights_ref.shape[0]):
        values = jnp.concatenate([p[2, h] for p in pieces] + [own[0, h]], axis=1)
        found.append(jnp.dot(values, weights_ref[h], preferred_element_type=F32)[:HEAD])
    stacked = jnp.concatenate(found, axis=0)
    for k, out in enumerate(outs):
        out[...] = stacked[:, k * rows : (k + 1) * rows].astype(BF16)


def contexts_of(weights, projections, pieces, last, n):
    heads, total = weights.shape[:2]
    rows, width, model = total // n, projections.shape[1], projections.shape[2]
    return pl.pallas_call(
        functools.partial(context_kernel, len(pieces), n),
        out_shape=[jax.ShapeDtypeStruct((heads * HEAD, rows), BF16)] * n,
        in_specs=[VMEM] * (1 + len(pieces)) + [HBM] + [VMEM] * len(last),
        out_specs=[VMEM] * n,
        scratch_shapes=[
            pltpu.VMEM((1, width, model), BF16),
            pltpu.VMEM((1, heads, PADDED, rows), BF16),
            pltpu.SemaphoreType.DMA,
        ],
        compiler_params=LIMIT,
        cost_estimate=SMALL,
        name="contexts",
    )(weights, *pieces, projections, *last)


def assemble_kernel(*refs):
    n = len(refs) - 3
    out, token, turned = refs[n:]
    width, me = refs[0].shape[0], lax.axis_index("seq")
    for k in range(n):
        start = pl.multiple_of((me ^ k) * width, 8)
        turned[pl.ds(start, width), :] = refs[k][...].astype(F32)
    out[...] = turned[...].T.astype(BF16)
    token[...] = jnp.zeros_like(token)


def assemble_context(pieces):
    n, (width, rows) = len(pieces), pieces[0].shape
    return pl.pallas_call(
        assemble_kernel,
        out_shape=[jax.ShapeDtypeStruct((rows, n * width), BF16), jax.ShapeDtypeStruct((8, PADDED), F32)],
        in_specs=[VMEM] * n,
        out_specs=[VMEM] * 2,
        scratch_shapes=[pltpu.VMEM((n * width, rows), F32)],
        compiler_params=LIMIT,
        cost_estimate=SMALL,
        name="assemble_context",
    )(*pieces)


def final_kernel(start, scale, *refs):
    pieces, out_ref, scratch, sem = refs[:4], refs[-3], refs[-2], refs[-1]
    rows, cut = pieces[0].shape
    place = 2 * core_index() + line_bit()
    for k, piece in enumerate(pieces):
        at = pl.multiple_of((place ^ k) * rows, 8)
        scratch[pl.ds(at, rows), :] = piece[...].astype(F32) * scale
    copy = pltpu.make_async_copy(scratch, out_ref.at[:, pl.ds(start, cut)], sem)
    copy.start()
    copy.wait()


def final(pieces, start, scale, model, out):
    rows, cut = pieces[0].shape
    earlier = [] if out is None else [out]
    return pl.pallas_call(
        functools.partial(final_kernel, start, scale),
        out_shape=jax.ShapeDtypeStruct((4 * rows, model), F32),
        in_specs=[VMEM] * 4 + [HBM] * len(earlier),
        out_specs=HBM,
        scratch_shapes=[pltpu.VMEM((4 * rows, cut), F32), pltpu.SemaphoreType.DMA],
        input_output_aliases={4: 0} if earlier else {},
        compiler_params=LIMIT,
        cost_estimate=SMALL,
        name="final",
    )(*pieces, *earlier)


def add_kernel(a_ref, b_ref, *refs):
    refs[-1][...] = (a_ref[...].astype(F32) + b_ref[...].astype(F32)).astype(BF16)


def add(a, b, *after):
    return pl.pallas_call(
        add_kernel,
        out_shape=jax.ShapeDtypeStruct(a.shape, BF16),
        in_specs=[VMEM, VMEM] + [ANY] * len(after),
        out_specs=VMEM,
        compiler_params=LIMIT,
        cost_estimate=SMALL,
        name="add",
    )(a, b, *after)


def split_sum_kernel(a_ref, b_ref, *refs):
    sent, kept = refs[-2:]
    total = a_ref[...].astype(F32) + b_ref[...].astype(F32)
    half = sent.shape[0]
    low = line_bit() == 0
    sent[...] = jnp.where(low, total[half:], total[:half]).astype(BF16)
    kept[...] = jnp.where(low, total[:half], total[half:]).astype(BF16)


def split_sum(a, b, *after):
    rows, columns = a.shape
    return pl.pallas_call(
        split_sum_kernel,
        out_shape=[jax.ShapeDtypeStruct((rows // 2, columns), BF16)] * 2,
        in_specs=[VMEM, VMEM] + [ANY] * len(after),
        out_specs=[VMEM] * 2,
        compiler_params=LIMIT,
        cost_estimate=SMALL,
        name="split_sum",
    )(a, b, *after)


def cube_sums(split, axis, after, late):
    n = lax.axis_size(axis)
    masks = [1 << b for b in range(2, n.bit_length() - 1)]
    out = []
    for k, (sent, own) in enumerate(split):
        total = add(own, swap(sent, axis, 2), *([out[-1][0]] if out else after))
        for mask in masks:
            wait = []
            if mask == masks[-1]:
                wait += out[-1][1:3] if out else ()
                wait += out[-2][3:] if len(out) > 1 else ()
                wait += late if k == 1 else ()
            total = add(total, swap(total, axis, mask), *wait)
        got = swap(total, axis, 2)
        out.append((total, got, swap(total, axis, 1), swap(got, axis, 1)))
    return out


def body(features, segment_ids, projections, cotangent):
    n = lax.axis_size("seq")
    model, width = features.shape[2], projections.shape[1]
    scale = 1.0 / lax.axis_size("dp")

    blocks = gather_blocks(features[0], "seq")

    def flat(some):
        return [part for block in some for part in block]

    first = [blocks[1][0], blocks[2][1]] if n == 4 else []
    shares = cotangent_shares(cotangent[0], n, first)
    cots = [shares[0]] + [swap(shares[k], "seq", k) for k in range(1, n)]
    pieces = [project(projections, flat(some)) for some in (blocks[:1], blocks[1 : n - 1]) if some]
    weights = attention_weights(segment_ids, projections, pieces, flat(blocks[n - 1 :]), n)
    split = gradient(weights, cots, flat(blocks), "dp")
    contexts = contexts_of(weights, projections, pieces, flat(blocks[n - 1 :]), n)
    received = [contexts[0]] + [swap(contexts[k], "seq", k) for k in range(1, n)]
    context, token = assemble_context(received)
    sums = cube_sums(split, "dp", contexts[:1], [token])
    if width % 32:
        chunks = []
        for kept, got, far_kept, far_got in sums:
            low = line_bit() == 0
            near = jnp.where(low, jnp.concatenate([kept, got]), jnp.concatenate([got, kept]))
            far = jnp.where(low, jnp.concatenate([far_kept, far_got]), jnp.concatenate([far_got, far_kept]))
            chunks.append(jnp.where(core_index() == 0, jnp.concatenate([near, far]), jnp.concatenate([far, near])))
        value_grad = jnp.concatenate(chunks, axis=1).astype(F32) * scale
    else:
        value_grad, start = None, 0
        for pieces in sums:
            value_grad = final(pieces, start, scale, model, value_grad)
            start += pieces[0].shape[1]
    return context[None], value_grad


def solution(mesh):
    in_specs = (P("dp", "seq", None), P("dp", None), P(None, "seq", None), P("dp", "seq", None))
    out_specs = (P("dp", "seq", None), P("seq", None))
    return jax.shard_map(body, mesh=mesh, in_specs=in_specs, out_specs=out_specs, check_vma=False)
```

```python
import functools

import jax
import jax.numpy as jnp
from jax import lax
from jax.experimental import pallas as pl
from jax.experimental.pallas import tpu as pltpu
from jax.sharding import PartitionSpec as P

HEAD = 120
PADDED = 128
BF16 = jnp.bfloat16
F32 = jnp.float32
VMEM = pl.BlockSpec(memory_space=pltpu.VMEM)
ANY = pl.BlockSpec(memory_space=pl.ANY)
HBM = pl.BlockSpec(memory_space=pltpu.HBM)
LIMIT = pltpu.CompilerParams(vmem_limit_bytes=12 * 1024 * 1024)
SMALL = pl.CostEstimate(flops=1000, bytes_accessed=1000, transcendentals=0)
CUTS = (1024, 896)


def core_index():
    return lax.axis_index("dp") % 2


def line_bit():
    return lax.axis_index("dp") // 2 % 2


def swap(array, axis, mask):
    return lax.ppermute(array, axis, [(i, i ^ mask) for i in range(lax.axis_size(axis))])


def halves_kernel(x_ref, top_ref, bottom_ref, sems):
    half = top_ref.shape[0]
    copies = [
        pltpu.make_async_copy(x_ref.at[pl.ds(i * half, half)], out, sems.at[i])
        for i, out in enumerate((top_ref, bottom_ref))
    ]
    for copy in copies:
        copy.start()
    for copy in copies:
        copy.wait()


def halves(block):
    rows, model = block.shape
    return pl.pallas_call(
        halves_kernel,
        out_shape=[jax.ShapeDtypeStruct((rows // 2, model), BF16)] * 2,
        in_specs=[HBM],
        out_specs=[VMEM] * 2,
        scratch_shapes=[pltpu.SemaphoreType.DMA((2,))],
        compiler_params=LIMIT,
        name="halves",
    )(block)


def gate(arrays, after):
    return pl.pallas_call(
        lambda *refs: None,
        out_shape=[jax.ShapeDtypeStruct(a.shape, a.dtype) for a in arrays],
        in_specs=[VMEM] * len(arrays) + [ANY] * len(after),
        out_specs=[VMEM] * len(arrays),
        input_output_aliases={i: i for i in range(len(arrays))},
        compiler_params=LIMIT,
        cost_estimate=SMALL,
        name="gate",
    )(*arrays, *after)


def gather_blocks(block, axis, meanwhile):
    n = lax.axis_size(axis)
    if n != 4:
        return [[block]] + [[swap(block, axis, k)] for k in range(1, n)], meanwhile([block])
    top, bottom = halves(block)
    made = meanwhile([top, bottom])
    top_x, bottom_y = gate([swap(top, axis, 1), swap(bottom, axis, 2)], made)
    bottom_x, top_y = swap(bottom, axis, 1), swap(top, axis, 2)
    top_xy, bottom_xy = swap(top_x, axis, 2), swap(bottom_y, axis, 1)
    return [[top, bottom], [top_x, bottom_x], [top_y, bottom_y], [top_xy, bottom_xy]], made


def padded_head(rows, h):
    own = rows[h * HEAD : (h + 1) * HEAD]
    zeros = jnp.zeros((PADDED - HEAD, rows.shape[1]), F32)
    return jnp.concatenate([own, zeros], axis=0).astype(BF16)


def shares_kernel(cot_ref, *refs):
    outs, turned = refs[:-1], refs[-1]
    turned[...] = cot_ref[...].astype(F32).T
    width, me = outs[0].shape[0], lax.axis_index("seq")
    for k, out in enumerate(outs):
        start = pl.multiple_of((me ^ k) * width, 8)
        out[...] = turned[pl.ds(start, width), :].astype(BF16)


def cotangent_shares(cotangent, n):
    rows, model = cotangent.shape
    return pl.pallas_call(
        shares_kernel,
        out_shape=[jax.ShapeDtypeStruct((model // n, rows), BF16)] * n,
        in_specs=[VMEM],
        out_specs=[VMEM] * n,
        scratch_shapes=[pltpu.VMEM((model, rows), F32)],
        compiler_params=LIMIT,
        cost_estimate=SMALL,
        name="cotangent_shares",
    )(cotangent)


def project_into(w_ref, first, frames, out_ref):
    count, heads = out_ref.shape[:2]

    def one(t, carry):
        rows = lax.dot_general(
            w_ref[first + t], frames, (((1,), (1,)), ((), ())), preferred_element_type=F32
        )
        for h in range(heads):
            out_ref[t, h] = padded_head(rows, h)
        return carry

    lax.fori_loop(0, count, one, 0)


def project_kernel(w_ref, *refs):
    project_into(w_ref, 0, jnp.concatenate([r[...] for r in refs[:-1]], axis=0), refs[-1])


def project(weights, blocks):
    rows = sum(b.shape[0] for b in blocks)
    heads = weights.shape[1] // HEAD
    return pl.pallas_call(
        project_kernel,
        out_shape=jax.ShapeDtypeStruct((2, heads, PADDED, rows), BF16),
        in_specs=[VMEM] * (1 + len(blocks)),
        out_specs=VMEM,
        compiler_params=LIMIT,
        cost_estimate=SMALL,
        name="project",
    )(weights, *blocks)


def attention_kernel(parts, n, ids_ref, w_ref, *refs):
    pieces, last, (out_ref, own) = refs[:parts], refs[parts:-2], refs[-2:]
    heads, total = out_ref.shape[:2]
    rows = total // n
    project_into(w_ref, 0, jnp.concatenate([r[...] for r in last], axis=0), own)
    labels, me = [], lax.axis_index("seq")
    for k in range(n):
        start = pl.multiple_of((me ^ k) * rows, PADDED)
        labels.append(ids_ref[:, pl.ds(start, rows)].astype(F32))
    down = [jnp.broadcast_to(row, (PADDED, rows)).T for row in labels]
    column = jnp.concatenate(down, axis=0)
    step = max(PADDED, min(total, 512 * 512 // total))
    for h in range(heads):
        queries, keys = (
            jnp.concatenate([p[t, h] for p in pieces] + [own[t, h]], axis=1) for t in range(2)
        )
        for at in range(0, total, step):
            scores = lax.dot_general(
                keys, queries[:, at : at + step], (((0,), (0,)), ((), ())), preferred_element_type=F32
            )
            same = jnp.concatenate(
                [column == labels[c // rows] for c in range(at, at + step, rows)], axis=1
            )
            scores = jnp.where(same, scores * HEAD**-0.5, -1e30)
            exponent = jnp.exp(scores - jnp.max(scores, axis=0, keepdims=True))
            inverse = 1.0 / jnp.sum(exponent, axis=0, keepdims=True)
            out_ref[h, :, at : at + step] = (exponent * inverse).astype(BF16)


def attention_weights(ids, weights, pieces, last, n):
    heads, total = weights.shape[1] // HEAD, ids.shape[1]
    rows = total // n
    return pl.pallas_call(
        functools.partial(attention_kernel, len(pieces), n),
        out_shape=jax.ShapeDtypeStruct((heads, total, total), BF16),
        in_specs=[VMEM] * (2 + len(pieces) + len(last)),
        out_specs=VMEM,
        scratch_shapes=[pltpu.VMEM((2, heads, PADDED, rows), BF16)],
        compiler_params=LIMIT,
        cost_estimate=SMALL,
        name="attention_weights",
    )(ids, weights, *pieces, *last)


def gradient_into(values, blocks, outs, cuts):
    core = core_index()
    for (start, cut), theirs, mine in zip(cuts, outs[::2], outs[1::2]):
        frames = jnp.concatenate([b[:, start : start + cut] for b in blocks], axis=0)
        grads = jnp.dot(values, frames, preferred_element_type=F32)
        half = theirs.shape[0]
        theirs[...] = jnp.where(core == 0, grads[half:], grads[:half]).astype(BF16)
        mine[...] = jnp.where(core == 0, grads[:half], grads[half:]).astype(BF16)


def first_gradient_kernel(n, cuts, weights_ref, *refs):
    cots, blocks, outs = refs[:n], refs[n : -1 - 2 * len(cuts)], refs[-1 - 2 * len(cuts) :]
    upstream = jnp.concatenate([c[...] for c in cots], axis=1).astype(F32)
    rows = []
    for h in range(weights_ref.shape[0]):
        rows.append(
            lax.dot_general(
                padded_head(upstream, h), weights_ref[h], (((1,), (1,)), ((), ())), preferred_element_type=F32
            )[:HEAD]
        )
    outs[0][...] = jnp.concatenate(rows, axis=0).astype(BF16)
    gradient_into(outs[0][...], blocks, outs[1:], cuts)


def next_gradient_kernel(cuts, values_ref, *refs):
    gradient_into(values_ref[...], refs[: -2 * len(cuts)], refs[-2 * len(cuts) :], cuts)


def gradient(weights, cots, blocks, axis):
    width, total, model = cots[0].shape[0], weights.shape[1], blocks[0].shape[1]
    cuts = [(sum(CUTS[:i]), cut) for i, cut in enumerate(CUTS)]

    def shapes(some):
        return [jax.ShapeDtypeStruct((width // 2, cut), BF16) for _, cut in some for _ in range(2)]

    values, theirs, mine = pl.pallas_call(
        functools.partial(first_gradient_kernel, len(cots), cuts[:1]),
        out_shape=[jax.ShapeDtypeStruct((width, total), BF16)] + shapes(cuts[:1]),
        in_specs=[VMEM] * (1 + len(cots) + len(blocks)),
        out_specs=[VMEM] * 3,
        compiler_params=LIMIT,
        cost_estimate=SMALL,
        name="first_gradient",
    )(weights, *cots, *blocks)
    passed = swap(theirs, axis, 1)
    outs = pl.pallas_call(
        functools.partial(next_gradient_kernel, cuts[1:]),
        out_shape=shapes(cuts[1:]),
        in_specs=[VMEM] * (1 + len(blocks)),
        out_specs=[VMEM] * (2 * len(cuts) - 2),
        compiler_params=LIMIT,
        cost_estimate=pl.CostEstimate(
            flops=4 * width * total * model, bytes_accessed=2 * total * model, transcendentals=0
        ),
        name="next_gradient",
    )(values, *blocks)
    split = [split_sum(mine, passed, outs[1])]
    for theirs, mine in zip(outs[::2], outs[1::2]):
        split.append(split_sum(mine, swap(theirs, axis, 1), split[-1][0]))
    return split


def context_kernel(n, weights_ref, w_ref, *refs):
    blocks, outs, values = refs[: -n - 1], refs[-n - 1 : -1], refs[-1]
    project_into(w_ref, 2, jnp.concatenate([r[...] for r in blocks], axis=0), values)
    rows = outs[0].shape[1]
    found = [
        jnp.dot(values[0, h], weights_ref[h], preferred_element_type=F32)[:HEAD]
        for h in range(weights_ref.shape[0])
    ]
    stacked = jnp.concatenate(found, axis=0)
    for k, out in enumerate(outs):
        out[...] = stacked[:, k * rows : (k + 1) * rows].astype(BF16)


def contexts_of(weights, projections, blocks, n):
    heads, total = weights.shape[:2]
    return pl.pallas_call(
        functools.partial(context_kernel, n),
        out_shape=[jax.ShapeDtypeStruct((heads * HEAD, total // n), BF16)] * n,
        in_specs=[VMEM] * (2 + len(blocks)),
        out_specs=[VMEM] * n,
        scratch_shapes=[pltpu.VMEM((1, heads, PADDED, total), BF16)],
        compiler_params=LIMIT,
        cost_estimate=SMALL,
        name="contexts",
    )(weights, projections, *blocks)


def assemble_kernel(*refs):
    n = len(refs) - 3
    out, token, turned = refs[n:]
    width, me = refs[0].shape[0], lax.axis_index("seq")
    for k in range(n):
        start = pl.multiple_of((me ^ k) * width, 8)
        turned[pl.ds(start, width), :] = refs[k][...].astype(F32)
    out[...] = turned[...].T.astype(BF16)
    token[...] = jnp.zeros_like(token)


def assemble_context(pieces):
    n, (width, rows) = len(pieces), pieces[0].shape
    return pl.pallas_call(
        assemble_kernel,
        out_shape=[jax.ShapeDtypeStruct((rows, n * width), BF16), jax.ShapeDtypeStruct((8, PADDED), F32)],
        in_specs=[VMEM] * n,
        out_specs=[VMEM] * 2,
        scratch_shapes=[pltpu.VMEM((n * width, rows), F32)],
        compiler_params=LIMIT,
        cost_estimate=SMALL,
        name="assemble_context",
    )(*pieces)


def final_kernel(spots, scale, *refs):
    pieces, (out_ref, token, sems), scratch = refs[: len(spots)], refs[-len(spots) - 3 : -len(spots)], refs[-len(spots) :]
    place = 2 * core_index() + line_bit()
    copies = []
    for i, ((k, start), piece) in enumerate(zip(spots, pieces)):
        rows, cut = piece.shape
        scratch[i][...] = piece[...].astype(F32) * scale
        at = pl.multiple_of((place ^ k) * rows, 8)
        copies.append(
            pltpu.make_async_copy(scratch[i], out_ref.at[pl.ds(at, rows), pl.ds(start, cut)], sems.at[i])
        )
        copies[-1].start()
    token[...] = jnp.zeros_like(token)
    for copy in copies:
        copy.wait()


def final(parts, scale, model, out):
    spots, pieces = [(k, start) for k, start, _ in parts], [piece for _, _, piece in parts]
    earlier = [] if out is None else [out]
    return pl.pallas_call(
        functools.partial(final_kernel, spots, scale),
        out_shape=[
            jax.ShapeDtypeStruct((4 * pieces[0].shape[0], model), F32),
            jax.ShapeDtypeStruct((8, PADDED), F32),
        ],
        in_specs=[VMEM] * len(pieces) + [HBM] * len(earlier),
        out_specs=[HBM, VMEM],
        scratch_shapes=[pltpu.SemaphoreType.DMA((len(pieces),))] + [pltpu.VMEM(p.shape, F32) for p in pieces],
        input_output_aliases={len(pieces): 0} if earlier else {},
        compiler_params=LIMIT,
        cost_estimate=SMALL,
        name="final",
    )(*pieces, *earlier)


def add_kernel(a_ref, b_ref, *refs):
    refs[-1][...] = (a_ref[...].astype(F32) + b_ref[...].astype(F32)).astype(BF16)


def add(a, b, *after):
    return pl.pallas_call(
        add_kernel,
        out_shape=jax.ShapeDtypeStruct(a.shape, BF16),
        in_specs=[VMEM, VMEM] + [ANY] * len(after),
        out_specs=VMEM,
        compiler_params=LIMIT,
        cost_estimate=SMALL,
        name="add",
    )(a, b, *after)


def split_sum_kernel(a_ref, b_ref, *refs):
    sent, kept = refs[-2:]
    total = a_ref[...].astype(F32) + b_ref[...].astype(F32)
    half = sent.shape[0]
    low = line_bit() == 0
    sent[...] = jnp.where(low, total[half:], total[:half]).astype(BF16)
    kept[...] = jnp.where(low, total[:half], total[half:]).astype(BF16)


def split_sum(a, b, *after):
    rows, columns = a.shape
    return pl.pallas_call(
        split_sum_kernel,
        out_shape=[jax.ShapeDtypeStruct((rows // 2, columns), BF16)] * 2,
        in_specs=[VMEM, VMEM] + [ANY] * len(after),
        out_specs=[VMEM] * 2,
        compiler_params=LIMIT,
        cost_estimate=SMALL,
        name="split_sum",
    )(a, b, *after)


def body(features, segment_ids, projections, cotangent):
    n, count = lax.axis_size("seq"), lax.axis_size("dp")
    model, width = features.shape[2], projections.shape[1]
    scale = 1.0 / count
    shares = cotangent_shares(cotangent[0], n)

    def meanwhile(own):
        return [project(projections, own), shares[0]]

    blocks, (own_piece, _) = gather_blocks(features[0], "seq", meanwhile)
    cots = [shares[0]] + [swap(shares[k], "seq", k) for k in range(1, n)]

    def flat(some):
        return [part for block in some for part in block]

    pieces = [own_piece]
    if n > 2:
        pieces.append(project(projections, flat(blocks[1 : n - 1])))
    weights = attention_weights(segment_ids, projections, pieces, flat(blocks[n - 1 :]), n)
    split = gradient(weights, cots, flat(blocks), "dp")

    contexts = contexts_of(weights, projections, flat(blocks), n)
    received = [contexts[0]] + [swap(contexts[k], "seq", k) for k in range(1, n)]
    context, context_token = assemble_context(received)

    masks = [1 << b for b in range(2, count.bit_length() - 1)]
    aligned = width % 32 == 0
    value_grad, start, sums, left = None, 0, [], []
    after = contexts[:1]
    passed = [swap(sent, "dp", 2) for sent, _ in split]
    for i, (_, own) in enumerate(split):
        last = i == len(split) - 1
        total = add(own, passed[i], *after)
        for mask in masks:
            wait = []
            if mask == masks[-1]:
                wait = [context_token] if last else passed[i + 1 : i + 2] + received[1:3]
                if i:
                    wait.append(sums[-1][2])
                    if aligned:
                        wait.append(token)
            total = add(total, swap(total, "dp", mask), *wait)
        after = [total]
        got = swap(total, "dp", 2)
        four = [total, swap(total, "dp", 1), got, swap(got, "dp", 1)]
        sums.append(four)
        if aligned:
            near = [(0, start, four[0]), (2, start, four[1])]
            value_grad, token = final(left + near, scale, model, value_grad)
            left = [(1, start, four[2]), (3, start, four[3])]
        start += total.shape[1]
    if aligned:
        value_grad, _ = final(left, scale, model, value_grad)
    if not aligned:
        chunks = []
        for kept, far_kept, got, far_got in sums:
            low = line_bit() == 0
            near = jnp.where(low, jnp.concatenate([kept, got]), jnp.concatenate([got, kept]))
            far = jnp.where(low, jnp.concatenate([far_kept, far_got]), jnp.concatenate([far_got, far_kept]))
            chunks.append(jnp.where(core_index() == 0, jnp.concatenate([near, far]), jnp.concatenate([far, near])))
        value_grad = jnp.concatenate(chunks, axis=1).astype(F32) * scale
    return context[None], value_grad


def solution(mesh):
    in_specs = (P("dp", "seq", None), P("dp", None), P(None, "seq", None), P("dp", "seq", None))
    out_specs = (P("dp", "seq", None), P("seq", None))
    return jax.shard_map(body, mesh=mesh, in_specs=in_specs, out_specs=out_specs, check_vma=False)
```

```python
import functools

import jax
import jax.numpy as jnp
from jax import lax
from jax.experimental import pallas as pl
from jax.experimental.pallas import tpu as pltpu
from jax.sharding import PartitionSpec as P

HEAD = 120
PADDED = 128
BF16 = jnp.bfloat16
F32 = jnp.float32
VMEM = pl.BlockSpec(memory_space=pltpu.VMEM)
ANY = pl.BlockSpec(memory_space=pl.ANY)
HBM = pl.BlockSpec(memory_space=pltpu.HBM)
LIMIT = pltpu.CompilerParams(vmem_limit_bytes=12 * 1024 * 1024)
SMALL = pl.CostEstimate(flops=1000, bytes_accessed=1000, transcendentals=0)
LARGE = pl.CostEstimate(flops=2_000_000_000, bytes_accessed=4_000_000, transcendentals=0)
CUTS = (1024, 896)


def core_index():
    return lax.axis_index("dp") % 2


def line_bit():
    return lax.axis_index("dp") // 2 % 2


def swap(array, axis, mask):
    return lax.ppermute(array, axis, [(i, i ^ mask) for i in range(lax.axis_size(axis))])


def halves_kernel(x_ref, top_ref, bottom_ref, sems):
    half = top_ref.shape[0]
    copies = [
        pltpu.make_async_copy(x_ref.at[pl.ds(i * half, half)], out, sems.at[i])
        for i, out in enumerate((top_ref, bottom_ref))
    ]
    for copy in copies:
        copy.start()
    for copy in copies:
        copy.wait()


def halves(block):
    rows, model = block.shape
    return pl.pallas_call(
        halves_kernel,
        out_shape=[jax.ShapeDtypeStruct((rows // 2, model), BF16)] * 2,
        in_specs=[HBM],
        out_specs=[VMEM] * 2,
        scratch_shapes=[pltpu.SemaphoreType.DMA((2,))],
        compiler_params=LIMIT,
        name="halves",
    )(block)


def gate(arrays, after, cost=SMALL):
    return pl.pallas_call(
        lambda *refs: None,
        out_shape=[jax.ShapeDtypeStruct(a.shape, a.dtype) for a in arrays],
        in_specs=[VMEM] * len(arrays) + [ANY] * len(after),
        out_specs=[VMEM] * len(arrays),
        input_output_aliases={i: i for i in range(len(arrays))},
        compiler_params=LIMIT,
        cost_estimate=cost,
        name="gate",
    )(*arrays, *after)


def gather_blocks(block, axis, meanwhile):
    n = lax.axis_size(axis)
    if n != 4:
        return [[block]] + [[swap(block, axis, k)] for k in range(1, n)], meanwhile([block])
    top, bottom = halves(block)
    made = meanwhile([top, bottom])
    top_x, bottom_y = gate([swap(top, axis, 1), swap(bottom, axis, 2)], made)
    bottom_x, top_y = swap(bottom, axis, 1), swap(top, axis, 2)
    top_xy, bottom_xy = swap(top_x, axis, 2), swap(bottom_y, axis, 1)
    return [[top, bottom], [top_x, bottom_x], [top_y, bottom_y], [top_xy, bottom_xy]], made


def padded_head(rows, h):
    own = rows[h * HEAD : (h + 1) * HEAD]
    zeros = jnp.zeros((PADDED - HEAD, rows.shape[1]), F32)
    return jnp.concatenate([own, zeros], axis=0).astype(BF16)


def shares_kernel(cot_ref, *refs):
    outs, turned = refs[:-1], refs[-1]
    turned[...] = cot_ref[...].astype(F32).T
    width, me = outs[0].shape[0], lax.axis_index("seq")
    for k, out in enumerate(outs):
        start = pl.multiple_of((me ^ k) * width, 8)
        out[...] = turned[pl.ds(start, width), :].astype(BF16)


def cotangent_shares(cotangent, n):
    rows, model = cotangent.shape
    return pl.pallas_call(
        shares_kernel,
        out_shape=[jax.ShapeDtypeStruct((model // n, rows), BF16)] * n,
        in_specs=[VMEM],
        out_specs=[VMEM] * n,
        scratch_shapes=[pltpu.VMEM((model, rows), F32)],
        compiler_params=LIMIT,
        cost_estimate=SMALL,
        name="cotangent_shares",
    )(cotangent)


def project_into(w_ref, first, frames, out_ref):
    count, heads = out_ref.shape[:2]

    def one(t, carry):
        rows = lax.dot_general(
            w_ref[first + t], frames, (((1,), (1,)), ((), ())), preferred_element_type=F32
        )
        for h in range(heads):
            out_ref[t, h] = padded_head(rows, h)
        return carry

    lax.fori_loop(0, count, one, 0)


def project_kernel(w_ref, *refs):
    project_into(w_ref, 0, jnp.concatenate([r[...] for r in refs[:-1]], axis=0), refs[-1])


def project(weights, blocks):
    rows = sum(b.shape[0] for b in blocks)
    heads = weights.shape[1] // HEAD
    return pl.pallas_call(
        project_kernel,
        out_shape=jax.ShapeDtypeStruct((2, heads, PADDED, rows), BF16),
        in_specs=[VMEM] * (1 + len(blocks)),
        out_specs=VMEM,
        compiler_params=LIMIT,
        cost_estimate=SMALL,
        name="project",
    )(weights, *blocks)


def attention_kernel(parts, n, ids_ref, w_ref, *refs):
    pieces, last, out_ref = refs[:parts], refs[parts:-1], refs[-1]
    heads, total = out_ref.shape[:2]
    rows = total // n
    frames = jnp.concatenate([r[...] for r in last], axis=0)
    labels, me = [], lax.axis_index("seq")
    for k in range(n):
        start = pl.multiple_of((me ^ k) * rows, PADDED)
        labels.append(ids_ref[:, pl.ds(start, rows)].astype(F32))
    down = [jnp.broadcast_to(row, (PADDED, rows)).T for row in labels]
    column = jnp.concatenate(down, axis=0)
    step = max(PADDED, min(total, 512 * 512 // total))
    group = 2 if heads % 2 == 0 else 1
    for first in range(0, heads, group):
        own = [
            lax.dot_general(
                w_ref[t, first * HEAD : (first + group) * HEAD, :],
                frames,
                (((1,), (1,)), ((), ())),
                preferred_element_type=F32,
            )
            for t in range(2)
        ]
        for h in range(first, first + group):
            queries, keys = (
                jnp.concatenate([p[t, h] for p in pieces] + [padded_head(own[t], h - first)], axis=1)
                for t in range(2)
            )
            for at in range(0, total, step):
                scores = lax.dot_general(
                    keys, queries[:, at : at + step], (((0,), (0,)), ((), ())), preferred_element_type=F32
                )
                same = jnp.concatenate(
                    [column == labels[c // rows] for c in range(at, at + step, rows)], axis=1
                )
                scores = jnp.where(same, scores * HEAD**-0.5, -1e30)
                exponent = jnp.exp(scores - jnp.max(scores, axis=0, keepdims=True))
                inverse = 1.0 / jnp.sum(exponent, axis=0, keepdims=True)
                out_ref[h, :, at : at + step] = (exponent * inverse).astype(BF16)


def attention_weights(ids, weights, pieces, last, n):
    heads, total = weights.shape[1] // HEAD, ids.shape[1]
    return pl.pallas_call(
        functools.partial(attention_kernel, len(pieces), n),
        out_shape=jax.ShapeDtypeStruct((heads, total, total), BF16),
        in_specs=[VMEM] * (2 + len(pieces) + len(last)),
        out_specs=VMEM,
        compiler_params=LIMIT,
        cost_estimate=SMALL,
        name="attention_weights",
    )(ids, weights, *pieces, *last)


def gradient_into(values, blocks, outs, cuts):
    core = core_index()
    for (start, cut), theirs, mine in zip(cuts, outs[::2], outs[1::2]):
        frames = jnp.concatenate([b[:, start : start + cut] for b in blocks], axis=0)
        grads = jnp.dot(values, frames, preferred_element_type=F32)
        half = theirs.shape[0]
        theirs[...] = jnp.where(core == 0, grads[half:], grads[:half]).astype(BF16)
        mine[...] = jnp.where(core == 0, grads[:half], grads[half:]).astype(BF16)


def first_gradient_kernel(n, cuts, weights_ref, *refs):
    cots, blocks, outs = refs[:n], refs[n : -1 - 2 * len(cuts)], refs[-1 - 2 * len(cuts) :]
    upstream = jnp.concatenate([c[...] for c in cots], axis=1).astype(F32)
    rows = []
    for h in range(weights_ref.shape[0]):
        rows.append(
            lax.dot_general(
                padded_head(upstream, h), weights_ref[h], (((1,), (1,)), ((), ())), preferred_element_type=F32
            )[:HEAD]
        )
    outs[0][...] = jnp.concatenate(rows, axis=0).astype(BF16)
    gradient_into(outs[0][...], blocks, outs[1:], cuts)


def next_gradient_kernel(cuts, values_ref, *refs):
    gradient_into(values_ref[...], refs[: -2 * len(cuts)], refs[-2 * len(cuts) :], cuts)


def gradient(weights, cots, blocks, axis):
    width, total, model = cots[0].shape[0], weights.shape[1], blocks[0].shape[1]
    cuts = [(sum(CUTS[:i]), cut) for i, cut in enumerate(CUTS)]

    def shapes(some):
        return [jax.ShapeDtypeStruct((width // 2, cut), BF16) for _, cut in some for _ in range(2)]

    values, theirs, mine = pl.pallas_call(
        functools.partial(first_gradient_kernel, len(cots), cuts[:1]),
        out_shape=[jax.ShapeDtypeStruct((width, total), BF16)] + shapes(cuts[:1]),
        in_specs=[VMEM] * (1 + len(cots) + len(blocks)),
        out_specs=[VMEM] * 3,
        compiler_params=LIMIT,
        cost_estimate=SMALL,
        name="first_gradient",
    )(weights, *cots, *blocks)
    passed = swap(theirs, axis, 1)
    outs = pl.pallas_call(
        functools.partial(next_gradient_kernel, cuts[1:]),
        out_shape=shapes(cuts[1:]),
        in_specs=[VMEM] * (1 + len(blocks)),
        out_specs=[VMEM] * (2 * len(cuts) - 2),
        compiler_params=LIMIT,
        cost_estimate=pl.CostEstimate(
            flops=4 * width * total * model, bytes_accessed=2 * total * model, transcendentals=0
        ),
        name="next_gradient",
    )(values, *blocks)
    split = [split_sum(mine, passed, outs[1])]
    for theirs, mine in zip(outs[::2], outs[1::2]):
        split.append(split_sum(mine, swap(theirs, axis, 1), split[-1][0]))
    return split


def context_kernel(n, weights_ref, w_ref, *refs):
    blocks, outs, values = refs[: -n - 1], refs[-n - 1 : -1], refs[-1]
    project_into(w_ref, 2, jnp.concatenate([r[...] for r in blocks], axis=0), values)
    rows = outs[0].shape[1]
    found = [
        jnp.dot(values[0, h], weights_ref[h], preferred_element_type=F32)[:HEAD]
        for h in range(weights_ref.shape[0])
    ]
    stacked = jnp.concatenate(found, axis=0)
    for k, out in enumerate(outs):
        out[...] = stacked[:, k * rows : (k + 1) * rows].astype(BF16)


def contexts_of(weights, projections, blocks, n):
    heads, total = weights.shape[:2]
    return pl.pallas_call(
        functools.partial(context_kernel, n),
        out_shape=[jax.ShapeDtypeStruct((heads * HEAD, total // n), BF16)] * n,
        in_specs=[VMEM] * (2 + len(blocks)),
        out_specs=[VMEM] * n,
        scratch_shapes=[pltpu.VMEM((1, heads, PADDED, total), BF16)],
        compiler_params=LIMIT,
        cost_estimate=SMALL,
        name="contexts",
    )(weights, projections, *blocks)


def assemble_kernel(*refs):
    n = len(refs) - 3
    out, token, turned = refs[n:]
    width, me = refs[0].shape[0], lax.axis_index("seq")
    for k in range(n):
        start = pl.multiple_of((me ^ k) * width, 8)
        turned[pl.ds(start, width), :] = refs[k][...].astype(F32)
    out[...] = turned[...].T.astype(BF16)
    token[...] = jnp.zeros_like(token)


def assemble_context(pieces):
    n, (width, rows) = len(pieces), pieces[0].shape
    return pl.pallas_call(
        assemble_kernel,
        out_shape=[jax.ShapeDtypeStruct((rows, n * width), BF16), jax.ShapeDtypeStruct((8, PADDED), F32)],
        in_specs=[VMEM] * n,
        out_specs=[VMEM] * 2,
        scratch_shapes=[pltpu.VMEM((n * width, rows), F32)],
        compiler_params=LIMIT,
        cost_estimate=SMALL,
        name="assemble_context",
    )(*pieces)


def final_kernel(start, scale, *refs):
    pieces, (out_ref, scratch, sem) = refs[:4], refs[-3:]
    rows, cut = pieces[0].shape
    place = 2 * core_index() + line_bit()
    for k, piece in enumerate(pieces):
        at = pl.multiple_of((place ^ k) * rows, 8)
        scratch[pl.ds(at, rows), :] = piece[...].astype(F32) * scale
    copy = pltpu.make_async_copy(scratch, out_ref.at[:, pl.ds(start, cut)], sem)
    copy.start()
    copy.wait()


def final(pieces, start, scale, model, out):
    rows, cut = pieces[0].shape
    earlier = [] if out is None else [out]
    return pl.pallas_call(
        functools.partial(final_kernel, start, scale),
        out_shape=jax.ShapeDtypeStruct((4 * rows, model), F32),
        in_specs=[VMEM] * 4 + [HBM] * len(earlier),
        out_specs=HBM,
        scratch_shapes=[pltpu.VMEM((4 * rows, cut), F32), pltpu.SemaphoreType.DMA],
        input_output_aliases={4: 0} if earlier else {},
        compiler_params=LIMIT,
        cost_estimate=SMALL,
        name="final",
    )(*pieces, *earlier)


def add_kernel(a_ref, b_ref, *refs):
    refs[-1][...] = (a_ref[...].astype(F32) + b_ref[...].astype(F32)).astype(BF16)


def add(a, b, *after):
    return pl.pallas_call(
        add_kernel,
        out_shape=jax.ShapeDtypeStruct(a.shape, BF16),
        in_specs=[VMEM, VMEM] + [ANY] * len(after),
        out_specs=VMEM,
        compiler_params=LIMIT,
        cost_estimate=SMALL,
        name="add",
    )(a, b, *after)


def split_sum_kernel(a_ref, b_ref, *refs):
    sent, kept = refs[-2:]
    total = a_ref[...].astype(F32) + b_ref[...].astype(F32)
    half = sent.shape[0]
    low = line_bit() == 0
    sent[...] = jnp.where(low, total[half:], total[:half]).astype(BF16)
    kept[...] = jnp.where(low, total[:half], total[half:]).astype(BF16)


def split_sum(a, b, *after):
    rows, columns = a.shape
    return pl.pallas_call(
        split_sum_kernel,
        out_shape=[jax.ShapeDtypeStruct((rows // 2, columns), BF16)] * 2,
        in_specs=[VMEM, VMEM] + [ANY] * len(after),
        out_specs=[VMEM] * 2,
        compiler_params=LIMIT,
        cost_estimate=SMALL,
        name="split_sum",
    )(a, b, *after)


def body(features, segment_ids, projections, cotangent):
    n, count = lax.axis_size("seq"), lax.axis_size("dp")
    model, width = features.shape[2], projections.shape[1]
    scale = 1.0 / count
    shares = cotangent_shares(cotangent[0], n)

    def meanwhile(own):
        return [project(projections, own), shares[0]]

    blocks, (own_piece, _) = gather_blocks(features[0], "seq", meanwhile)
    cots = [shares[0]] + [swap(shares[k], "seq", k) for k in range(1, n)]

    def flat(some):
        return [part for block in some for part in block]

    pieces = [own_piece]
    if n > 2:
        pieces.append(project(projections, flat(blocks[1 : n - 1])))
    weights = attention_weights(segment_ids, projections, pieces, flat(blocks[n - 1 :]), n)
    split = gradient(weights, cots, flat(blocks), "dp")

    contexts = contexts_of(weights, projections, flat(blocks), n)
    received = [contexts[0]] + [swap(contexts[k], "seq", k) for k in range(1, n)]
    context, context_token = assemble_context(received)

    masks = [1 << b for b in range(2, count.bit_length() - 1)]
    aligned = width % 32 == 0
    passed = [swap(sent, "dp", 2) for sent, _ in split]
    value_grad, start, sums, after = None, 0, [], contexts[:1]
    for i, (_, own) in enumerate(split):
        last = i == len(split) - 1
        total = add(own, passed[i], *after)
        for mask in masks:
            got = swap(total, "dp", mask)
            wait = []
            if mask == masks[-1]:
                wait = [context_token] if last else passed[i + 1 : i + 2] + received[1:3]
                if i:
                    wait.append(sums[-1][1])
                    (got,) = gate([got], [], LARGE)
            total = add(total, got, *wait)
        after = [total]
        got = swap(total, "dp", 2)
        four = [total, got, swap(total, "dp", 1), swap(got, "dp", 1)]
        sums.append(four)
        if aligned:
            value_grad = final(four, start, scale, model, value_grad)
        start += total.shape[1]
    if not aligned:
        chunks = []
        for kept, got, far_kept, far_got in sums:
            low = line_bit() == 0
            near = jnp.where(low, jnp.concatenate([kept, got]), jnp.concatenate([got, kept]))
            far = jnp.where(low, jnp.concatenate([far_kept, far_got]), jnp.concatenate([far_got, far_kept]))
            chunks.append(jnp.where(core_index() == 0, jnp.concatenate([near, far]), jnp.concatenate([far, near])))
        value_grad = jnp.concatenate(chunks, axis=1).astype(F32) * scale
    return context[None], value_grad


def solution(mesh):
    in_specs = (P("dp", "seq", None), P("dp", None), P(None, "seq", None), P("dp", "seq", None))
    out_specs = (P("dp", "seq", None), P("seq", None))
    return jax.shard_map(body, mesh=mesh, in_specs=in_specs, out_specs=out_specs, check_vma=False)
```

```python
import functools

import jax
import jax.numpy as jnp
from jax import lax
from jax.experimental import pallas as pl
from jax.experimental.pallas import tpu as pltpu
from jax.sharding import PartitionSpec as P

HEAD = 120
PADDED = 128
BF16 = jnp.bfloat16
F32 = jnp.float32
VMEM = pl.BlockSpec(memory_space=pltpu.VMEM)
ANY = pl.BlockSpec(memory_space=pl.ANY)
HBM = pl.BlockSpec(memory_space=pltpu.HBM)
LIMIT = pltpu.CompilerParams(vmem_limit_bytes=12 * 1024 * 1024)
SMALL = pl.CostEstimate(flops=1000, bytes_accessed=1000, transcendentals=0)
CUTS = (640, 640, 640)


def core_index():
    return lax.axis_index("dp") % 2


def line_bit():
    return lax.axis_index("dp") // 2 % 2


def swap(array, axis, mask):
    return lax.ppermute(array, axis, [(i, i ^ mask) for i in range(lax.axis_size(axis))])


def halves_kernel(x_ref, top_ref, bottom_ref, sems):
    half = top_ref.shape[0]
    copies = [
        pltpu.make_async_copy(x_ref.at[pl.ds(i * half, half)], out, sems.at[i])
        for i, out in enumerate((top_ref, bottom_ref))
    ]
    for copy in copies:
        copy.start()
    for copy in copies:
        copy.wait()


def halves(block):
    rows, model = block.shape
    return pl.pallas_call(
        halves_kernel,
        out_shape=[jax.ShapeDtypeStruct((rows // 2, model), BF16)] * 2,
        in_specs=[HBM],
        out_specs=[VMEM] * 2,
        scratch_shapes=[pltpu.SemaphoreType.DMA((2,))],
        compiler_params=pltpu.CompilerParams(vmem_limit_bytes=60 * 1024 * 1024),
        name="halves",
    )(block)


def gate(arrays, after):
    return pl.pallas_call(
        lambda *refs: None,
        out_shape=[jax.ShapeDtypeStruct(a.shape, a.dtype) for a in arrays],
        in_specs=[VMEM] * len(arrays) + [ANY] * len(after),
        out_specs=[VMEM] * len(arrays),
        input_output_aliases={i: i for i in range(len(arrays))},
        compiler_params=LIMIT,
        cost_estimate=SMALL,
        name="gate",
    )(*arrays, *after)


def gather_blocks(block, axis, meanwhile):
    n = lax.axis_size(axis)
    if n != 4:
        return [[block]] + [[swap(block, axis, k)] for k in range(1, n)], meanwhile([block])
    top, bottom = halves(block)
    made = meanwhile([top, bottom])
    top_x, bottom_y = gate([swap(top, axis, 1), swap(bottom, axis, 2)], made)
    bottom_x, top_y = swap(bottom, axis, 1), swap(top, axis, 2)
    top_xy, bottom_xy = swap(top_x, axis, 2), swap(bottom_y, axis, 1)
    return [[top, bottom], [top_x, bottom_x], [top_y, bottom_y], [top_xy, bottom_xy]], made


def padded_head(rows, h):
    own = rows[h * HEAD : (h + 1) * HEAD]
    zeros = jnp.zeros((PADDED - HEAD, rows.shape[1]), F32)
    return jnp.concatenate([own, zeros], axis=0).astype(BF16)


def shares_kernel(cot_ref, *refs):
    outs, turned = refs[:-1], refs[-1]
    turned[...] = cot_ref[...].astype(F32).T
    width, me = outs[0].shape[0], lax.axis_index("seq")
    for k, out in enumerate(outs):
        start = pl.multiple_of((me ^ k) * width, 8)
        out[...] = turned[pl.ds(start, width), :].astype(BF16)


def cotangent_shares(cotangent, n):
    rows, model = cotangent.shape
    return pl.pallas_call(
        shares_kernel,
        out_shape=[jax.ShapeDtypeStruct((model // n, rows), BF16)] * n,
        in_specs=[VMEM],
        out_specs=[VMEM] * n,
        scratch_shapes=[pltpu.VMEM((model, rows), F32)],
        compiler_params=LIMIT,
        cost_estimate=SMALL,
        name="cotangent_shares",
    )(cotangent)


def project_into(w_ref, first, frames, out_ref):
    count, heads = out_ref.shape[:2]

    def one(t, carry):
        rows = lax.dot_general(
            w_ref[first + t], frames, (((1,), (1,)), ((), ())), preferred_element_type=F32
        )
        for h in range(heads):
            out_ref[t, h] = padded_head(rows, h)
        return carry

    lax.fori_loop(0, count, one, 0)


def project_kernel(w_ref, *refs):
    project_into(w_ref, 0, jnp.concatenate([r[...] for r in refs[:-1]], axis=0), refs[-1])


def project(weights, blocks):
    rows = sum(b.shape[0] for b in blocks)
    heads = weights.shape[1] // HEAD
    return pl.pallas_call(
        project_kernel,
        out_shape=jax.ShapeDtypeStruct((2, heads, PADDED, rows), BF16),
        in_specs=[VMEM] * (1 + len(blocks)),
        out_specs=VMEM,
        compiler_params=LIMIT,
        cost_estimate=SMALL,
        name="project",
    )(weights, *blocks)


def attention_kernel(parts, n, ids_ref, w_ref, *refs):
    pieces, last, out_ref = refs[:parts], refs[parts:-1], refs[-1]
    heads, total = out_ref.shape[:2]
    rows = total // n
    frames = jnp.concatenate([r[...] for r in last], axis=0)
    labels, me = [], lax.axis_index("seq")
    for k in range(n):
        start = pl.multiple_of((me ^ k) * rows, PADDED)
        labels.append(ids_ref[:, pl.ds(start, rows)].astype(F32))
    down = [jnp.broadcast_to(row, (PADDED, rows)).T for row in labels]
    column = jnp.concatenate(down, axis=0)
    step = max(PADDED, min(total, 512 * 512 // total))
    group = 2 if heads % 2 == 0 else 1
    for first in range(0, heads, group):
        own = [
            lax.dot_general(
                w_ref[t, first * HEAD : (first + group) * HEAD, :],
                frames,
                (((1,), (1,)), ((), ())),
                preferred_element_type=F32,
            )
            for t in range(2)
        ]
        for h in range(first, first + group):
            queries, keys = (
                jnp.concatenate([p[t, h] for p in pieces] + [padded_head(own[t], h - first)], axis=1)
                for t in range(2)
            )
            for at in range(0, total, step):
                scores = lax.dot_general(
                    keys, queries[:, at : at + step], (((0,), (0,)), ((), ())), preferred_element_type=F32
                )
                same = jnp.concatenate(
                    [column == labels[c // rows] for c in range(at, at + step, rows)], axis=1
                )
                scores = jnp.where(same, scores * HEAD**-0.5, -1e30)
                exponent = jnp.exp(scores - jnp.max(scores, axis=0, keepdims=True))
                inverse = 1.0 / jnp.sum(exponent, axis=0, keepdims=True)
                out_ref[h, :, at : at + step] = (exponent * inverse).astype(BF16)


def attention_weights(ids, weights, pieces, last, n):
    heads, total = weights.shape[1] // HEAD, ids.shape[1]
    return pl.pallas_call(
        functools.partial(attention_kernel, len(pieces), n),
        out_shape=jax.ShapeDtypeStruct((heads, total, total), BF16),
        in_specs=[VMEM] * (2 + len(pieces) + len(last)),
        out_specs=VMEM,
        compiler_params=LIMIT,
        cost_estimate=SMALL,
        name="attention_weights",
    )(ids, weights, *pieces, *last)


def gradient_into(values, blocks, outs, cuts):
    core = core_index()
    for (start, cut), theirs, mine in zip(cuts, outs[::2], outs[1::2]):
        frames = jnp.concatenate([b[:, start : start + cut] for b in blocks], axis=0)
        grads = jnp.dot(values, frames, preferred_element_type=F32)
        half = theirs.shape[0]
        theirs[...] = jnp.where(core == 0, grads[half:], grads[:half]).astype(BF16)
        mine[...] = jnp.where(core == 0, grads[:half], grads[half:]).astype(BF16)


def first_gradient_kernel(n, cuts, weights_ref, *refs):
    cots, blocks, outs = refs[:n], refs[n : -1 - 2 * len(cuts)], refs[-1 - 2 * len(cuts) :]
    upstream = jnp.concatenate([c[...] for c in cots], axis=1).astype(F32)
    rows = []
    for h in range(weights_ref.shape[0]):
        rows.append(
            lax.dot_general(
                padded_head(upstream, h), weights_ref[h], (((1,), (1,)), ((), ())), preferred_element_type=F32
            )[:HEAD]
        )
    outs[0][...] = jnp.concatenate(rows, axis=0).astype(BF16)
    gradient_into(outs[0][...], blocks, outs[1:], cuts)


def next_gradient_kernel(cuts, values_ref, *refs):
    gradient_into(values_ref[...], refs[: -2 * len(cuts)], refs[-2 * len(cuts) :], cuts)


def gradient(weights, cots, blocks):
    width, total, model = cots[0].shape[0], weights.shape[1], blocks[0].shape[1]
    cuts = [(sum(CUTS[:i]), cut) for i, cut in enumerate(CUTS)]

    def shapes(some):
        return [jax.ShapeDtypeStruct((width // 2, cut), BF16) for _, cut in some for _ in range(2)]

    values, theirs, mine = pl.pallas_call(
        functools.partial(first_gradient_kernel, len(cots), cuts[:1]),
        out_shape=[jax.ShapeDtypeStruct((width, total), BF16)] + shapes(cuts[:1]),
        in_specs=[VMEM] * (1 + len(cots) + len(blocks)),
        out_specs=[VMEM] * 3,
        compiler_params=LIMIT,
        cost_estimate=SMALL,
        name="first_gradient",
    )(weights, *cots, *blocks)
    outs = pl.pallas_call(
        functools.partial(next_gradient_kernel, cuts[1:]),
        out_shape=shapes(cuts[1:]),
        in_specs=[VMEM] * (1 + len(blocks)),
        out_specs=[VMEM] * (2 * len(cuts) - 2),
        compiler_params=LIMIT,
        cost_estimate=pl.CostEstimate(
            flops=4 * width * total * model, bytes_accessed=2 * total * model, transcendentals=0
        ),
        name="next_gradient",
    )(values, *blocks)
    return [(theirs, mine)] + list(zip(outs[::2], outs[1::2]))


def context_kernel(n, weights_ref, w_ref, *refs):
    blocks, outs, values = refs[: -n - 1], refs[-n - 1 : -1], refs[-1]
    project_into(w_ref, 2, jnp.concatenate([r[...] for r in blocks], axis=0), values)
    rows = outs[0].shape[1]
    found = [
        jnp.dot(values[0, h], weights_ref[h], preferred_element_type=F32)[:HEAD]
        for h in range(weights_ref.shape[0])
    ]
    stacked = jnp.concatenate(found, axis=0)
    for k, out in enumerate(outs):
        out[...] = stacked[:, k * rows : (k + 1) * rows].astype(BF16)


def contexts_of(weights, projections, blocks, n):
    heads, total = weights.shape[:2]
    return pl.pallas_call(
        functools.partial(context_kernel, n),
        out_shape=[jax.ShapeDtypeStruct((heads * HEAD, total // n), BF16)] * n,
        in_specs=[VMEM] * (2 + len(blocks)),
        out_specs=[VMEM] * n,
        scratch_shapes=[pltpu.VMEM((1, heads, PADDED, total), BF16)],
        compiler_params=LIMIT,
        cost_estimate=SMALL,
        name="contexts",
    )(weights, projections, *blocks)


def assemble_kernel(*refs):
    n = len(refs) - 3
    out, token, turned = refs[n:]
    width, me = refs[0].shape[0], lax.axis_index("seq")
    for k in range(n):
        start = pl.multiple_of((me ^ k) * width, 8)
        turned[pl.ds(start, width), :] = refs[k][...].astype(F32)
    out[...] = turned[...].T.astype(BF16)
    token[...] = jnp.zeros_like(token)


def assemble_context(pieces):
    n, (width, rows) = len(pieces), pieces[0].shape
    return pl.pallas_call(
        assemble_kernel,
        out_shape=[jax.ShapeDtypeStruct((rows, n * width), BF16), jax.ShapeDtypeStruct((8, PADDED), F32)],
        in_specs=[VMEM] * n,
        out_specs=[VMEM] * 2,
        scratch_shapes=[pltpu.VMEM((n * width, rows), F32)],
        compiler_params=LIMIT,
        cost_estimate=SMALL,
        name="assemble_context",
    )(*pieces)


def final_kernel(start, scale, *refs):
    pieces, (out_ref, token, scratch, sem) = refs[:4], refs[-4:]
    rows, cut = pieces[0].shape
    place = 2 * core_index() + line_bit()
    for k, piece in enumerate(pieces):
        at = pl.multiple_of((place ^ k) * rows, 8)
        scratch[pl.ds(at, rows), :] = piece[...].astype(F32) * scale
    copy = pltpu.make_async_copy(scratch, out_ref.at[:, pl.ds(start, cut)], sem)
    copy.start()
    token[...] = jnp.zeros_like(token)
    copy.wait()


def final(pieces, start, scale, model, out):
    rows, cut = pieces[0].shape
    earlier = [] if out is None else [out]
    return pl.pallas_call(
        functools.partial(final_kernel, start, scale),
        out_shape=[jax.ShapeDtypeStruct((4 * rows, model), F32), jax.ShapeDtypeStruct((8, PADDED), F32)],
        in_specs=[VMEM] * 4 + [HBM] * len(earlier),
        out_specs=[HBM, VMEM],
        scratch_shapes=[pltpu.VMEM((4 * rows, cut), F32), pltpu.SemaphoreType.DMA],
        input_output_aliases={4: 0} if earlier else {},
        compiler_params=LIMIT,
        cost_estimate=SMALL,
        name="final",
    )(*pieces, *earlier)


def add_kernel(a_ref, b_ref, *refs):
    refs[-1][...] = (a_ref[...].astype(F32) + b_ref[...].astype(F32)).astype(BF16)


def add(a, b, *after):
    return pl.pallas_call(
        add_kernel,
        out_shape=jax.ShapeDtypeStruct(a.shape, BF16),
        in_specs=[VMEM, VMEM] + [ANY] * len(after),
        out_specs=VMEM,
        compiler_params=LIMIT,
        cost_estimate=SMALL,
        name="add",
    )(a, b, *after)


def split_sum_kernel(a_ref, b_ref, *refs):
    sent, kept = refs[-2:]
    total = a_ref[...].astype(F32) + b_ref[...].astype(F32)
    half = sent.shape[0]
    low = line_bit() == 0
    sent[...] = jnp.where(low, total[half:], total[:half]).astype(BF16)
    kept[...] = jnp.where(low, total[:half], total[half:]).astype(BF16)


def split_sum(a, b, *after):
    rows, columns = a.shape
    return pl.pallas_call(
        split_sum_kernel,
        out_shape=[jax.ShapeDtypeStruct((rows // 2, columns), BF16)] * 2,
        in_specs=[VMEM, VMEM] + [ANY] * len(after),
        out_specs=[VMEM] * 2,
        compiler_params=LIMIT,
        cost_estimate=SMALL,
        name="split_sum",
    )(a, b, *after)


def body(features, segment_ids, projections, cotangent):
    n, count = lax.axis_size("seq"), lax.axis_size("dp")
    model, width = features.shape[2], projections.shape[1]
    scale = 1.0 / count
    shares = cotangent_shares(cotangent[0], n)

    def meanwhile(own):
        return [project(projections, own), shares[0]]

    blocks, (own_piece, _) = gather_blocks(features[0], "seq", meanwhile)
    cots = [shares[0]] + [swap(shares[k], "seq", k) for k in range(1, n)]

    def flat(some):
        return [part for block in some for part in block]

    pieces = [own_piece]
    if n > 2:
        pieces.append(project(projections, flat(blocks[1 : n - 1])))
    weights = attention_weights(segment_ids, projections, pieces, flat(blocks[n - 1 :]), n)
    pairs = gradient(weights, cots, flat(blocks))

    contexts = contexts_of(weights, projections, flat(blocks), n)
    received = [contexts[0]] + [swap(contexts[k], "seq", k) for k in range(1, n)]
    context, context_token = assemble_context(received)

    masks = [1 << b for b in range(2, count.bit_length() - 1)]
    aligned = width % 32 == 0
    parts, split = [], []
    for i, (theirs, mine) in enumerate(pairs):
        if i < 2:
            after = split[0][:1] if i else pairs[-1][1:]
        else:
            after = parts[-1:]
        split.append(split_sum(mine, swap(theirs, "dp", 1), *after))
        sent, own = split[-1]
        parts.append(add(own, swap(sent, "dp", 2), *(parts[-1:] if i else contexts[:1])))
    value_grad, start, sums, tokens = None, 0, [], []
    for i, total in enumerate(parts):
        for mask in masks:
            wait = []
            if mask == masks[-1]:
                wait = [sums[-1][0]] if sums else parts[-1:] + received[1:3]
                wait += [context_token] if i == len(parts) - 1 else []
            total = add(total, swap(total, "dp", mask), *wait)
        got = swap(total, "dp", 2)
        if i > 1 and aligned:
            (got,) = gate([got], tokens[: i - 1])
        four = [total, got, swap(total, "dp", 1), swap(got, "dp", 1)]
        sums.append(four)
        if aligned:
            value_grad, token = final(four, start, scale, model, value_grad)
            tokens.append(token)
        start += total.shape[1]
    if not aligned:
        chunks = []
        for kept, got, far_kept, far_got in sums:
            low = line_bit() == 0
            near = jnp.where(low, jnp.concatenate([kept, got]), jnp.concatenate([got, kept]))
            far = jnp.where(low, jnp.concatenate([far_kept, far_got]), jnp.concatenate([far_got, far_kept]))
            chunks.append(jnp.where(core_index() == 0, jnp.concatenate([near, far]), jnp.concatenate([far, near])))
        value_grad = jnp.concatenate(chunks, axis=1).astype(F32) * scale
    return context[None], value_grad


def solution(mesh):
    in_specs = (P("dp", "seq", None), P("dp", None), P(None, "seq", None), P("dp", "seq", None))
    out_specs = (P("dp", "seq", None), P("seq", None))
    return jax.shard_map(body, mesh=mesh, in_specs=in_specs, out_specs=out_specs, check_vma=False)
```

```python
import functools

import jax
import jax.numpy as jnp
from jax import lax
from jax.experimental import pallas as pl
from jax.experimental.pallas import tpu as pltpu
from jax.sharding import PartitionSpec as P

HEAD = 120
PADDED = 128
BF16 = jnp.bfloat16
F32 = jnp.float32
VMEM = pl.BlockSpec(memory_space=pltpu.VMEM)
ANY = pl.BlockSpec(memory_space=pl.ANY)
HBM = pl.BlockSpec(memory_space=pltpu.HBM)
LIMIT = pltpu.CompilerParams(vmem_limit_bytes=12 * 1024 * 1024)
SMALL = pl.CostEstimate(flops=1000, bytes_accessed=1000, transcendentals=0)
LARGE = pl.CostEstimate(flops=2_000_000_000, bytes_accessed=4_000_000, transcendentals=0)
CUTS = (1024, 896)


def core_index():
    return lax.axis_index("dp") % 2


def line_bit():
    return lax.axis_index("dp") // 2 % 2


def swap(array, axis, mask):
    return lax.ppermute(array, axis, [(i, i ^ mask) for i in range(lax.axis_size(axis))])


def halves_kernel(x_ref, top_ref, bottom_ref):
    half = top_ref.shape[0]
    top_ref[...] = x_ref[:half]
    bottom_ref[...] = x_ref[half:]


def halves(block):
    rows, model = block.shape
    return pl.pallas_call(
        halves_kernel,
        out_shape=[jax.ShapeDtypeStruct((rows // 2, model), BF16)] * 2,
        in_specs=[VMEM],
        out_specs=[VMEM] * 2,
        compiler_params=LIMIT,
        cost_estimate=SMALL,
        name="halves",
    )(block)


def gate(arrays, after, cost=SMALL):
    return pl.pallas_call(
        lambda *refs: None,
        out_shape=[jax.ShapeDtypeStruct(a.shape, a.dtype) for a in arrays],
        in_specs=[VMEM] * len(arrays) + [ANY] * len(after),
        out_specs=[VMEM] * len(arrays),
        input_output_aliases={i: i for i in range(len(arrays))},
        compiler_params=LIMIT,
        cost_estimate=cost,
        name="gate",
    )(*arrays, *after)


def gather_blocks(block, axis, meanwhile):
    n = lax.axis_size(axis)
    if n != 4:
        return [[block]] + [[swap(block, axis, k)] for k in range(1, n)], meanwhile([block])
    top, bottom = halves(block)
    made = meanwhile([top, bottom])
    top_x, bottom_y = gate([swap(top, axis, 1), swap(bottom, axis, 2)], made)
    bottom_x, top_y = swap(bottom, axis, 1), swap(top, axis, 2)
    top_xy, bottom_xy = swap(top_x, axis, 2), swap(bottom_y, axis, 1)
    return [[top, bottom], [top_x, bottom_x], [top_y, bottom_y], [top_xy, bottom_xy]], made


def padded_head(rows, h):
    own = rows[h * HEAD : (h + 1) * HEAD]
    zeros = jnp.zeros((PADDED - HEAD, rows.shape[1]), F32)
    return jnp.concatenate([own, zeros], axis=0).astype(BF16)


def shares_kernel(cot_ref, *refs):
    outs, turned = refs[:-1], refs[-1]
    turned[...] = cot_ref[...].astype(F32).T
    width, me = outs[0].shape[0], lax.axis_index("seq")
    for k, out in enumerate(outs):
        start = pl.multiple_of((me ^ k) * width, 8)
        out[...] = turned[pl.ds(start, width), :].astype(BF16)


def cotangent_shares(cotangent, n):
    rows, model = cotangent.shape
    return pl.pallas_call(
        shares_kernel,
        out_shape=[jax.ShapeDtypeStruct((model // n, rows), BF16)] * n,
        in_specs=[VMEM],
        out_specs=[VMEM] * n,
        scratch_shapes=[pltpu.VMEM((model, rows), F32)],
        compiler_params=LIMIT,
        cost_estimate=SMALL,
        name="cotangent_shares",
    )(cotangent)


def project_into(w_ref, first, frames, out_ref):
    count, heads = out_ref.shape[:2]

    def one(t, carry):
        rows = lax.dot_general(
            w_ref[first + t], frames, (((1,), (1,)), ((), ())), preferred_element_type=F32
        )
        for h in range(heads):
            out_ref[t, h] = padded_head(rows, h)
        return carry

    lax.fori_loop(0, count, one, 0)


def project_kernel(w_ref, *refs):
    project_into(w_ref, 0, jnp.concatenate([r[...] for r in refs[:-1]], axis=0), refs[-1])


def project(weights, blocks):
    rows = sum(b.shape[0] for b in blocks)
    heads = weights.shape[1] // HEAD
    return pl.pallas_call(
        project_kernel,
        out_shape=jax.ShapeDtypeStruct((2, heads, PADDED, rows), BF16),
        in_specs=[VMEM] * (1 + len(blocks)),
        out_specs=VMEM,
        compiler_params=LIMIT,
        cost_estimate=SMALL,
        name="project",
    )(weights, *blocks)


def attention_kernel(parts, n, ids_ref, w_ref, *refs):
    pieces, last, out_ref = refs[:parts], refs[parts:-1], refs[-1]
    heads, total = out_ref.shape[:2]
    rows = total // n
    frames = jnp.concatenate([r[...] for r in last], axis=0)
    labels, me = [], lax.axis_index("seq")
    for k in range(n):
        start = pl.multiple_of((me ^ k) * rows, PADDED)
        labels.append(ids_ref[:, pl.ds(start, rows)].astype(F32))
    down = [jnp.broadcast_to(row, (PADDED, rows)).T for row in labels]
    column = jnp.concatenate(down, axis=0)
    step = max(PADDED, min(total, 512 * 512 // total))
    group = 2 if heads % 2 == 0 else 1
    for first in range(0, heads, group):
        own = [
            lax.dot_general(
                w_ref[t, first * HEAD : (first + group) * HEAD, :],
                frames,
                (((1,), (1,)), ((), ())),
                preferred_element_type=F32,
            )
            for t in range(2)
        ]
        for h in range(first, first + group):
            queries, keys = (
                jnp.concatenate([p[t, h] for p in pieces] + [padded_head(own[t], h - first)], axis=1)
                for t in range(2)
            )
            for at in range(0, total, step):
                scores = lax.dot_general(
                    keys, queries[:, at : at + step], (((0,), (0,)), ((), ())), preferred_element_type=F32
                )
                same = jnp.concatenate(
                    [column == labels[c // rows] for c in range(at, at + step, rows)], axis=1
                )
                scores = jnp.where(same, scores * HEAD**-0.5, -1e30)
                exponent = jnp.exp(scores - jnp.max(scores, axis=0, keepdims=True))
                inverse = 1.0 / jnp.sum(exponent, axis=0, keepdims=True)
                out_ref[h, :, at : at + step] = (exponent * inverse).astype(BF16)


def attention_weights(ids, weights, pieces, last, n):
    heads, total = weights.shape[1] // HEAD, ids.shape[1]
    return pl.pallas_call(
        functools.partial(attention_kernel, len(pieces), n),
        out_shape=jax.ShapeDtypeStruct((heads, total, total), BF16),
        in_specs=[VMEM] * (2 + len(pieces) + len(last)),
        out_specs=VMEM,
        compiler_params=LIMIT,
        cost_estimate=SMALL,
        name="attention_weights",
    )(ids, weights, *pieces, *last)


def rows_times(values_ref, mine, blocks, start, cut):
    half = values_ref.shape[0] // 2
    core = core_index()
    at = half * (core if mine else 1 - core)
    if half % 16 == 0:
        values = values_ref[pl.ds(pl.multiple_of(at, 16), half), :]
    else:
        values = values_ref[...].astype(F32)
        values = jnp.where(at == 0, values[:half], values[half:]).astype(BF16)
    frames = jnp.concatenate([b[:, start : start + cut] for b in blocks], axis=0)
    return jnp.dot(values, frames, preferred_element_type=F32).astype(BF16)


def first_gradient_kernel(n, cut, weights_ref, *refs):
    cots, blocks, (values_ref, theirs) = refs[:n], refs[n:-2], refs[-2:]
    upstream = jnp.concatenate([c[...] for c in cots], axis=1).astype(F32)
    rows = []
    for h in range(weights_ref.shape[0]):
        rows.append(
            lax.dot_general(
                padded_head(upstream, h), weights_ref[h], (((1,), (1,)), ((), ())), preferred_element_type=F32
            )[:HEAD]
        )
    values_ref[...] = jnp.concatenate(rows, axis=0).astype(BF16)
    theirs[...] = rows_times(values_ref, False, blocks, 0, cut)


def next_gradient_kernel(values_ref, *refs):
    outs, blocks = refs[1 - 2 * len(CUTS) :], refs[: 1 - 2 * len(CUTS)]
    start = 0
    for i, cut in enumerate(CUTS):
        for mine in (False, True) if i else (True,):
            outs[2 * i - 1 + mine][...] = rows_times(values_ref, mine, blocks, start, cut)
        start += cut


def gradient(weights, cots, blocks):
    width, total, model = cots[0].shape[0], weights.shape[1], blocks[0].shape[1]

    def shape(cut):
        return jax.ShapeDtypeStruct((width // 2, cut), BF16)

    values, first = pl.pallas_call(
        functools.partial(first_gradient_kernel, len(cots), CUTS[0]),
        out_shape=[jax.ShapeDtypeStruct((width, total), BF16), shape(CUTS[0])],
        in_specs=[VMEM] * (1 + len(cots) + len(blocks)),
        out_specs=[VMEM] * 2,
        compiler_params=LIMIT,
        cost_estimate=SMALL,
        name="first_gradient",
    )(weights, *cots, *blocks)
    outs = pl.pallas_call(
        next_gradient_kernel,
        out_shape=[shape(CUTS[0])] + [shape(cut) for cut in CUTS[1:] for _ in range(2)],
        in_specs=[VMEM] * (1 + len(blocks)),
        out_specs=[VMEM] * (2 * len(CUTS) - 1),
        compiler_params=LIMIT,
        cost_estimate=pl.CostEstimate(
            flops=4 * width * total * model, bytes_accessed=2 * total * model, transcendentals=0
        ),
        name="next_gradient",
    )(values, *blocks)
    outs = [first] + list(outs)
    return list(zip(outs[::2], outs[1::2]))


def context_kernel(n, weights_ref, w_ref, *refs):
    blocks, outs, values = refs[: -n - 1], refs[-n - 1 : -1], refs[-1]
    project_into(w_ref, 2, jnp.concatenate([r[...] for r in blocks], axis=0), values)
    rows = outs[0].shape[1]
    found = [
        jnp.dot(values[0, h], weights_ref[h], preferred_element_type=F32)[:HEAD]
        for h in range(weights_ref.shape[0])
    ]
    stacked = jnp.concatenate(found, axis=0)
    for k, out in enumerate(outs):
        out[...] = stacked[:, k * rows : (k + 1) * rows].astype(BF16)


def contexts_of(weights, projections, blocks, n):
    heads, total = weights.shape[:2]
    return pl.pallas_call(
        functools.partial(context_kernel, n),
        out_shape=[jax.ShapeDtypeStruct((heads * HEAD, total // n), BF16)] * n,
        in_specs=[VMEM] * (2 + len(blocks)),
        out_specs=[VMEM] * n,
        scratch_shapes=[pltpu.VMEM((1, heads, PADDED, total), BF16)],
        compiler_params=LIMIT,
        cost_estimate=SMALL,
        name="contexts",
    )(weights, projections, *blocks)


def assemble_kernel(*refs):
    n = len(refs) - 3
    out, token, turned = refs[n:]
    width, me = refs[0].shape[0], lax.axis_index("seq")
    for k in range(n):
        start = pl.multiple_of((me ^ k) * width, 8)
        turned[pl.ds(start, width), :] = refs[k][...].astype(F32)
    out[...] = turned[...].T.astype(BF16)
    token[...] = jnp.zeros_like(token)


def assemble_context(pieces):
    n, (width, rows) = len(pieces), pieces[0].shape
    return pl.pallas_call(
        assemble_kernel,
        out_shape=[jax.ShapeDtypeStruct((rows, n * width), BF16), jax.ShapeDtypeStruct((8, PADDED), F32)],
        in_specs=[VMEM] * n,
        out_specs=[VMEM] * 2,
        scratch_shapes=[pltpu.VMEM((n * width, rows), F32)],
        compiler_params=LIMIT,
        cost_estimate=LARGE,
        name="assemble_context",
    )(*pieces)


def final_kernel(start, scale, *refs):
    pieces, (out_ref, scratch, sem) = refs[:4], refs[-3:]
    rows, cut = pieces[0].shape
    place = 2 * core_index() + line_bit()
    for k, piece in enumerate(pieces):
        at = pl.multiple_of((place ^ k) * rows, 8)
        scratch[pl.ds(at, rows), :] = piece[...].astype(F32) * scale
    copy = pltpu.make_async_copy(scratch, out_ref.at[:, pl.ds(start, cut)], sem)
    copy.start()
    copy.wait()


def final(pieces, start, scale, model, out):
    rows, cut = pieces[0].shape
    earlier = [] if out is None else [out]
    return pl.pallas_call(
        functools.partial(final_kernel, start, scale),
        out_shape=jax.ShapeDtypeStruct((4 * rows, model), F32),
        in_specs=[VMEM] * 4 + [HBM] * len(earlier),
        out_specs=HBM,
        scratch_shapes=[pltpu.VMEM((4 * rows, cut), F32), pltpu.SemaphoreType.DMA],
        input_output_aliases={4: 0} if earlier else {},
        compiler_params=LIMIT,
        cost_estimate=SMALL,
        name="final",
    )(*pieces, *earlier)


def add_kernel(a_ref, b_ref, *refs):
    refs[-1][...] = (a_ref[...].astype(F32) + b_ref[...].astype(F32)).astype(BF16)


def add(a, b, *after):
    return pl.pallas_call(
        add_kernel,
        out_shape=jax.ShapeDtypeStruct(a.shape, BF16),
        in_specs=[VMEM, VMEM] + [ANY] * len(after),
        out_specs=VMEM,
        compiler_params=LIMIT,
        cost_estimate=SMALL,
        name="add",
    )(a, b, *after)


def split_sum_kernel(a_ref, b_ref, *refs):
    sent, kept = refs[-2:]
    total = a_ref[...].astype(F32) + b_ref[...].astype(F32)
    half = sent.shape[0]
    low = line_bit() == 0
    sent[...] = jnp.where(low, total[half:], total[:half]).astype(BF16)
    kept[...] = jnp.where(low, total[:half], total[half:]).astype(BF16)


def split_sum(a, b, *after):
    rows, columns = a.shape
    return pl.pallas_call(
        split_sum_kernel,
        out_shape=[jax.ShapeDtypeStruct((rows // 2, columns), BF16)] * 2,
        in_specs=[VMEM, VMEM] + [ANY] * len(after),
        out_specs=[VMEM] * 2,
        compiler_params=LIMIT,
        cost_estimate=SMALL,
        name="split_sum",
    )(a, b, *after)


def body(features, segment_ids, projections, cotangent):
    n, count = lax.axis_size("seq"), lax.axis_size("dp")
    model, width = features.shape[2], projections.shape[1]
    scale = 1.0 / count
    shares = cotangent_shares(cotangent[0], n)

    def meanwhile(own):
        return [project(projections, own), shares[0]]

    blocks, (own_piece, _) = gather_blocks(features[0], "seq", meanwhile)
    cots = [shares[0]] + [swap(shares[k], "seq", k) for k in range(1, n)]

    def flat(some):
        return [part for block in some for part in block]

    pieces = [own_piece]
    if n > 2:
        pieces.append(project(projections, flat(blocks[1 : n - 1])))
    weights = attention_weights(segment_ids, projections, pieces, flat(blocks[n - 1 :]), n)
    split = []
    for theirs, mine in gradient(weights, cots, flat(blocks)):
        split.append(split_sum(mine, swap(theirs, "dp", 1), *(split[-1][:1] if split else ())))

    contexts = contexts_of(weights, projections, flat(blocks), n)
    received = [contexts[0]] + [swap(contexts[k], "seq", k) for k in range(1, n)]
    context, context_token = assemble_context(received)

    masks = [1 << b for b in range(2, count.bit_length() - 1)]
    aligned = width % 32 == 0
    passed = [swap(sent, "dp", 2) for sent, _ in split]
    value_grad, start, sums, after = None, 0, [], contexts[:1]
    for i, (_, own) in enumerate(split):
        last = i == len(split) - 1
        total = add(own, passed[i], *after)
        for mask in masks:
            got = swap(total, "dp", mask)
            wait = []
            if mask == masks[-1]:
                wait = [context_token] if last else passed[i + 1 : i + 2] + received[1:3]
                if i:
                    wait.append(sums[-1][1])
                    (got,) = gate([got], [], LARGE)
            total = add(total, got, *wait)
        after = [total]
        got = swap(total, "dp", 2)
        four = [total, got, swap(total, "dp", 1), swap(got, "dp", 1)]
        sums.append(four)
        if aligned:
            value_grad = final(four, start, scale, model, value_grad)
        start += total.shape[1]
    if not aligned:
        chunks = []
        for kept, got, far_kept, far_got in sums:
            low = line_bit() == 0
            near = jnp.where(low, jnp.concatenate([kept, got]), jnp.concatenate([got, kept]))
            far = jnp.where(low, jnp.concatenate([far_kept, far_got]), jnp.concatenate([far_got, far_kept]))
            chunks.append(jnp.where(core_index() == 0, jnp.concatenate([near, far]), jnp.concatenate([far, near])))
        value_grad = jnp.concatenate(chunks, axis=1).astype(F32) * scale
    return context[None], value_grad


def solution(mesh):
    in_specs = (P("dp", "seq", None), P("dp", None), P(None, "seq", None), P("dp", "seq", None))
    out_specs = (P("dp", "seq", None), P("seq", None))
    return jax.shard_map(body, mesh=mesh, in_specs=in_specs, out_specs=out_specs, check_vma=False)
```

```python
import functools

import jax
import jax.numpy as jnp
from jax import lax
from jax.experimental import pallas as pl
from jax.experimental.pallas import tpu as pltpu
from jax.sharding import PartitionSpec as P

HEAD = 120
PADDED = 128
BF16 = jnp.bfloat16
F32 = jnp.float32
VMEM = pl.BlockSpec(memory_space=pltpu.VMEM)
ANY = pl.BlockSpec(memory_space=pl.ANY)
HBM = pl.BlockSpec(memory_space=pltpu.HBM)
LIMIT = pltpu.CompilerParams(vmem_limit_bytes=12 * 1024 * 1024)
SMALL = pl.CostEstimate(flops=1000, bytes_accessed=1000, transcendentals=0)
def slow(work):
    return pl.CostEstimate(flops=int(work * 1e9), bytes_accessed=int(work * 2e6), transcendentals=0)


LARGE = slow(2)
GATES = (slow(2), slow(1), slow(0))
CUTS = (640, 640, 640)


def core_index():
    return lax.axis_index("dp") % 2


def line_bit():
    return lax.axis_index("dp") // 2 % 2


def swap(array, axis, mask):
    return lax.ppermute(array, axis, [(i, i ^ mask) for i in range(lax.axis_size(axis))])


def halves_kernel(x_ref, top_ref, bottom_ref):
    half = top_ref.shape[0]
    top_ref[...] = x_ref[:half]
    bottom_ref[...] = x_ref[half:]


def halves(block):
    rows, model = block.shape
    return pl.pallas_call(
        halves_kernel,
        out_shape=[jax.ShapeDtypeStruct((rows // 2, model), BF16)] * 2,
        in_specs=[VMEM],
        out_specs=[VMEM] * 2,
        compiler_params=LIMIT,
        cost_estimate=SMALL,
        name="halves",
    )(block)


def gate(arrays, after, cost=SMALL):
    return pl.pallas_call(
        lambda *refs: None,
        out_shape=[jax.ShapeDtypeStruct(a.shape, a.dtype) for a in arrays],
        in_specs=[VMEM] * len(arrays) + [ANY] * len(after),
        out_specs=[VMEM] * len(arrays),
        input_output_aliases={i: i for i in range(len(arrays))},
        compiler_params=LIMIT,
        cost_estimate=cost,
        name="gate",
    )(*arrays, *after)


def gather_blocks(block, axis, meanwhile):
    n = lax.axis_size(axis)
    if n != 4:
        return [[block]] + [[swap(block, axis, k)] for k in range(1, n)], meanwhile([block])
    top, bottom = halves(block)
    made = meanwhile([top, bottom])
    top_x, bottom_y = gate([swap(top, axis, 1), swap(bottom, axis, 2)], made)
    bottom_x, top_y = swap(bottom, axis, 1), swap(top, axis, 2)
    top_xy, bottom_xy = swap(top_x, axis, 2), swap(bottom_y, axis, 1)
    return [[top, bottom], [top_x, bottom_x], [top_y, bottom_y], [top_xy, bottom_xy]], made


def padded_head(rows, h):
    own = rows[h * HEAD : (h + 1) * HEAD]
    zeros = jnp.zeros((PADDED - HEAD, rows.shape[1]), F32)
    return jnp.concatenate([own, zeros], axis=0).astype(BF16)


def shares_kernel(cot_ref, *refs):
    outs, turned = refs[:-1], refs[-1]
    turned[...] = cot_ref[...].astype(F32).T
    width, me = outs[0].shape[0], lax.axis_index("seq")
    for k, out in enumerate(outs):
        start = pl.multiple_of((me ^ k) * width, 8)
        out[...] = turned[pl.ds(start, width), :].astype(BF16)


def cotangent_shares(cotangent, n):
    rows, model = cotangent.shape
    return pl.pallas_call(
        shares_kernel,
        out_shape=[jax.ShapeDtypeStruct((model // n, rows), BF16)] * n,
        in_specs=[VMEM],
        out_specs=[VMEM] * n,
        scratch_shapes=[pltpu.VMEM((model, rows), F32)],
        compiler_params=LIMIT,
        cost_estimate=SMALL,
        name="cotangent_shares",
    )(cotangent)


def project_into(w_ref, first, frames, out_ref):
    count, heads = out_ref.shape[:2]

    def one(t, carry):
        rows = lax.dot_general(
            w_ref[first + t], frames, (((1,), (1,)), ((), ())), preferred_element_type=F32
        )
        for h in range(heads):
            out_ref[t, h] = padded_head(rows, h)
        return carry

    lax.fori_loop(0, count, one, 0)


def project_kernel(w_ref, *refs):
    project_into(w_ref, 0, jnp.concatenate([r[...] for r in refs[:-1]], axis=0), refs[-1])


def project(weights, blocks):
    rows = sum(b.shape[0] for b in blocks)
    heads = weights.shape[1] // HEAD
    return pl.pallas_call(
        project_kernel,
        out_shape=jax.ShapeDtypeStruct((2, heads, PADDED, rows), BF16),
        in_specs=[VMEM] * (1 + len(blocks)),
        out_specs=VMEM,
        compiler_params=LIMIT,
        cost_estimate=SMALL,
        name="project",
    )(weights, *blocks)


def attention_kernel(parts, n, ids_ref, w_ref, *refs):
    pieces, last, out_ref = refs[:parts], refs[parts:-1], refs[-1]
    heads, total = out_ref.shape[:2]
    rows = total // n
    frames = jnp.concatenate([r[...] for r in last], axis=0)
    labels, me = [], lax.axis_index("seq")
    for k in range(n):
        start = pl.multiple_of((me ^ k) * rows, PADDED)
        labels.append(ids_ref[:, pl.ds(start, rows)].astype(F32))
    down = [jnp.broadcast_to(row, (PADDED, rows)).T for row in labels]
    column = jnp.concatenate(down, axis=0)
    step = max(PADDED, min(total, 512 * 512 // total))
    group = 2 if heads % 2 == 0 else 1
    for first in range(0, heads, group):
        own = [
            lax.dot_general(
                w_ref[t, first * HEAD : (first + group) * HEAD, :],
                frames,
                (((1,), (1,)), ((), ())),
                preferred_element_type=F32,
            )
            for t in range(2)
        ]
        for h in range(first, first + group):
            queries, keys = (
                jnp.concatenate([p[t, h] for p in pieces] + [padded_head(own[t], h - first)], axis=1)
                for t in range(2)
            )
            for at in range(0, total, step):
                scores = lax.dot_general(
                    keys, queries[:, at : at + step], (((0,), (0,)), ((), ())), preferred_element_type=F32
                )
                same = jnp.concatenate(
                    [column == labels[c // rows] for c in range(at, at + step, rows)], axis=1
                )
                scores = jnp.where(same, scores * HEAD**-0.5, -1e30)
                exponent = jnp.exp(scores - jnp.max(scores, axis=0, keepdims=True))
                inverse = 1.0 / jnp.sum(exponent, axis=0, keepdims=True)
                out_ref[h, :, at : at + step] = (exponent * inverse).astype(BF16)


def attention_weights(ids, weights, pieces, last, n):
    heads, total = weights.shape[1] // HEAD, ids.shape[1]
    return pl.pallas_call(
        functools.partial(attention_kernel, len(pieces), n),
        out_shape=jax.ShapeDtypeStruct((heads, total, total), BF16),
        in_specs=[VMEM] * (2 + len(pieces) + len(last)),
        out_specs=VMEM,
        compiler_params=LIMIT,
        cost_estimate=SMALL,
        name="attention_weights",
    )(ids, weights, *pieces, *last)


def rows_times(values_ref, mine, blocks, start, cut):
    half = values_ref.shape[0] // 2
    core = core_index()
    at = half * (core if mine else 1 - core)
    if half % 16 == 0:
        values = values_ref[pl.ds(pl.multiple_of(at, 16), half), :]
    else:
        values = values_ref[...].astype(F32)
        values = jnp.where(at == 0, values[:half], values[half:]).astype(BF16)
    frames = jnp.concatenate([b[:, start : start + cut] for b in blocks], axis=0)
    return jnp.dot(values, frames, preferred_element_type=F32).astype(BF16)


def first_gradient_kernel(n, cut, weights_ref, *refs):
    cots, blocks, (values_ref, theirs) = refs[:n], refs[n:-2], refs[-2:]
    upstream = jnp.concatenate([c[...] for c in cots], axis=1).astype(F32)
    rows = []
    for h in range(weights_ref.shape[0]):
        rows.append(
            lax.dot_general(
                padded_head(upstream, h), weights_ref[h], (((1,), (1,)), ((), ())), preferred_element_type=F32
            )[:HEAD]
        )
    values_ref[...] = jnp.concatenate(rows, axis=0).astype(BF16)
    theirs[...] = rows_times(values_ref, False, blocks, 0, cut)


def next_gradient_kernel(values_ref, *refs):
    outs, blocks = refs[1 - 2 * len(CUTS) :], refs[: 1 - 2 * len(CUTS)]
    start = 0
    for i, cut in enumerate(CUTS):
        for mine in (False, True) if i else (True,):
            outs[2 * i - 1 + mine][...] = rows_times(values_ref, mine, blocks, start, cut)
        start += cut


def gradient(weights, cots, blocks):
    width, total, model = cots[0].shape[0], weights.shape[1], blocks[0].shape[1]

    def shape(cut):
        return jax.ShapeDtypeStruct((width // 2, cut), BF16)

    values, first = pl.pallas_call(
        functools.partial(first_gradient_kernel, len(cots), CUTS[0]),
        out_shape=[jax.ShapeDtypeStruct((width, total), BF16), shape(CUTS[0])],
        in_specs=[VMEM] * (1 + len(cots) + len(blocks)),
        out_specs=[VMEM] * 2,
        compiler_params=LIMIT,
        cost_estimate=SMALL,
        name="first_gradient",
    )(weights, *cots, *blocks)
    outs = pl.pallas_call(
        next_gradient_kernel,
        out_shape=[shape(CUTS[0])] + [shape(cut) for cut in CUTS[1:] for _ in range(2)],
        in_specs=[VMEM] * (1 + len(blocks)),
        out_specs=[VMEM] * (2 * len(CUTS) - 1),
        compiler_params=LIMIT,
        cost_estimate=pl.CostEstimate(
            flops=4 * width * total * model, bytes_accessed=2 * total * model, transcendentals=0
        ),
        name="next_gradient",
    )(values, *blocks)
    outs = [first] + list(outs)
    return list(zip(outs[::2], outs[1::2]))


def context_kernel(n, weights_ref, w_ref, *refs):
    blocks, outs, values = refs[: -n - 1], refs[-n - 1 : -1], refs[-1]
    project_into(w_ref, 2, jnp.concatenate([r[...] for r in blocks], axis=0), values)
    rows = outs[0].shape[1]
    found = [
        jnp.dot(values[0, h], weights_ref[h], preferred_element_type=F32)[:HEAD]
        for h in range(weights_ref.shape[0])
    ]
    stacked = jnp.concatenate(found, axis=0)
    for k, out in enumerate(outs):
        out[...] = stacked[:, k * rows : (k + 1) * rows].astype(BF16)


def contexts_of(weights, projections, blocks, n):
    heads, total = weights.shape[:2]
    return pl.pallas_call(
        functools.partial(context_kernel, n),
        out_shape=[jax.ShapeDtypeStruct((heads * HEAD, total // n), BF16)] * n,
        in_specs=[VMEM] * (2 + len(blocks)),
        out_specs=[VMEM] * n,
        scratch_shapes=[pltpu.VMEM((1, heads, PADDED, total), BF16)],
        compiler_params=LIMIT,
        cost_estimate=SMALL,
        name="contexts",
    )(weights, projections, *blocks)


def assemble_kernel(*refs):
    n = len(refs) - 3
    out, token, turned = refs[n:]
    width, me = refs[0].shape[0], lax.axis_index("seq")
    for k in range(n):
        start = pl.multiple_of((me ^ k) * width, 8)
        turned[pl.ds(start, width), :] = refs[k][...].astype(F32)
    out[...] = turned[...].T.astype(BF16)
    token[...] = jnp.zeros_like(token)


def assemble_context(pieces):
    n, (width, rows) = len(pieces), pieces[0].shape
    return pl.pallas_call(
        assemble_kernel,
        out_shape=[jax.ShapeDtypeStruct((rows, n * width), BF16), jax.ShapeDtypeStruct((8, PADDED), F32)],
        in_specs=[VMEM] * n,
        out_specs=[VMEM] * 2,
        scratch_shapes=[pltpu.VMEM((n * width, rows), F32)],
        compiler_params=LIMIT,
        cost_estimate=LARGE,
        name="assemble_context",
    )(*pieces)


def final_kernel(start, scale, *refs):
    pieces, (out_ref, scratch, sem) = refs[:4], refs[-3:]
    rows, cut = pieces[0].shape
    place = 2 * core_index() + line_bit()
    for k, piece in enumerate(pieces):
        at = pl.multiple_of((place ^ k) * rows, 8)
        scratch[pl.ds(at, rows), :] = piece[...].astype(F32) * scale
    copy = pltpu.make_async_copy(scratch, out_ref.at[:, pl.ds(start, cut)], sem)
    copy.start()
    copy.wait()


def final(pieces, start, scale, model, out):
    rows, cut = pieces[0].shape
    earlier = [] if out is None else [out]
    return pl.pallas_call(
        functools.partial(final_kernel, start, scale),
        out_shape=jax.ShapeDtypeStruct((4 * rows, model), F32),
        in_specs=[VMEM] * 4 + [HBM] * len(earlier),
        out_specs=HBM,
        scratch_shapes=[pltpu.VMEM((4 * rows, cut), F32), pltpu.SemaphoreType.DMA],
        input_output_aliases={4: 0} if earlier else {},
        compiler_params=LIMIT,
        cost_estimate=SMALL,
        name="final",
    )(*pieces, *earlier)


def add_kernel(a_ref, b_ref, *refs):
    refs[-1][...] = (a_ref[...].astype(F32) + b_ref[...].astype(F32)).astype(BF16)


def add(a, b, *after):
    return pl.pallas_call(
        add_kernel,
        out_shape=jax.ShapeDtypeStruct(a.shape, BF16),
        in_specs=[VMEM, VMEM] + [ANY] * len(after),
        out_specs=VMEM,
        compiler_params=LIMIT,
        cost_estimate=SMALL,
        name="add",
    )(a, b, *after)


def split_sum_kernel(a_ref, b_ref, *refs):
    sent, kept = refs[-2:]
    total = a_ref[...].astype(F32) + b_ref[...].astype(F32)
    half = sent.shape[0]
    low = line_bit() == 0
    sent[...] = jnp.where(low, total[half:], total[:half]).astype(BF16)
    kept[...] = jnp.where(low, total[:half], total[half:]).astype(BF16)


def split_sum(a, b, *after):
    rows, columns = a.shape
    return pl.pallas_call(
        split_sum_kernel,
        out_shape=[jax.ShapeDtypeStruct((rows // 2, columns), BF16)] * 2,
        in_specs=[VMEM, VMEM] + [ANY] * len(after),
        out_specs=[VMEM] * 2,
        compiler_params=LIMIT,
        cost_estimate=SMALL,
        name="split_sum",
    )(a, b, *after)


def body(features, segment_ids, projections, cotangent):
    n, count = lax.axis_size("seq"), lax.axis_size("dp")
    model, width = features.shape[2], projections.shape[1]
    scale = 1.0 / count
    shares = cotangent_shares(cotangent[0], n)

    def meanwhile(own):
        return [project(projections, own), shares[0]]

    blocks, (own_piece, _) = gather_blocks(features[0], "seq", meanwhile)
    cots = [shares[0]] + [swap(shares[k], "seq", k) for k in range(1, n)]

    def flat(some):
        return [part for block in some for part in block]

    pieces = [own_piece]
    if n > 2:
        pieces.append(project(projections, flat(blocks[1 : n - 1])))
    weights = attention_weights(segment_ids, projections, pieces, flat(blocks[n - 1 :]), n)
    contexts = contexts_of(weights, projections, flat(blocks), n)
    received = [contexts[0]] + [swap(contexts[k], "seq", k) for k in range(1, n)]
    context, context_token = assemble_context(received)

    parts, split = [], []
    for i, (theirs, mine) in enumerate(gradient(weights, cots, flat(blocks))):
        after = [] if not split else split[0][:1] if i < 2 else parts[:1]
        split.append(split_sum(mine, swap(theirs, "dp", 1), *after))
        sent, own = split[-1]
        passed = swap(sent, "dp", 2)
        parts.append(add(own, passed, *(parts[-1:] or contexts[:1])))

    masks = [1 << b for b in range(2, count.bit_length() - 1)]
    aligned = width % 32 == 0
    value_grad, start, sums = None, 0, []
    for i, total in enumerate(parts):
        last = i == len(parts) - 1
        for mask in masks:
            got = swap(total, "dp", mask)
            wait = []
            if mask == masks[-1]:
                (got,) = gate([got], [], GATES[i])
                wait = [sums[-1][0]] if sums else parts[-1:]
                wait += [context_token] + sums[0][1:2] if last and sums else []
            total = add(total, got, *wait)
        got = swap(total, "dp", 2)
        four = [total, got, swap(total, "dp", 1), swap(got, "dp", 1)]
        sums.append(four)
        if aligned:
            value_grad = final(four, start, scale, model, value_grad)
        start += total.shape[1]
    if not aligned:
        chunks = []
        for kept, got, far_kept, far_got in sums:
            low = line_bit() == 0
            near = jnp.where(low, jnp.concatenate([kept, got]), jnp.concatenate([got, kept]))
            far = jnp.where(low, jnp.concatenate([far_kept, far_got]), jnp.concatenate([far_got, far_kept]))
            chunks.append(jnp.where(core_index() == 0, jnp.concatenate([near, far]), jnp.concatenate([far, near])))
        value_grad = jnp.concatenate(chunks, axis=1).astype(F32) * scale
    return context[None], value_grad


def solution(mesh):
    in_specs = (P("dp", "seq", None), P("dp", None), P(None, "seq", None), P("dp", "seq", None))
    out_specs = (P("dp", "seq", None), P("seq", None))
    return jax.shard_map(body, mesh=mesh, in_specs=in_specs, out_specs=out_specs, check_vma=False)
```

```python
import functools

import jax
import jax.numpy as jnp
from jax import lax
from jax.experimental import pallas as pl
from jax.experimental.pallas import tpu as pltpu
from jax.sharding import PartitionSpec as P

HEAD = 120
PADDED = 128
BF16 = jnp.bfloat16
F32 = jnp.float32
VMEM = pl.BlockSpec(memory_space=pltpu.VMEM)
ANY = pl.BlockSpec(memory_space=pl.ANY)
HBM = pl.BlockSpec(memory_space=pltpu.HBM)
LIMIT = pltpu.CompilerParams(vmem_limit_bytes=12 * 1024 * 1024)
SMALL = pl.CostEstimate(flops=1000, bytes_accessed=1000, transcendentals=0)
def slow(work):
    return pl.CostEstimate(flops=int(work * 1e9), bytes_accessed=int(work * 2e6), transcendentals=0)


LARGE = slow(2)
GATES = (slow(3), slow(1), slow(0))
CUTS = (640, 640, 640)


def core_index():
    return lax.axis_index("dp") % 2


def line_bit():
    return lax.axis_index("dp") // 2 % 2


def swap(array, axis, mask):
    return lax.ppermute(array, axis, [(i, i ^ mask) for i in range(lax.axis_size(axis))])


def halves_kernel(x_ref, top_ref, bottom_ref):
    half = top_ref.shape[0]
    top_ref[...] = x_ref[:half]
    bottom_ref[...] = x_ref[half:]


def halves(block):
    rows, model = block.shape
    return pl.pallas_call(
        halves_kernel,
        out_shape=[jax.ShapeDtypeStruct((rows // 2, model), BF16)] * 2,
        in_specs=[VMEM],
        out_specs=[VMEM] * 2,
        compiler_params=LIMIT,
        cost_estimate=SMALL,
        name="halves",
    )(block)


def gate(arrays, after, cost=SMALL):
    return pl.pallas_call(
        lambda *refs: None,
        out_shape=[jax.ShapeDtypeStruct(a.shape, a.dtype) for a in arrays],
        in_specs=[VMEM] * len(arrays) + [ANY] * len(after),
        out_specs=[VMEM] * len(arrays),
        input_output_aliases={i: i for i in range(len(arrays))},
        compiler_params=LIMIT,
        cost_estimate=cost,
        name="gate",
    )(*arrays, *after)


def gather_blocks(block, axis, meanwhile):
    n = lax.axis_size(axis)
    if n != 4:
        return [[block]] + [[swap(block, axis, k)] for k in range(1, n)], meanwhile([block])
    top, bottom = halves(block)
    made = meanwhile([top, bottom])
    top_x, bottom_y = gate([swap(top, axis, 1), swap(bottom, axis, 2)], made)
    bottom_x, top_y = swap(bottom, axis, 1), swap(top, axis, 2)
    top_xy, bottom_xy = swap(top_x, axis, 2), swap(bottom_y, axis, 1)
    return [[top, bottom], [top_x, bottom_x], [top_y, bottom_y], [top_xy, bottom_xy]], made


def padded_head(rows, h):
    own = rows[h * HEAD : (h + 1) * HEAD]
    zeros = jnp.zeros((PADDED - HEAD, rows.shape[1]), F32)
    return jnp.concatenate([own, zeros], axis=0).astype(BF16)


def shares_kernel(cot_ref, *refs):
    outs, turned = refs[:-1], refs[-1]
    turned[...] = cot_ref[...].astype(F32).T
    width, me = outs[0].shape[0], lax.axis_index("seq")
    for k, out in enumerate(outs):
        start = pl.multiple_of((me ^ k) * width, 8)
        out[...] = turned[pl.ds(start, width), :].astype(BF16)


def cotangent_shares(cotangent, n):
    rows, model = cotangent.shape
    return pl.pallas_call(
        shares_kernel,
        out_shape=[jax.ShapeDtypeStruct((model // n, rows), BF16)] * n,
        in_specs=[VMEM],
        out_specs=[VMEM] * n,
        scratch_shapes=[pltpu.VMEM((model, rows), F32)],
        compiler_params=LIMIT,
        cost_estimate=SMALL,
        name="cotangent_shares",
    )(cotangent)


def project_into(w_ref, first, frames, out_ref):
    count, heads = out_ref.shape[:2]

    def one(t, carry):
        rows = lax.dot_general(
            w_ref[first + t], frames, (((1,), (1,)), ((), ())), preferred_element_type=F32
        )
        for h in range(heads):
            out_ref[t, h] = padded_head(rows, h)
        return carry

    lax.fori_loop(0, count, one, 0)


def project_kernel(w_ref, *refs):
    project_into(w_ref, 0, jnp.concatenate([r[...] for r in refs[:-1]], axis=0), refs[-1])


def project(weights, blocks):
    rows = sum(b.shape[0] for b in blocks)
    heads = weights.shape[1] // HEAD
    return pl.pallas_call(
        project_kernel,
        out_shape=jax.ShapeDtypeStruct((2, heads, PADDED, rows), BF16),
        in_specs=[VMEM] * (1 + len(blocks)),
        out_specs=VMEM,
        compiler_params=LIMIT,
        cost_estimate=SMALL,
        name="project",
    )(weights, *blocks)


def attention_kernel(parts, n, ids_ref, w_ref, *refs):
    pieces, last, out_ref = refs[:parts], refs[parts:-1], refs[-1]
    heads, total = out_ref.shape[:2]
    rows = total // n
    frames = jnp.concatenate([r[...] for r in last], axis=0)
    labels, me = [], lax.axis_index("seq")
    for k in range(n):
        start = pl.multiple_of((me ^ k) * rows, PADDED)
        labels.append(ids_ref[:, pl.ds(start, rows)].astype(F32))
    down = [jnp.broadcast_to(row, (PADDED, rows)).T for row in labels]
    column = jnp.concatenate(down, axis=0)
    step = max(PADDED, min(total, 512 * 512 // total))
    group = 2 if heads % 2 == 0 else 1
    for first in range(0, heads, group):
        own = [
            lax.dot_general(
                w_ref[t, first * HEAD : (first + group) * HEAD, :],
                frames,
                (((1,), (1,)), ((), ())),
                preferred_element_type=F32,
            )
            for t in range(2)
        ]
        for h in range(first, first + group):
            queries, keys = (
                jnp.concatenate([p[t, h] for p in pieces] + [padded_head(own[t], h - first)], axis=1)
                for t in range(2)
            )
            for at in range(0, total, step):
                scores = lax.dot_general(
                    keys, queries[:, at : at + step], (((0,), (0,)), ((), ())), preferred_element_type=F32
                )
                same = jnp.concatenate(
                    [column == labels[c // rows] for c in range(at, at + step, rows)], axis=1
                )
                scores = jnp.where(same, scores * HEAD**-0.5, -1e30)
                exponent = jnp.exp(scores - jnp.max(scores, axis=0, keepdims=True))
                inverse = 1.0 / jnp.sum(exponent, axis=0, keepdims=True)
                out_ref[h, :, at : at + step] = (exponent * inverse).astype(BF16)


def attention_weights(ids, weights, pieces, last, n):
    heads, total = weights.shape[1] // HEAD, ids.shape[1]
    return pl.pallas_call(
        functools.partial(attention_kernel, len(pieces), n),
        out_shape=jax.ShapeDtypeStruct((heads, total, total), BF16),
        in_specs=[VMEM] * (2 + len(pieces) + len(last)),
        out_specs=VMEM,
        compiler_params=LIMIT,
        cost_estimate=SMALL,
        name="attention_weights",
    )(ids, weights, *pieces, *last)


def rows_times(values_ref, mine, blocks, start, cut):
    half = values_ref.shape[0] // 2
    core = core_index()
    at = half * (core if mine else 1 - core)
    if half % 16 == 0:
        values = values_ref[pl.ds(pl.multiple_of(at, 16), half), :]
    else:
        values = values_ref[...].astype(F32)
        values = jnp.where(at == 0, values[:half], values[half:]).astype(BF16)
    frames = jnp.concatenate([b[:, start : start + cut] for b in blocks], axis=0)
    return jnp.dot(values, frames, preferred_element_type=F32).astype(BF16)


def first_gradient_kernel(n, cut, weights_ref, *refs):
    cots, blocks, (values_ref, theirs) = refs[:n], refs[n:-2], refs[-2:]
    upstream = jnp.concatenate([c[...] for c in cots], axis=1).astype(F32)
    rows = []
    for h in range(weights_ref.shape[0]):
        rows.append(
            lax.dot_general(
                padded_head(upstream, h), weights_ref[h], (((1,), (1,)), ((), ())), preferred_element_type=F32
            )[:HEAD]
        )
    values_ref[...] = jnp.concatenate(rows, axis=0).astype(BF16)
    theirs[...] = rows_times(values_ref, False, blocks, 0, cut)


def next_gradient_kernel(values_ref, *refs):
    outs, blocks = refs[1 - 2 * len(CUTS) :], refs[: 1 - 2 * len(CUTS)]
    start = 0
    for i, cut in enumerate(CUTS):
        for mine in (False, True) if i else (True,):
            outs[2 * i - 1 + mine][...] = rows_times(values_ref, mine, blocks, start, cut)
        start += cut


def gradient(weights, cots, blocks):
    width, total, model = cots[0].shape[0], weights.shape[1], blocks[0].shape[1]

    def shape(cut):
        return jax.ShapeDtypeStruct((width // 2, cut), BF16)

    values, first = pl.pallas_call(
        functools.partial(first_gradient_kernel, len(cots), CUTS[0]),
        out_shape=[jax.ShapeDtypeStruct((width, total), BF16), shape(CUTS[0])],
        in_specs=[VMEM] * (1 + len(cots) + len(blocks)),
        out_specs=[VMEM] * 2,
        compiler_params=LIMIT,
        cost_estimate=SMALL,
        name="first_gradient",
    )(weights, *cots, *blocks)
    outs = pl.pallas_call(
        next_gradient_kernel,
        out_shape=[shape(CUTS[0])] + [shape(cut) for cut in CUTS[1:] for _ in range(2)],
        in_specs=[VMEM] * (1 + len(blocks)),
        out_specs=[VMEM] * (2 * len(CUTS) - 1),
        compiler_params=LIMIT,
        cost_estimate=pl.CostEstimate(
            flops=4 * width * total * model, bytes_accessed=2 * total * model, transcendentals=0
        ),
        name="next_gradient",
    )(values, *blocks)
    outs = [first] + list(outs)
    return list(zip(outs[::2], outs[1::2]))


def context_kernel(n, weights_ref, w_ref, *refs):
    blocks, outs, values = refs[: -n - 1], refs[-n - 1 : -1], refs[-1]
    project_into(w_ref, 2, jnp.concatenate([r[...] for r in blocks], axis=0), values)
    rows = outs[0].shape[1]
    found = [
        jnp.dot(values[0, h], weights_ref[h], preferred_element_type=F32)[:HEAD]
        for h in range(weights_ref.shape[0])
    ]
    stacked = jnp.concatenate(found, axis=0)
    for k, out in enumerate(outs):
        out[...] = stacked[:, k * rows : (k + 1) * rows].astype(BF16)


def contexts_of(weights, projections, blocks, n):
    heads, total = weights.shape[:2]
    return pl.pallas_call(
        functools.partial(context_kernel, n),
        out_shape=[jax.ShapeDtypeStruct((heads * HEAD, total // n), BF16)] * n,
        in_specs=[VMEM] * (2 + len(blocks)),
        out_specs=[VMEM] * n,
        scratch_shapes=[pltpu.VMEM((1, heads, PADDED, total), BF16)],
        compiler_params=LIMIT,
        cost_estimate=SMALL,
        name="contexts",
    )(weights, projections, *blocks)


def assemble_kernel(*refs):
    n = len(refs) - 3
    out, token, turned = refs[n:]
    width, me = refs[0].shape[0], lax.axis_index("seq")
    for k in range(n):
        start = pl.multiple_of((me ^ k) * width, 8)
        turned[pl.ds(start, width), :] = refs[k][...].astype(F32)
    out[...] = turned[...].T.astype(BF16)
    token[...] = jnp.zeros_like(token)


def assemble_context(pieces):
    n, (width, rows) = len(pieces), pieces[0].shape
    return pl.pallas_call(
        assemble_kernel,
        out_shape=[jax.ShapeDtypeStruct((rows, n * width), BF16), jax.ShapeDtypeStruct((8, PADDED), F32)],
        in_specs=[VMEM] * n,
        out_specs=[VMEM] * 2,
        scratch_shapes=[pltpu.VMEM((n * width, rows), F32)],
        compiler_params=LIMIT,
        cost_estimate=LARGE,
        name="assemble_context",
    )(*pieces)


def final_kernel(start, scale, *refs):
    pieces, (out_ref, token, scratch, sem) = refs[:4], refs[-4:]
    rows, cut = pieces[0].shape
    place = 2 * core_index() + line_bit()
    for k, piece in enumerate(pieces):
        at = pl.multiple_of((place ^ k) * rows, 8)
        scratch[pl.ds(at, rows), :] = piece[...].astype(F32) * scale
    copy = pltpu.make_async_copy(scratch, out_ref.at[:, pl.ds(start, cut)], sem)
    copy.start()
    token[...] = jnp.zeros_like(token)
    copy.wait()


def final(pieces, start, scale, model, out):
    rows, cut = pieces[0].shape
    earlier = [] if out is None else [out]
    return pl.pallas_call(
        functools.partial(final_kernel, start, scale),
        out_shape=[jax.ShapeDtypeStruct((4 * rows, model), F32), jax.ShapeDtypeStruct((8, PADDED), F32)],
        in_specs=[VMEM] * 4 + [HBM] * len(earlier),
        out_specs=[HBM, VMEM],
        scratch_shapes=[pltpu.VMEM((4 * rows, cut), F32), pltpu.SemaphoreType.DMA],
        input_output_aliases={4: 0} if earlier else {},
        compiler_params=LIMIT,
        cost_estimate=SMALL,
        name="final",
    )(*pieces, *earlier)


def add_kernel(a_ref, b_ref, *refs):
    refs[-1][...] = (a_ref[...].astype(F32) + b_ref[...].astype(F32)).astype(BF16)


def add(a, b, *after):
    return pl.pallas_call(
        add_kernel,
        out_shape=jax.ShapeDtypeStruct(a.shape, BF16),
        in_specs=[VMEM, VMEM] + [ANY] * len(after),
        out_specs=VMEM,
        compiler_params=LIMIT,
        cost_estimate=SMALL,
        name="add",
    )(a, b, *after)


def split_sum_kernel(a_ref, b_ref, *refs):
    sent, kept = refs[-2:]
    total = a_ref[...].astype(F32) + b_ref[...].astype(F32)
    half = sent.shape[0]
    low = line_bit() == 0
    sent[...] = jnp.where(low, total[half:], total[:half]).astype(BF16)
    kept[...] = jnp.where(low, total[:half], total[half:]).astype(BF16)


def split_sum(a, b, *after):
    rows, columns = a.shape
    return pl.pallas_call(
        split_sum_kernel,
        out_shape=[jax.ShapeDtypeStruct((rows // 2, columns), BF16)] * 2,
        in_specs=[VMEM, VMEM] + [ANY] * len(after),
        out_specs=[VMEM] * 2,
        compiler_params=LIMIT,
        cost_estimate=SMALL,
        name="split_sum",
    )(a, b, *after)


def body(features, segment_ids, projections, cotangent):
    n, count = lax.axis_size("seq"), lax.axis_size("dp")
    model, width = features.shape[2], projections.shape[1]
    scale = 1.0 / count
    shares = cotangent_shares(cotangent[0], n)

    def meanwhile(own):
        return [project(projections, own), shares[0]]

    blocks, (own_piece, _) = gather_blocks(features[0], "seq", meanwhile)
    sent = gate(shares[1:], blocks[1][1:] + blocks[2][:1]) if n == 4 else shares[1:]
    cots = [shares[0]] + [swap(share, "seq", k + 1) for k, share in enumerate(sent)]

    def flat(some):
        return [part for block in some for part in block]

    pieces = [own_piece]
    if n > 2:
        pieces.append(project(projections, flat(blocks[1 : n - 1])))
    weights = attention_weights(segment_ids, projections, pieces, flat(blocks[n - 1 :]), n)
    contexts = contexts_of(weights, projections, flat(blocks), n)
    received = [contexts[0]] + [swap(contexts[k], "seq", k) for k in range(1, n)]
    context, context_token = assemble_context(received)

    parts, split = [], []
    for i, (theirs, mine) in enumerate(gradient(weights, cots, flat(blocks))):
        after = [] if not split else split[0][:1] if i < 2 else parts[:1]
        split.append(split_sum(mine, swap(theirs, "dp", 1), *after))
        sent, own = split[-1]
        passed = swap(sent, "dp", 2)
        parts.append(add(own, passed, *(parts[-1:] or contexts[:1])))

    masks = [1 << b for b in range(2, count.bit_length() - 1)]
    aligned = width % 32 == 0
    value_grad, start, sums, tokens = None, 0, [], []
    for i, total in enumerate(parts):
        last = i == len(parts) - 1
        for mask in masks:
            got = swap(total, "dp", mask)
            wait = []
            if mask == masks[-1]:
                (got,) = gate([got], [], GATES[i])
                wait = [sums[-1][0]] if sums else parts[-1:]
                wait += [context_token] + sums[0][1:2] if last and sums else []
            total = add(total, got, *wait)
        got = swap(total, "dp", 2)
        if last and tokens:
            (got,) = gate([got], tokens[:1])
        four = [total, got, swap(total, "dp", 1), swap(got, "dp", 1)]
        sums.append(four)
        if aligned:
            value_grad, token = final(four, start, scale, model, value_grad)
            tokens.append(token)
        start += total.shape[1]
    if not aligned:
        chunks = []
        for kept, got, far_kept, far_got in sums:
            low = line_bit() == 0
            near = jnp.where(low, jnp.concatenate([kept, got]), jnp.concatenate([got, kept]))
            far = jnp.where(low, jnp.concatenate([far_kept, far_got]), jnp.concatenate([far_got, far_kept]))
            chunks.append(jnp.where(core_index() == 0, jnp.concatenate([near, far]), jnp.concatenate([far, near])))
        value_grad = jnp.concatenate(chunks, axis=1).astype(F32) * scale
    return context[None], value_grad


def solution(mesh):
    in_specs = (P("dp", "seq", None), P("dp", None), P(None, "seq", None), P("dp", "seq", None))
    out_specs = (P("dp", "seq", None), P("seq", None))
    return jax.shard_map(body, mesh=mesh, in_specs=in_specs, out_specs=out_specs, check_vma=False)
```

```python
import functools

import jax
import jax.numpy as jnp
from jax import lax
from jax.experimental import pallas as pl
from jax.experimental.pallas import tpu as pltpu
from jax.sharding import PartitionSpec as P

HEAD = 120
PADDED = 128
BF16 = jnp.bfloat16
F32 = jnp.float32
VMEM = pl.BlockSpec(memory_space=pltpu.VMEM)
ANY = pl.BlockSpec(memory_space=pl.ANY)
HBM = pl.BlockSpec(memory_space=pltpu.HBM)
LIMIT = pltpu.CompilerParams(vmem_limit_bytes=12 * 1024 * 1024)
SMALL = pl.CostEstimate(flops=1000, bytes_accessed=1000, transcendentals=0)
def slow(work):
    return pl.CostEstimate(flops=int(work * 1e9), bytes_accessed=int(work * 2e6), transcendentals=0)


LARGE = slow(2)
GATES = (slow(3), slow(1), slow(0))
CUTS = (640, 640, 640)


def core_index():
    return lax.axis_index("dp") % 2


def line_bit():
    return lax.axis_index("dp") // 2 % 2


def swap(array, axis, mask):
    return lax.ppermute(array, axis, [(i, i ^ mask) for i in range(lax.axis_size(axis))])


def halves_kernel(x_ref, top_ref, bottom_ref):
    half = top_ref.shape[0]
    top_ref[...] = x_ref[:half]
    bottom_ref[...] = x_ref[half:]


def halves(block):
    rows, model = block.shape
    return pl.pallas_call(
        halves_kernel,
        out_shape=[jax.ShapeDtypeStruct((rows // 2, model), BF16)] * 2,
        in_specs=[VMEM],
        out_specs=[VMEM] * 2,
        compiler_params=LIMIT,
        cost_estimate=SMALL,
        name="halves",
    )(block)


def gate(arrays, after, cost=SMALL):
    return pl.pallas_call(
        lambda *refs: None,
        out_shape=[jax.ShapeDtypeStruct(a.shape, a.dtype) for a in arrays],
        in_specs=[VMEM] * len(arrays) + [ANY] * len(after),
        out_specs=[VMEM] * len(arrays),
        input_output_aliases={i: i for i in range(len(arrays))},
        compiler_params=LIMIT,
        cost_estimate=cost,
        name="gate",
    )(*arrays, *after)


def gather_blocks(block, axis, meanwhile):
    n = lax.axis_size(axis)
    if n != 4:
        return [[block]] + [[swap(block, axis, k)] for k in range(1, n)], meanwhile([block])
    top, bottom = halves(block)
    made = meanwhile([top, bottom])
    top_x, bottom_y = gate([swap(top, axis, 1), swap(bottom, axis, 2)], made)
    bottom_x, top_y = swap(bottom, axis, 1), swap(top, axis, 2)
    top_xy, bottom_xy = swap(top_x, axis, 2), swap(bottom_y, axis, 1)
    return [[top, bottom], [top_x, bottom_x], [top_y, bottom_y], [top_xy, bottom_xy]], made


def padded_head(rows, h):
    own = rows[h * HEAD : (h + 1) * HEAD]
    zeros = jnp.zeros((PADDED - HEAD, rows.shape[1]), F32)
    return jnp.concatenate([own, zeros], axis=0).astype(BF16)


def shares_kernel(cot_ref, *refs):
    outs, turned = refs[:-1], refs[-1]
    turned[...] = cot_ref[...].astype(F32).T
    width, me = outs[0].shape[0], lax.axis_index("seq")
    for k, out in enumerate(outs):
        start = pl.multiple_of((me ^ k) * width, 8)
        out[...] = turned[pl.ds(start, width), :].astype(BF16)


def cotangent_shares(cotangent, n):
    rows, model = cotangent.shape
    return pl.pallas_call(
        shares_kernel,
        out_shape=[jax.ShapeDtypeStruct((model // n, rows), BF16)] * n,
        in_specs=[VMEM],
        out_specs=[VMEM] * n,
        scratch_shapes=[pltpu.VMEM((model, rows), F32)],
        compiler_params=LIMIT,
        cost_estimate=SMALL,
        name="cotangent_shares",
    )(cotangent)


def project_into(w_ref, first, frames, out_ref):
    count, heads = out_ref.shape[:2]

    def one(t, carry):
        rows = lax.dot_general(
            w_ref[first + t], frames, (((1,), (1,)), ((), ())), preferred_element_type=F32
        )
        for h in range(heads):
            out_ref[t, h] = padded_head(rows, h)
        return carry

    lax.fori_loop(0, count, one, 0)


def project_kernel(w_ref, *refs):
    project_into(w_ref, 0, jnp.concatenate([r[...] for r in refs[:-1]], axis=0), refs[-1])


def project(weights, blocks):
    rows = sum(b.shape[0] for b in blocks)
    heads = weights.shape[1] // HEAD
    return pl.pallas_call(
        project_kernel,
        out_shape=jax.ShapeDtypeStruct((2, heads, PADDED, rows), BF16),
        in_specs=[VMEM] * (1 + len(blocks)),
        out_specs=VMEM,
        compiler_params=LIMIT,
        cost_estimate=SMALL,
        name="project",
    )(weights, *blocks)


def attention_kernel(parts, n, ids_ref, w_ref, *refs):
    pieces, last, (out_ref, queries, keys) = refs[:parts], refs[parts:-3], refs[-3:]
    heads, total = out_ref.shape[:2]
    rows = total // n
    reach = total // 4 // rows
    frames = jnp.concatenate([r[...] for r in last], axis=0)
    me = lax.axis_index("seq")
    spot = [pl.ds(pl.multiple_of((me ^ k) * rows, PADDED), rows) for k in range(n)]
    k = 0
    for piece in pieces:
        for at in range(0, piece.shape[3], rows):
            for h in range(heads):
                queries[h, :, spot[k]] = piece[0, h, :, at : at + rows]
                keys[h, :, spot[k]] = piece[1, h, :, at : at + rows]
            k += 1
    labels = [ids_ref[:, b * rows : (b + 1) * rows].astype(F32) for b in range(n)]
    down = [jnp.broadcast_to(row, (PADDED, rows)).T for row in labels]
    group = 2 if heads % 2 == 0 else 1
    for first in range(0, heads, group):
        for t, ref in enumerate((queries, keys)):
            own = lax.dot_general(
                w_ref[t, first * HEAD : (first + group) * HEAD, :],
                frames,
                (((1,), (1,)), ((), ())),
                preferred_element_type=F32,
            )
            for h in range(group):
                ref[first + h, :, spot[n - 1]] = padded_head(own, h)
        for h in range(first, first + group):
            for b in range(n):
                low, high = max(0, b - reach), min(n, b + reach + 1)
                scores = lax.dot_general(
                    keys[h, :, low * rows : high * rows],
                    queries[h, :, b * rows : (b + 1) * rows],
                    (((0,), (0,)), ((), ())),
                    preferred_element_type=F32,
                )
                same = jnp.concatenate(down[low:high], axis=0) == labels[b]
                scores = jnp.where(same, scores * HEAD**-0.5, -1e30)
                exponent = jnp.exp(scores - jnp.max(scores, axis=0, keepdims=True))
                inverse = 1.0 / jnp.sum(exponent, axis=0, keepdims=True)
                weights = (exponent * inverse).astype(BF16)
                for c in range(n):
                    if low <= c < high:
                        value = weights[(c - low) * rows : (c - low + 1) * rows]
                    else:
                        value = jnp.zeros((rows, rows), BF16)
                    out_ref[h, spot[c], spot[b]] = value


def attention_weights(ids, weights, pieces, last, n):
    heads, total = weights.shape[1] // HEAD, ids.shape[1]
    return pl.pallas_call(
        functools.partial(attention_kernel, len(pieces), n),
        out_shape=jax.ShapeDtypeStruct((heads, total, total), BF16),
        in_specs=[VMEM] * (2 + len(pieces) + len(last)),
        out_specs=VMEM,
        scratch_shapes=[pltpu.VMEM((heads, PADDED, total), BF16)] * 2,
        compiler_params=LIMIT,
        cost_estimate=SMALL,
        name="attention_weights",
    )(ids, weights, *pieces, *last)


def rows_times(values_ref, mine, blocks, start, cut):
    half = values_ref.shape[0] // 2
    core = core_index()
    at = half * (core if mine else 1 - core)
    if half % 16 == 0:
        values = values_ref[pl.ds(pl.multiple_of(at, 16), half), :]
    else:
        values = values_ref[...].astype(F32)
        values = jnp.where(at == 0, values[:half], values[half:]).astype(BF16)
    frames = jnp.concatenate([b[:, start : start + cut] for b in blocks], axis=0)
    return jnp.dot(values, frames, preferred_element_type=F32).astype(BF16)


def first_gradient_kernel(n, cut, weights_ref, *refs):
    cots, blocks, (values_ref, theirs) = refs[:n], refs[n:-2], refs[-2:]
    upstream = jnp.concatenate([c[...] for c in cots], axis=1).astype(F32)
    rows = []
    for h in range(weights_ref.shape[0]):
        rows.append(
            lax.dot_general(
                padded_head(upstream, h), weights_ref[h], (((1,), (1,)), ((), ())), preferred_element_type=F32
            )[:HEAD]
        )
    values_ref[...] = jnp.concatenate(rows, axis=0).astype(BF16)
    theirs[...] = rows_times(values_ref, False, blocks, 0, cut)


def next_gradient_kernel(values_ref, *refs):
    outs, blocks = refs[1 - 2 * len(CUTS) :], refs[: 1 - 2 * len(CUTS)]
    start = 0
    for i, cut in enumerate(CUTS):
        for mine in (False, True) if i else (True,):
            outs[2 * i - 1 + mine][...] = rows_times(values_ref, mine, blocks, start, cut)
        start += cut


def gradient(weights, cots, blocks):
    width, total, model = cots[0].shape[0], weights.shape[1], blocks[0].shape[1]

    def shape(cut):
        return jax.ShapeDtypeStruct((width // 2, cut), BF16)

    values, first = pl.pallas_call(
        functools.partial(first_gradient_kernel, len(cots), CUTS[0]),
        out_shape=[jax.ShapeDtypeStruct((width, total), BF16), shape(CUTS[0])],
        in_specs=[VMEM] * (1 + len(cots) + len(blocks)),
        out_specs=[VMEM] * 2,
        compiler_params=LIMIT,
        cost_estimate=SMALL,
        name="first_gradient",
    )(weights, *cots, *blocks)
    outs = pl.pallas_call(
        next_gradient_kernel,
        out_shape=[shape(CUTS[0])] + [shape(cut) for cut in CUTS[1:] for _ in range(2)],
        in_specs=[VMEM] * (1 + len(blocks)),
        out_specs=[VMEM] * (2 * len(CUTS) - 1),
        compiler_params=LIMIT,
        cost_estimate=pl.CostEstimate(
            flops=4 * width * total * model, bytes_accessed=2 * total * model, transcendentals=0
        ),
        name="next_gradient",
    )(values, *blocks)
    outs = [first] + list(outs)
    return list(zip(outs[::2], outs[1::2]))


def context_kernel(n, weights_ref, w_ref, *refs):
    blocks, outs, values = refs[: -n - 1], refs[-n - 1 : -1], refs[-1]
    project_into(w_ref, 2, jnp.concatenate([r[...] for r in blocks], axis=0), values)
    rows = outs[0].shape[1]
    found = [
        jnp.dot(values[0, h], weights_ref[h], preferred_element_type=F32)[:HEAD]
        for h in range(weights_ref.shape[0])
    ]
    stacked = jnp.concatenate(found, axis=0)
    for k, out in enumerate(outs):
        out[...] = stacked[:, k * rows : (k + 1) * rows].astype(BF16)


def contexts_of(weights, projections, blocks, n):
    heads, total = weights.shape[:2]
    return pl.pallas_call(
        functools.partial(context_kernel, n),
        out_shape=[jax.ShapeDtypeStruct((heads * HEAD, total // n), BF16)] * n,
        in_specs=[VMEM] * (2 + len(blocks)),
        out_specs=[VMEM] * n,
        scratch_shapes=[pltpu.VMEM((1, heads, PADDED, total), BF16)],
        compiler_params=LIMIT,
        cost_estimate=SMALL,
        name="contexts",
    )(weights, projections, *blocks)


def assemble_kernel(*refs):
    n = len(refs) - 3
    out, token, turned = refs[n:]
    width, me = refs[0].shape[0], lax.axis_index("seq")
    for k in range(n):
        start = pl.multiple_of((me ^ k) * width, 8)
        turned[pl.ds(start, width), :] = refs[k][...].astype(F32)
    out[...] = turned[...].T.astype(BF16)
    token[...] = jnp.zeros_like(token)


def assemble_context(pieces):
    n, (width, rows) = len(pieces), pieces[0].shape
    return pl.pallas_call(
        assemble_kernel,
        out_shape=[jax.ShapeDtypeStruct((rows, n * width), BF16), jax.ShapeDtypeStruct((8, PADDED), F32)],
        in_specs=[VMEM] * n,
        out_specs=[VMEM] * 2,
        scratch_shapes=[pltpu.VMEM((n * width, rows), F32)],
        compiler_params=LIMIT,
        cost_estimate=LARGE,
        name="assemble_context",
    )(*pieces)


def final_kernel(start, scale, marked, *refs):
    pieces, (scratch, sem) = refs[:4], refs[-2:]
    out_ref = refs[-4] if marked else refs[-3]
    rows, cut = pieces[0].shape
    place = 2 * core_index() + line_bit()
    for k, piece in enumerate(pieces):
        at = pl.multiple_of((place ^ k) * rows, 8)
        scratch[pl.ds(at, rows), :] = piece[...].astype(F32) * scale
    copy = pltpu.make_async_copy(scratch, out_ref.at[:, pl.ds(start, cut)], sem)
    copy.start()
    if marked:
        refs[-3][...] = jnp.zeros_like(refs[-3])
    copy.wait()


def final(pieces, start, scale, model, out, marked):
    rows, cut = pieces[0].shape
    earlier = [] if out is None else [out]
    return pl.pallas_call(
        functools.partial(final_kernel, start, scale, marked),
        out_shape=[jax.ShapeDtypeStruct((4 * rows, model), F32)] + [jax.ShapeDtypeStruct((8, PADDED), F32)] * marked,
        in_specs=[VMEM] * 4 + [HBM] * len(earlier),
        out_specs=[HBM] + [VMEM] * marked,
        scratch_shapes=[pltpu.VMEM((4 * rows, cut), F32), pltpu.SemaphoreType.DMA],
        input_output_aliases={4: 0} if earlier else {},
        compiler_params=LIMIT,
        cost_estimate=SMALL,
        name="final",
    )(*pieces, *earlier)


def add_kernel(a_ref, b_ref, *refs):
    refs[-1][...] = (a_ref[...].astype(F32) + b_ref[...].astype(F32)).astype(BF16)


def add(a, b, *after):
    return pl.pallas_call(
        add_kernel,
        out_shape=jax.ShapeDtypeStruct(a.shape, BF16),
        in_specs=[VMEM, VMEM] + [ANY] * len(after),
        out_specs=VMEM,
        compiler_params=LIMIT,
        cost_estimate=SMALL,
        name="add",
    )(a, b, *after)


def split_sum_kernel(a_ref, b_ref, *refs):
    sent, kept = refs[-2:]
    total = a_ref[...].astype(F32) + b_ref[...].astype(F32)
    half = sent.shape[0]
    low = line_bit() == 0
    sent[...] = jnp.where(low, total[half:], total[:half]).astype(BF16)
    kept[...] = jnp.where(low, total[:half], total[half:]).astype(BF16)


def split_sum(a, b, *after):
    rows, columns = a.shape
    return pl.pallas_call(
        split_sum_kernel,
        out_shape=[jax.ShapeDtypeStruct((rows // 2, columns), BF16)] * 2,
        in_specs=[VMEM, VMEM] + [ANY] * len(after),
        out_specs=[VMEM] * 2,
        compiler_params=LIMIT,
        cost_estimate=SMALL,
        name="split_sum",
    )(a, b, *after)


def body(features, segment_ids, projections, cotangent):
    n, count = lax.axis_size("seq"), lax.axis_size("dp")
    model, width = features.shape[2], projections.shape[1]
    scale = 1.0 / count
    shares = cotangent_shares(cotangent[0], n)

    def meanwhile(own):
        return [project(projections, own), shares[0]]

    blocks, (own_piece, _) = gather_blocks(features[0], "seq", meanwhile)

    def flat(some):
        return [part for block in some for part in block]

    pieces = [own_piece]
    if n > 2:
        pieces.append(project(projections, flat(blocks[1 : n - 1])))
    sent = gate(shares[1:], pieces[1:])
    cots = [shares[0]] + [swap(share, "seq", k + 1) for k, share in enumerate(sent)]
    weights = attention_weights(segment_ids, projections, pieces, flat(blocks[n - 1 :]), n)
    contexts = contexts_of(weights, projections, flat(blocks), n)
    received = [contexts[0]] + [swap(contexts[k], "seq", k) for k in range(1, n)]
    context, context_token = assemble_context(received)

    parts, split = [], []
    for i, (theirs, mine) in enumerate(gradient(weights, cots, flat(blocks))):
        after = [] if not split else split[0][:1] if i < 2 else parts[:1]
        split.append(split_sum(mine, swap(theirs, "dp", 1), *after))
        sent, own = split[-1]
        passed = swap(sent, "dp", 2)
        parts.append(add(own, passed, *(parts[-1:] or contexts[:1])))

    masks = [1 << b for b in range(2, count.bit_length() - 1)]
    aligned = width % 32 == 0
    value_grad, start, sums, tokens = None, 0, [], []
    for i, total in enumerate(parts):
        last = i == len(parts) - 1
        for mask in masks:
            got = swap(total, "dp", mask)
            wait = []
            if mask == masks[-1]:
                (got,) = gate([got], [], GATES[i])
                wait = [sums[-1][0]] if sums else parts[-1:]
                wait += [context_token] + sums[0][1:2] if last and sums else []
            total = add(total, got, *wait)
        got = swap(total, "dp", 2)
        if last and tokens:
            (got,) = gate([got], tokens[:1])
        four = [total, got, swap(total, "dp", 1), swap(got, "dp", 1)]
        sums.append(four)
        if aligned:
            value_grad, *token = final(four, start, scale, model, value_grad, not tokens)
            tokens += token
        start += total.shape[1]
    if not aligned:
        chunks = []
        for kept, got, far_kept, far_got in sums:
            low = line_bit() == 0
            near = jnp.where(low, jnp.concatenate([kept, got]), jnp.concatenate([got, kept]))
            far = jnp.where(low, jnp.concatenate([far_kept, far_got]), jnp.concatenate([far_got, far_kept]))
            chunks.append(jnp.where(core_index() == 0, jnp.concatenate([near, far]), jnp.concatenate([far, near])))
        value_grad = jnp.concatenate(chunks, axis=1).astype(F32) * scale
    return context[None], value_grad


def solution(mesh):
    in_specs = (P("dp", "seq", None), P("dp", None), P(None, "seq", None), P("dp", "seq", None))
    out_specs = (P("dp", "seq", None), P("seq", None))
    return jax.shard_map(body, mesh=mesh, in_specs=in_specs, out_specs=out_specs, check_vma=False)
```

```python
import functools

import jax
import jax.numpy as jnp
from jax import lax
from jax.experimental import pallas as pl
from jax.experimental.pallas import tpu as pltpu
from jax.sharding import PartitionSpec as P

HEAD = 120
PADDED = 128
BF16 = jnp.bfloat16
F32 = jnp.float32
VMEM = pl.BlockSpec(memory_space=pltpu.VMEM)
ANY = pl.BlockSpec(memory_space=pl.ANY)
HBM = pl.BlockSpec(memory_space=pltpu.HBM)
LIMIT = pltpu.CompilerParams(vmem_limit_bytes=12 * 1024 * 1024)
SMALL = pl.CostEstimate(flops=1000, bytes_accessed=1000, transcendentals=0)
def slow(work):
    return pl.CostEstimate(flops=int(work * 1e9), bytes_accessed=int(work * 2e6), transcendentals=0)


LARGE = slow(2)
GATES = (slow(3), slow(1), slow(0))
CUTS = (640, 640, 640)


def core_index():
    return lax.axis_index("dp") % 2


def line_bit():
    return lax.axis_index("dp") // 2 % 2


def swap(array, axis, mask):
    return lax.ppermute(array, axis, [(i, i ^ mask) for i in range(lax.axis_size(axis))])


def halves_kernel(x_ref, top_ref, bottom_ref):
    half = top_ref.shape[0]
    top_ref[...] = x_ref[:half]
    bottom_ref[...] = x_ref[half:]


def halves(block):
    rows, model = block.shape
    return pl.pallas_call(
        halves_kernel,
        out_shape=[jax.ShapeDtypeStruct((rows // 2, model), BF16)] * 2,
        in_specs=[VMEM],
        out_specs=[VMEM] * 2,
        compiler_params=LIMIT,
        cost_estimate=SMALL,
        name="halves",
    )(block)


def gate(arrays, after, cost=SMALL):
    return pl.pallas_call(
        lambda *refs: None,
        out_shape=[jax.ShapeDtypeStruct(a.shape, a.dtype) for a in arrays],
        in_specs=[VMEM] * len(arrays) + [ANY] * len(after),
        out_specs=[VMEM] * len(arrays),
        input_output_aliases={i: i for i in range(len(arrays))},
        compiler_params=LIMIT,
        cost_estimate=cost,
        name="gate",
    )(*arrays, *after)


def gather_blocks(block, axis, meanwhile):
    n = lax.axis_size(axis)
    if n != 4:
        return [[block]] + [[swap(block, axis, k)] for k in range(1, n)], meanwhile([block])
    top, bottom = halves(block)
    made = meanwhile([top, bottom])
    top_x, bottom_y = swap(top, axis, 1), swap(bottom, axis, 2)
    (top_x,), (bottom_y,) = gate([top_x], made), gate([bottom_y], made)
    bottom_x, top_y = swap(bottom, axis, 1), swap(top, axis, 2)
    top_xy, bottom_xy = swap(top_x, axis, 2), swap(bottom_y, axis, 1)
    return [[top, bottom], [top_x, bottom_x], [top_y, bottom_y], [top_xy, bottom_xy]], made


def padded_head(rows, h):
    own = rows[h * HEAD : (h + 1) * HEAD]
    zeros = jnp.zeros((PADDED - HEAD, rows.shape[1]), F32)
    return jnp.concatenate([own, zeros], axis=0).astype(BF16)


def shares_kernel(cot_ref, *refs):
    outs, turned = refs[:-1], refs[-1]
    turned[...] = cot_ref[...].astype(F32).T
    width, me = outs[0].shape[0], lax.axis_index("seq")
    for k, out in enumerate(outs):
        start = pl.multiple_of((me ^ k) * width, 8)
        out[...] = turned[pl.ds(start, width), :].astype(BF16)


def cotangent_shares(cotangent, n):
    rows, model = cotangent.shape
    return pl.pallas_call(
        shares_kernel,
        out_shape=[jax.ShapeDtypeStruct((model // n, rows), BF16)] * n,
        in_specs=[VMEM],
        out_specs=[VMEM] * n,
        scratch_shapes=[pltpu.VMEM((model, rows), F32)],
        compiler_params=LIMIT,
        cost_estimate=SMALL,
        name="cotangent_shares",
    )(cotangent)


def project_into(w_ref, first, frames, out_ref):
    count, heads = out_ref.shape[:2]

    def one(t, carry):
        rows = lax.dot_general(
            w_ref[first + t], frames, (((1,), (1,)), ((), ())), preferred_element_type=F32
        )
        for h in range(heads):
            out_ref[t, h] = padded_head(rows, h)
        return carry

    lax.fori_loop(0, count, one, 0)


def project_kernel(w_ref, *refs):
    project_into(w_ref, 0, jnp.concatenate([r[...] for r in refs[:-1]], axis=0), refs[-1])


def project(weights, blocks):
    rows = sum(b.shape[0] for b in blocks)
    heads = weights.shape[1] // HEAD
    return pl.pallas_call(
        project_kernel,
        out_shape=jax.ShapeDtypeStruct((2, heads, PADDED, rows), BF16),
        in_specs=[VMEM] * (1 + len(blocks)),
        out_specs=VMEM,
        compiler_params=LIMIT,
        cost_estimate=SMALL,
        name="project",
    )(weights, *blocks)


def block_spots(n, rows):
    me = lax.axis_index("seq")
    return [pl.ds(pl.multiple_of((me ^ k) * rows, PADDED), rows) for k in range(n)]


def arrange_kernel(n, ids_ref, *refs):
    pieces, (queries, keys, column) = refs[:-3], refs[-3:]
    heads, rows = queries.shape[0], ids_ref.shape[1] // n
    spot = block_spots(n, rows)
    for b in range(n):
        row = ids_ref[:, b * rows : (b + 1) * rows].astype(F32)
        column[b * rows : (b + 1) * rows, :] = jnp.broadcast_to(row, (PADDED, rows)).T
    k = 0
    for piece in pieces:
        for at in range(0, piece.shape[3], rows):
            for h in range(heads):
                queries[h, :, spot[k]] = piece[0, h, :, at : at + rows]
                keys[h, spot[k], :] = piece[1, h, :, at : at + rows].astype(F32).T.astype(BF16)
            k += 1


def arrange(ids, pieces, n):
    heads, total = pieces[0].shape[1], ids.shape[1]
    return pl.pallas_call(
        functools.partial(arrange_kernel, n),
        out_shape=[
            jax.ShapeDtypeStruct((heads, PADDED, total), BF16),
            jax.ShapeDtypeStruct((heads, total, PADDED), BF16),
            jax.ShapeDtypeStruct((total, PADDED), F32),
        ],
        in_specs=[VMEM] * (1 + len(pieces)),
        out_specs=[VMEM] * 3,
        compiler_params=LIMIT,
        cost_estimate=SMALL,
        name="arrange",
    )(ids, *pieces)


def attention_kernel(n, ids_ref, w_ref, column, *refs):
    last, (out_ref, queries, keys) = refs[:-5], refs[-3:]
    heads, total = out_ref.shape[:2]
    rows = total // n
    reach = total // 4 // rows
    frames = jnp.concatenate([r[...] for r in last], axis=0)
    spot = block_spots(n, rows)
    group = 2 if heads % 2 == 0 else 1
    for first in range(0, heads, group):
        own = [
            lax.dot_general(
                w_ref[t, first * HEAD : (first + group) * HEAD, :],
                frames,
                (((1,), (1,)), ((), ())),
                preferred_element_type=F32,
            )
            for t in range(2)
        ]
        for h in range(group):
            queries[first + h, :, spot[n - 1]] = padded_head(own[0], h)
            keys[first + h, spot[n - 1], :] = padded_head(own[1], h).astype(F32).T.astype(BF16)
        for h in range(first, first + group):
            for b in range(n):
                low, high = max(0, b - reach), min(n, b + reach + 1)
                scores = jnp.dot(
                    keys[h, low * rows : high * rows, :],
                    queries[h, :, b * rows : (b + 1) * rows],
                    preferred_element_type=F32,
                )
                same = column[low * rows : high * rows, :] == ids_ref[:, b * rows : (b + 1) * rows].astype(F32)
                scores = jnp.where(same, scores * HEAD**-0.5, -1e30)
                exponent = jnp.exp(scores - jnp.max(scores, axis=0, keepdims=True))
                inverse = 1.0 / jnp.sum(exponent, axis=0, keepdims=True)
                weights = (exponent * inverse).astype(BF16)
                for c in range(n):
                    if low <= c < high:
                        value = weights[(c - low) * rows : (c - low + 1) * rows]
                    else:
                        value = jnp.zeros((rows, rows), BF16)
                    out_ref[h, spot[c], spot[b]] = value


def attention_weights(ids, weights, pieces, last, n):
    heads, total = weights.shape[1] // HEAD, ids.shape[1]
    queries, keys, column = arrange(ids, pieces, n)
    out, _, _ = pl.pallas_call(
        functools.partial(attention_kernel, n),
        out_shape=[
            jax.ShapeDtypeStruct((heads, total, total), BF16),
            jax.ShapeDtypeStruct(queries.shape, BF16),
            jax.ShapeDtypeStruct(keys.shape, BF16),
        ],
        in_specs=[VMEM] * (5 + len(last)),
        out_specs=[VMEM] * 3,
        input_output_aliases={3 + len(last): 1, 4 + len(last): 2},
        compiler_params=LIMIT,
        cost_estimate=SMALL,
        name="attention_weights",
    )(ids, weights, column, *last, queries, keys)
    return out


def rows_times(values_ref, mine, blocks, start, cut):
    half = values_ref.shape[0] // 2
    core = core_index()
    at = half * (core if mine else 1 - core)
    if half % 16 == 0:
        values = values_ref[pl.ds(pl.multiple_of(at, 16), half), :]
    else:
        values = values_ref[...].astype(F32)
        values = jnp.where(at == 0, values[:half], values[half:]).astype(BF16)
    frames = jnp.concatenate([b[:, start : start + cut] for b in blocks], axis=0)
    return jnp.dot(values, frames, preferred_element_type=F32).astype(BF16)


def first_gradient_kernel(n, cut, weights_ref, *refs):
    cots, blocks, (values_ref, theirs) = refs[:n], refs[n:-2], refs[-2:]
    upstream = jnp.concatenate([c[...] for c in cots], axis=1).astype(F32)
    rows = []
    for h in range(weights_ref.shape[0]):
        rows.append(
            lax.dot_general(
                padded_head(upstream, h), weights_ref[h], (((1,), (1,)), ((), ())), preferred_element_type=F32
            )[:HEAD]
        )
    values_ref[...] = jnp.concatenate(rows, axis=0).astype(BF16)
    theirs[...] = rows_times(values_ref, False, blocks, 0, cut)


def next_gradient_kernel(values_ref, *refs):
    outs, blocks = refs[1 - 2 * len(CUTS) :], refs[: 1 - 2 * len(CUTS)]
    start = 0
    for i, cut in enumerate(CUTS):
        for mine in (False, True) if i else (True,):
            outs[2 * i - 1 + mine][...] = rows_times(values_ref, mine, blocks, start, cut)
        start += cut


def gradient(weights, cots, blocks):
    width, total, model = cots[0].shape[0], weights.shape[1], blocks[0].shape[1]

    def shape(cut):
        return jax.ShapeDtypeStruct((width // 2, cut), BF16)

    values, first = pl.pallas_call(
        functools.partial(first_gradient_kernel, len(cots), CUTS[0]),
        out_shape=[jax.ShapeDtypeStruct((width, total), BF16), shape(CUTS[0])],
        in_specs=[VMEM] * (1 + len(cots) + len(blocks)),
        out_specs=[VMEM] * 2,
        compiler_params=LIMIT,
        cost_estimate=SMALL,
        name="first_gradient",
    )(weights, *cots, *blocks)
    outs = pl.pallas_call(
        next_gradient_kernel,
        out_shape=[shape(CUTS[0])] + [shape(cut) for cut in CUTS[1:] for _ in range(2)],
        in_specs=[VMEM] * (1 + len(blocks)),
        out_specs=[VMEM] * (2 * len(CUTS) - 1),
        compiler_params=LIMIT,
        cost_estimate=pl.CostEstimate(
            flops=4 * width * total * model, bytes_accessed=2 * total * model, transcendentals=0
        ),
        name="next_gradient",
    )(values, *blocks)
    outs = [first] + list(outs)
    return list(zip(outs[::2], outs[1::2]))


def context_kernel(n, weights_ref, w_ref, *refs):
    blocks, outs, values = refs[: -n - 1], refs[-n - 1 : -1], refs[-1]
    project_into(w_ref, 2, jnp.concatenate([r[...] for r in blocks], axis=0), values)
    rows = outs[0].shape[1]
    found = [
        jnp.dot(values[0, h], weights_ref[h], preferred_element_type=F32)[:HEAD]
        for h in range(weights_ref.shape[0])
    ]
    stacked = jnp.concatenate(found, axis=0)
    for k, out in enumerate(outs):
        out[...] = stacked[:, k * rows : (k + 1) * rows].astype(BF16)


def contexts_of(weights, projections, blocks, n):
    heads, total = weights.shape[:2]
    return pl.pallas_call(
        functools.partial(context_kernel, n),
        out_shape=[jax.ShapeDtypeStruct((heads * HEAD, total // n), BF16)] * n,
        in_specs=[VMEM] * (2 + len(blocks)),
        out_specs=[VMEM] * n,
        scratch_shapes=[pltpu.VMEM((1, heads, PADDED, total), BF16)],
        compiler_params=LIMIT,
        cost_estimate=SMALL,
        name="contexts",
    )(weights, projections, *blocks)


def assemble_kernel(*refs):
    n = len(refs) - 3
    out, token, turned = refs[n:]
    width, me = refs[0].shape[0], lax.axis_index("seq")
    for k in range(n):
        start = pl.multiple_of((me ^ k) * width, 8)
        turned[pl.ds(start, width), :] = refs[k][...].astype(F32)
    out[...] = turned[...].T.astype(BF16)
    token[...] = jnp.zeros_like(token)


def assemble_context(pieces):
    n, (width, rows) = len(pieces), pieces[0].shape
    return pl.pallas_call(
        assemble_kernel,
        out_shape=[jax.ShapeDtypeStruct((rows, n * width), BF16), jax.ShapeDtypeStruct((8, PADDED), F32)],
        in_specs=[VMEM] * n,
        out_specs=[VMEM] * 2,
        scratch_shapes=[pltpu.VMEM((n * width, rows), F32)],
        compiler_params=LIMIT,
        cost_estimate=LARGE,
        name="assemble_context",
    )(*pieces)


def final_kernel(places, start, scale, marked, *refs):
    pieces, (scratch, sems) = refs[: len(places)], refs[-2:]
    out_ref = refs[-4] if marked else refs[-3]
    rows, cut = pieces[0].shape
    place = 2 * core_index() + line_bit()
    copies = []
    for i, (k, piece) in enumerate(zip(places, pieces)):
        at = pl.multiple_of((place ^ k) * rows, 8)
        if len(places) == 4:
            scratch[pl.ds(at, rows), :] = piece[...].astype(F32) * scale
        else:
            scratch[i * rows : (i + 1) * rows, :] = piece[...].astype(F32) * scale
            copies.append(
                pltpu.make_async_copy(
                    scratch.at[pl.ds(i * rows, rows)],
                    out_ref.at[pl.ds(at, rows), pl.ds(start, cut)],
                    sems.at[i],
                )
            )
            copies[-1].start()
    if not copies:
        copies = [pltpu.make_async_copy(scratch, out_ref.at[:, pl.ds(start, cut)], sems.at[0])]
        copies[0].start()
    if marked:
        refs[-3][...] = jnp.zeros_like(refs[-3])
    for copy in copies:
        copy.wait()


def final(places, pieces, start, scale, model, out, marked):
    rows, cut = pieces[0].shape
    earlier = [] if out is None else [out]
    return pl.pallas_call(
        functools.partial(final_kernel, places, start, scale, marked),
        out_shape=[jax.ShapeDtypeStruct((4 * rows, model), F32)] + [jax.ShapeDtypeStruct((8, PADDED), F32)] * marked,
        in_specs=[VMEM] * len(pieces) + [HBM] * len(earlier),
        out_specs=[HBM] + [VMEM] * marked,
        scratch_shapes=[pltpu.VMEM((len(pieces) * rows, cut), F32), pltpu.SemaphoreType.DMA((len(pieces),))],
        input_output_aliases={len(pieces): 0} if earlier else {},
        compiler_params=LIMIT,
        cost_estimate=SMALL,
        name="final",
    )(*pieces, *earlier)


def add_kernel(a_ref, b_ref, *refs):
    refs[-1][...] = (a_ref[...].astype(F32) + b_ref[...].astype(F32)).astype(BF16)


def add(a, b, *after):
    return pl.pallas_call(
        add_kernel,
        out_shape=jax.ShapeDtypeStruct(a.shape, BF16),
        in_specs=[VMEM, VMEM] + [ANY] * len(after),
        out_specs=VMEM,
        compiler_params=LIMIT,
        cost_estimate=SMALL,
        name="add",
    )(a, b, *after)


def split_sum_kernel(a_ref, b_ref, *refs):
    sent, kept = refs[-2:]
    total = a_ref[...].astype(F32) + b_ref[...].astype(F32)
    half = sent.shape[0]
    low = line_bit() == 0
    sent[...] = jnp.where(low, total[half:], total[:half]).astype(BF16)
    kept[...] = jnp.where(low, total[:half], total[half:]).astype(BF16)


def split_sum(a, b, *after):
    rows, columns = a.shape
    return pl.pallas_call(
        split_sum_kernel,
        out_shape=[jax.ShapeDtypeStruct((rows // 2, columns), BF16)] * 2,
        in_specs=[VMEM, VMEM] + [ANY] * len(after),
        out_specs=[VMEM] * 2,
        compiler_params=LIMIT,
        cost_estimate=SMALL,
        name="split_sum",
    )(a, b, *after)


def body(features, segment_ids, projections, cotangent):
    n, count = lax.axis_size("seq"), lax.axis_size("dp")
    model, width = features.shape[2], projections.shape[1]
    scale = 1.0 / count
    shares = cotangent_shares(cotangent[0], n)

    def meanwhile(own):
        return [project(projections, own), shares[0]]

    blocks, (own_piece, _) = gather_blocks(features[0], "seq", meanwhile)

    def flat(some):
        return [part for block in some for part in block]

    pieces = [own_piece]
    if n > 2:
        pieces.append(project(projections, flat(blocks[1 : n - 1])))
    sent = gate(shares[1:], pieces[1:])
    cots = [shares[0]] + [swap(share, "seq", k + 1) for k, share in enumerate(sent)]
    weights = attention_weights(segment_ids, projections, pieces, flat(blocks[n - 1 :]), n)
    contexts = contexts_of(weights, projections, flat(blocks), n)
    received = [contexts[0]] + [swap(contexts[k], "seq", k) for k in range(1, n)]
    context, context_token = assemble_context(received)

    parts, split = [], []
    for i, (theirs, mine) in enumerate(gradient(weights, cots, flat(blocks))):
        after = [] if not split else split[0][:1] if i < 2 else parts[:1]
        split.append(split_sum(mine, swap(theirs, "dp", 1), *after))
        sent, own = split[-1]
        passed = swap(sent, "dp", 2)
        parts.append(add(own, passed, *(parts[-1:] or contexts[:1])))

    masks = [1 << b for b in range(2, count.bit_length() - 1)]
    aligned = width % 32 == 0
    value_grad, start, sums, tokens = None, 0, [], []
    for i, total in enumerate(parts):
        last = i == len(parts) - 1
        for mask in masks:
            got = swap(total, "dp", mask)
            wait = []
            if mask == masks[-1]:
                (got,) = gate([got], [], GATES[i])
                wait = [sums[-1][0]] if sums else parts[-1:]
                wait += [context_token] + sums[0][1:2] if last and sums else []
            total = add(total, got, *wait)
        got = swap(total, "dp", 2)
        if last and tokens:
            (got,) = gate([got], tokens[:1])
        four = [total, got, swap(total, "dp", 1), swap(got, "dp", 1)]
        sums.append(four)
        if aligned:
            value_grad, *token = final((0, 1, 2, 3), four, start, scale, model, value_grad, not tokens)
            tokens += token
        start += total.shape[1]
    if not aligned:
        chunks = []
        for kept, got, far_kept, far_got in sums:
            low = line_bit() == 0
            near = jnp.where(low, jnp.concatenate([kept, got]), jnp.concatenate([got, kept]))
            far = jnp.where(low, jnp.concatenate([far_kept, far_got]), jnp.concatenate([far_got, far_kept]))
            chunks.append(jnp.where(core_index() == 0, jnp.concatenate([near, far]), jnp.concatenate([far, near])))
        value_grad = jnp.concatenate(chunks, axis=1).astype(F32) * scale
    return context[None], value_grad


def solution(mesh):
    in_specs = (P("dp", "seq", None), P("dp", None), P(None, "seq", None), P("dp", "seq", None))
    out_specs = (P("dp", "seq", None), P("seq", None))
    return jax.shard_map(body, mesh=mesh, in_specs=in_specs, out_specs=out_specs, check_vma=False)
```

```python
import functools

import jax
import jax.numpy as jnp
from jax import lax
from jax.experimental import pallas as pl
from jax.experimental.pallas import tpu as pltpu
from jax.sharding import PartitionSpec as P

HEAD = 120
PADDED = 128
BF16 = jnp.bfloat16
F32 = jnp.float32
VMEM = pl.BlockSpec(memory_space=pltpu.VMEM)
ANY = pl.BlockSpec(memory_space=pl.ANY)
HBM = pl.BlockSpec(memory_space=pltpu.HBM)
LIMIT = pltpu.CompilerParams(vmem_limit_bytes=12 * 1024 * 1024)
SMALL = pl.CostEstimate(flops=1000, bytes_accessed=1000, transcendentals=0)
def slow(work):
    return pl.CostEstimate(flops=int(work * 1e9), bytes_accessed=int(work * 2e6), transcendentals=0)


LARGE = slow(2)
GATES = (slow(3), slow(1), slow(0))
CUTS = (640, 640, 640)


def core_index():
    return lax.axis_index("dp") % 2


def line_bit():
    return lax.axis_index("dp") // 2 % 2


def swap(array, axis, mask):
    return lax.ppermute(array, axis, [(i, i ^ mask) for i in range(lax.axis_size(axis))])


def halves_kernel(x_ref, top_ref, bottom_ref):
    half = top_ref.shape[0]
    top_ref[...] = x_ref[:half]
    bottom_ref[...] = x_ref[half:]


def halves(block):
    rows, model = block.shape
    return pl.pallas_call(
        halves_kernel,
        out_shape=[jax.ShapeDtypeStruct((rows // 2, model), BF16)] * 2,
        in_specs=[VMEM],
        out_specs=[VMEM] * 2,
        compiler_params=LIMIT,
        cost_estimate=SMALL,
        name="halves",
    )(block)


def gate(arrays, after, cost=SMALL):
    return pl.pallas_call(
        lambda *refs: None,
        out_shape=[jax.ShapeDtypeStruct(a.shape, a.dtype) for a in arrays],
        in_specs=[VMEM] * len(arrays) + [ANY] * len(after),
        out_specs=[VMEM] * len(arrays),
        input_output_aliases={i: i for i in range(len(arrays))},
        compiler_params=LIMIT,
        cost_estimate=cost,
        name="gate",
    )(*arrays, *after)


def gather_blocks(block, axis, meanwhile):
    n = lax.axis_size(axis)
    if n != 4:
        return [[block]] + [[swap(block, axis, k)] for k in range(1, n)], meanwhile([block])
    top, bottom = halves(block)
    made = meanwhile([top, bottom])
    top_x, bottom_y = swap(top, axis, 1), swap(bottom, axis, 2)
    (top_x,), (bottom_y,) = gate([top_x], made), gate([bottom_y], made)
    bottom_x, top_y = swap(bottom, axis, 1), swap(top, axis, 2)
    top_xy, bottom_xy = swap(top_x, axis, 2), swap(bottom_y, axis, 1)
    return [[top, bottom], [top_x, bottom_x], [top_y, bottom_y], [top_xy, bottom_xy]], made


def padded_head(rows, h):
    own = rows[h * HEAD : (h + 1) * HEAD]
    zeros = jnp.zeros((PADDED - HEAD, rows.shape[1]), F32)
    return jnp.concatenate([own, zeros], axis=0).astype(BF16)


def shares_kernel(cot_ref, *refs):
    outs, turned = refs[:-1], refs[-1]
    turned[...] = cot_ref[...].astype(F32).T
    width, me = outs[0].shape[0], lax.axis_index("seq")
    for k, out in enumerate(outs):
        start = pl.multiple_of((me ^ k) * width, 8)
        out[...] = turned[pl.ds(start, width), :].astype(BF16)


def cotangent_shares(cotangent, n):
    rows, model = cotangent.shape
    return pl.pallas_call(
        shares_kernel,
        out_shape=[jax.ShapeDtypeStruct((model // n, rows), BF16)] * n,
        in_specs=[VMEM],
        out_specs=[VMEM] * n,
        scratch_shapes=[pltpu.VMEM((model, rows), F32)],
        compiler_params=LIMIT,
        cost_estimate=SMALL,
        name="cotangent_shares",
    )(cotangent)


def project_into(w_ref, first, frames, out_ref):
    count, heads = out_ref.shape[:2]

    def one(t, carry):
        rows = lax.dot_general(
            w_ref[first + t], frames, (((1,), (1,)), ((), ())), preferred_element_type=F32
        )
        for h in range(heads):
            out_ref[t, h] = padded_head(rows, h)
        return carry

    lax.fori_loop(0, count, one, 0)


def project_kernel(w_ref, *refs):
    project_into(w_ref, 0, jnp.concatenate([r[...] for r in refs[:-1]], axis=0), refs[-1])


def project(weights, blocks):
    rows = sum(b.shape[0] for b in blocks)
    heads = weights.shape[1] // HEAD
    return pl.pallas_call(
        project_kernel,
        out_shape=jax.ShapeDtypeStruct((2, heads, PADDED, rows), BF16),
        in_specs=[VMEM] * (1 + len(blocks)),
        out_specs=VMEM,
        compiler_params=LIMIT,
        cost_estimate=SMALL,
        name="project",
    )(weights, *blocks)


def block_spots(n, rows):
    me = lax.axis_index("seq")
    return [pl.ds(pl.multiple_of((me ^ k) * rows, PADDED), rows) for k in range(n)]


def arrange_kernel(n, ids_ref, *refs):
    pieces, (queries, keys, column) = refs[:-3], refs[-3:]
    heads, rows = queries.shape[0], ids_ref.shape[1] // n
    spot = block_spots(n, rows)
    for b in range(n):
        row = ids_ref[:, b * rows : (b + 1) * rows].astype(F32)
        column[b * rows : (b + 1) * rows, :] = jnp.broadcast_to(row, (PADDED, rows)).T
    k = 0
    for piece in pieces:
        for at in range(0, piece.shape[3], rows):
            for h in range(heads):
                queries[h, :, spot[k]] = piece[0, h, :, at : at + rows]
                keys[h, spot[k], :] = piece[1, h, :, at : at + rows].astype(F32).T.astype(BF16)
            k += 1


def arrange(ids, pieces, n):
    heads, total = pieces[0].shape[1], ids.shape[1]
    return pl.pallas_call(
        functools.partial(arrange_kernel, n),
        out_shape=[
            jax.ShapeDtypeStruct((heads, PADDED, total), BF16),
            jax.ShapeDtypeStruct((heads, total, PADDED), BF16),
            jax.ShapeDtypeStruct((total, PADDED), F32),
        ],
        in_specs=[VMEM] * (1 + len(pieces)),
        out_specs=[VMEM] * 3,
        compiler_params=LIMIT,
        cost_estimate=SMALL,
        name="arrange",
    )(ids, *pieces)


def attention_kernel(n, ids_ref, w_ref, column, *refs):
    last, (out_ref, queries, keys) = refs[:-5], refs[-3:]
    heads, total = out_ref.shape[:2]
    rows = total // n
    reach = total // 4 // rows
    frames = jnp.concatenate([r[...] for r in last], axis=0)
    spot = block_spots(n, rows)
    group = 2 if heads % 2 == 0 else 1
    for first in range(0, heads, group):
        own = [
            lax.dot_general(
                w_ref[t, first * HEAD : (first + group) * HEAD, :],
                frames,
                (((1,), (1,)), ((), ())),
                preferred_element_type=F32,
            )
            for t in range(2)
        ]
        for h in range(group):
            queries[first + h, :, spot[n - 1]] = padded_head(own[0], h)
            keys[first + h, spot[n - 1], :] = padded_head(own[1], h).astype(F32).T.astype(BF16)
        for h in range(first, first + group):
            for b in range(n):
                low, high = max(0, b - reach), min(n, b + reach + 1)
                scores = jnp.dot(
                    keys[h, low * rows : high * rows, :],
                    queries[h, :, b * rows : (b + 1) * rows],
                    preferred_element_type=F32,
                )
                same = column[low * rows : high * rows, :] == ids_ref[:, b * rows : (b + 1) * rows].astype(F32)
                scores = jnp.where(same, scores * HEAD**-0.5, -1e30)
                exponent = jnp.exp(scores - jnp.max(scores, axis=0, keepdims=True))
                inverse = 1.0 / jnp.sum(exponent, axis=0, keepdims=True)
                weights = (exponent * inverse).astype(BF16)
                for c in range(n):
                    if low <= c < high:
                        value = weights[(c - low) * rows : (c - low + 1) * rows]
                    else:
                        value = jnp.zeros((rows, rows), BF16)
                    out_ref[h, spot[c], spot[b]] = value


def attention_weights(ids, weights, pieces, last, n):
    heads, total = weights.shape[1] // HEAD, ids.shape[1]
    queries, keys, column = arrange(ids, pieces, n)
    out, _, _ = pl.pallas_call(
        functools.partial(attention_kernel, n),
        out_shape=[
            jax.ShapeDtypeStruct((heads, total, total), BF16),
            jax.ShapeDtypeStruct(queries.shape, BF16),
            jax.ShapeDtypeStruct(keys.shape, BF16),
        ],
        in_specs=[VMEM] * (5 + len(last)),
        out_specs=[VMEM] * 3,
        input_output_aliases={3 + len(last): 1, 4 + len(last): 2},
        compiler_params=LIMIT,
        cost_estimate=SMALL,
        name="attention_weights",
    )(ids, weights, column, *last, queries, keys)
    return out


def rows_times(values_ref, mine, blocks, start, cut):
    half = values_ref.shape[0] // 2
    core = core_index()
    at = half * (core if mine else 1 - core)
    if half % 16 == 0:
        values = values_ref[pl.ds(pl.multiple_of(at, 16), half), :]
    else:
        values = values_ref[...].astype(F32)
        values = jnp.where(at == 0, values[:half], values[half:]).astype(BF16)
    frames = jnp.concatenate([b[:, start : start + cut] for b in blocks], axis=0)
    return jnp.dot(values, frames, preferred_element_type=F32).astype(BF16)


def first_gradient_kernel(n, cut, weights_ref, *refs):
    cots, blocks, (values_ref, theirs) = refs[:n], refs[n:-2], refs[-2:]
    upstream = jnp.concatenate([c[...] for c in cots], axis=1).astype(F32)
    rows = []
    for h in range(weights_ref.shape[0]):
        rows.append(
            lax.dot_general(
                padded_head(upstream, h), weights_ref[h], (((1,), (1,)), ((), ())), preferred_element_type=F32
            )[:HEAD]
        )
    values_ref[...] = jnp.concatenate(rows, axis=0).astype(BF16)
    theirs[...] = rows_times(values_ref, False, blocks, 0, cut)


def next_gradient_kernel(values_ref, *refs):
    outs, blocks = refs[1 - 2 * len(CUTS) :], refs[: 1 - 2 * len(CUTS)]
    start = 0
    for i, cut in enumerate(CUTS):
        for mine in (False, True) if i else (True,):
            outs[2 * i - 1 + mine][...] = rows_times(values_ref, mine, blocks, start, cut)
        start += cut


def gradient(weights, cots, blocks):
    width, total, model = cots[0].shape[0], weights.shape[1], blocks[0].shape[1]

    def shape(cut):
        return jax.ShapeDtypeStruct((width // 2, cut), BF16)

    values, first = pl.pallas_call(
        functools.partial(first_gradient_kernel, len(cots), CUTS[0]),
        out_shape=[jax.ShapeDtypeStruct((width, total), BF16), shape(CUTS[0])],
        in_specs=[VMEM] * (1 + len(cots) + len(blocks)),
        out_specs=[VMEM] * 2,
        compiler_params=LIMIT,
        cost_estimate=SMALL,
        name="first_gradient",
    )(weights, *cots, *blocks)
    outs = pl.pallas_call(
        next_gradient_kernel,
        out_shape=[shape(CUTS[0])] + [shape(cut) for cut in CUTS[1:] for _ in range(2)],
        in_specs=[VMEM] * (1 + len(blocks)),
        out_specs=[VMEM] * (2 * len(CUTS) - 1),
        compiler_params=LIMIT,
        cost_estimate=pl.CostEstimate(
            flops=4 * width * total * model, bytes_accessed=2 * total * model, transcendentals=0
        ),
        name="next_gradient",
    )(values, *blocks)
    outs = [first] + list(outs)
    return list(zip(outs[::2], outs[1::2]))


def context_kernel(n, weights_ref, w_ref, *refs):
    blocks, outs, values = refs[: -n - 1], refs[-n - 1 : -1], refs[-1]
    project_into(w_ref, 2, jnp.concatenate([r[...] for r in blocks], axis=0), values)
    rows = outs[0].shape[1]
    found = [
        jnp.dot(values[0, h], weights_ref[h], preferred_element_type=F32)[:HEAD]
        for h in range(weights_ref.shape[0])
    ]
    stacked = jnp.concatenate(found, axis=0)
    for k, out in enumerate(outs):
        out[...] = stacked[:, k * rows : (k + 1) * rows].astype(BF16)


def contexts_of(weights, projections, blocks, n):
    heads, total = weights.shape[:2]
    return pl.pallas_call(
        functools.partial(context_kernel, n),
        out_shape=[jax.ShapeDtypeStruct((heads * HEAD, total // n), BF16)] * n,
        in_specs=[VMEM] * (2 + len(blocks)),
        out_specs=[VMEM] * n,
        scratch_shapes=[pltpu.VMEM((1, heads, PADDED, total), BF16)],
        compiler_params=LIMIT,
        cost_estimate=SMALL,
        name="contexts",
    )(weights, projections, *blocks)


def assemble_kernel(*refs):
    n = len(refs) - 3
    out, token, turned = refs[n:]
    width, me = refs[0].shape[0], lax.axis_index("seq")
    for k in range(n):
        start = pl.multiple_of((me ^ k) * width, 8)
        turned[pl.ds(start, width), :] = refs[k][...].astype(F32)
    out[...] = turned[...].T.astype(BF16)
    token[...] = jnp.zeros_like(token)


def assemble_context(pieces):
    n, (width, rows) = len(pieces), pieces[0].shape
    return pl.pallas_call(
        assemble_kernel,
        out_shape=[jax.ShapeDtypeStruct((rows, n * width), BF16), jax.ShapeDtypeStruct((8, PADDED), F32)],
        in_specs=[VMEM] * n,
        out_specs=[VMEM] * 2,
        scratch_shapes=[pltpu.VMEM((n * width, rows), F32)],
        compiler_params=LIMIT,
        cost_estimate=LARGE,
        name="assemble_context",
    )(*pieces)


def final_kernel(places, start, scale, marked, *refs):
    pieces, (scratch, sems) = refs[: len(places)], refs[-2:]
    out_ref = refs[-4] if marked else refs[-3]
    rows, cut = pieces[0].shape
    place = 2 * core_index() + line_bit()
    copies = []
    for i, (k, piece) in enumerate(zip(places, pieces)):
        at = pl.multiple_of((place ^ k) * rows, 8)
        if len(places) == 4:
            scratch[pl.ds(at, rows), :] = piece[...].astype(F32) * scale
        else:
            scratch[i * rows : (i + 1) * rows, :] = piece[...].astype(F32) * scale
            copies.append(
                pltpu.make_async_copy(
                    scratch.at[pl.ds(i * rows, rows)],
                    out_ref.at[pl.ds(at, rows), pl.ds(start, cut)],
                    sems.at[i],
                )
            )
            copies[-1].start()
    if not copies:
        copies = [pltpu.make_async_copy(scratch, out_ref.at[:, pl.ds(start, cut)], sems.at[0])]
        copies[0].start()
    if marked:
        refs[-3][...] = jnp.zeros_like(refs[-3])
    for copy in copies:
        copy.wait()


def final(places, pieces, start, scale, model, out, marked):
    rows, cut = pieces[0].shape
    earlier = [] if out is None else [out]
    return pl.pallas_call(
        functools.partial(final_kernel, places, start, scale, marked),
        out_shape=[jax.ShapeDtypeStruct((4 * rows, model), F32)] + [jax.ShapeDtypeStruct((8, PADDED), F32)] * marked,
        in_specs=[VMEM] * len(pieces) + [HBM] * len(earlier),
        out_specs=[HBM] + [VMEM] * marked,
        scratch_shapes=[pltpu.VMEM((len(pieces) * rows, cut), F32), pltpu.SemaphoreType.DMA((len(pieces),))],
        input_output_aliases={len(pieces): 0} if earlier else {},
        compiler_params=LIMIT,
        cost_estimate=SMALL,
        name="final",
    )(*pieces, *earlier)


def add_kernel(a_ref, b_ref, *refs):
    refs[-1][...] = (a_ref[...].astype(F32) + b_ref[...].astype(F32)).astype(BF16)


def add(a, b, *after):
    return pl.pallas_call(
        add_kernel,
        out_shape=jax.ShapeDtypeStruct(a.shape, BF16),
        in_specs=[VMEM, VMEM] + [ANY] * len(after),
        out_specs=VMEM,
        compiler_params=LIMIT,
        cost_estimate=SMALL,
        name="add",
    )(a, b, *after)


def split_sum_kernel(a_ref, b_ref, *refs):
    sent, kept = refs[-2:]
    total = a_ref[...].astype(F32) + b_ref[...].astype(F32)
    half = sent.shape[0]
    low = line_bit() == 0
    sent[...] = jnp.where(low, total[half:], total[:half]).astype(BF16)
    kept[...] = jnp.where(low, total[:half], total[half:]).astype(BF16)


def split_sum(a, b, *after):
    rows, columns = a.shape
    return pl.pallas_call(
        split_sum_kernel,
        out_shape=[jax.ShapeDtypeStruct((rows // 2, columns), BF16)] * 2,
        in_specs=[VMEM, VMEM] + [ANY] * len(after),
        out_specs=[VMEM] * 2,
        compiler_params=LIMIT,
        cost_estimate=SMALL,
        name="split_sum",
    )(a, b, *after)


def body(features, segment_ids, projections, cotangent):
    n, count = lax.axis_size("seq"), lax.axis_size("dp")
    model, width = features.shape[2], projections.shape[1]
    scale = 1.0 / count
    shares = cotangent_shares(cotangent[0], n)

    def meanwhile(own):
        return [project(projections, own), shares[0]]

    blocks, (own_piece, _) = gather_blocks(features[0], "seq", meanwhile)

    def flat(some):
        return [part for block in some for part in block]

    pieces = [own_piece]
    if n > 2:
        pieces.append(project(projections, flat(blocks[1 : n - 1])))
    sent = gate(shares[1:], flat(blocks[1:3])[1:3])
    cots = [shares[0]] + [swap(share, "seq", k + 1) for k, share in enumerate(sent)]
    weights = attention_weights(segment_ids, projections, pieces, flat(blocks[n - 1 :]), n)
    contexts = contexts_of(weights, projections, flat(blocks), n)
    received = [contexts[0]] + [swap(contexts[k], "seq", k) for k in range(1, n)]
    context, context_token = assemble_context(received)

    masks = [1 << b for b in range(2, count.bit_length() - 1)]
    aligned = width % 32 == 0
    pairs = gradient(weights, cots, flat(blocks))
    parts, sums, split = [], [], []

    def halved(i, split_after, sum_after):
        theirs, mine = pairs[i]
        split.append(split_sum(mine, swap(theirs, "dp", 1), *split_after))
        sent, own = split[-1]
        parts.append(add(own, swap(sent, "dp", 2), *sum_after))

    def summed(i, wait, cost):
        total = parts[i]
        for mask in masks:
            got = swap(total, "dp", mask)
            if mask == masks[-1]:
                (got,) = gate([got], [], cost)
            total = add(total, got, *(wait if mask == masks[-1] else ()))
        sums.append([total, swap(total, "dp", 2)])

    halved(0, [], contexts[:1])
    halved(1, split[0][:1], parts[:1])
    summed(0, parts[1:2], GATES[0])
    halved(2, parts[:1], [parts[1], sums[0][0], context_token])
    summed(1, sums[0][:1], GATES[1])
    summed(2, [sums[1][0], sums[0][1]], GATES[2])
    value_grad, start, tokens = None, 0, []
    for i, (total, got) in enumerate(sums):
        if i == len(sums) - 1 and tokens:
            (got,) = gate([got], tokens[:1])
        sums[i] = four = [total, got, swap(total, "dp", 1), swap(got, "dp", 1)]
        if aligned:
            value_grad, *token = final((0, 1, 2, 3), four, start, scale, model, value_grad, not tokens)
            tokens += token
        start += total.shape[1]
    if not aligned:
        chunks = []
        for kept, got, far_kept, far_got in sums:
            low = line_bit() == 0
            near = jnp.where(low, jnp.concatenate([kept, got]), jnp.concatenate([got, kept]))
            far = jnp.where(low, jnp.concatenate([far_kept, far_got]), jnp.concatenate([far_got, far_kept]))
            chunks.append(jnp.where(core_index() == 0, jnp.concatenate([near, far]), jnp.concatenate([far, near])))
        value_grad = jnp.concatenate(chunks, axis=1).astype(F32) * scale
    return context[None], value_grad


def solution(mesh):
    in_specs = (P("dp", "seq", None), P("dp", None), P(None, "seq", None), P("dp", "seq", None))
    out_specs = (P("dp", "seq", None), P("seq", None))
    return jax.shard_map(body, mesh=mesh, in_specs=in_specs, out_specs=out_specs, check_vma=False)
```

```python
import functools

import jax
import jax.numpy as jnp
from jax import lax
from jax.experimental import pallas as pl
from jax.experimental.pallas import tpu as pltpu
from jax.sharding import PartitionSpec as P

HEAD = 120
PADDED = 128
BF16 = jnp.bfloat16
F32 = jnp.float32
VMEM = pl.BlockSpec(memory_space=pltpu.VMEM)
ANY = pl.BlockSpec(memory_space=pl.ANY)
HBM = pl.BlockSpec(memory_space=pltpu.HBM)
LIMIT = pltpu.CompilerParams(vmem_limit_bytes=12 * 1024 * 1024)
SMALL = pl.CostEstimate(flops=1000, bytes_accessed=1000, transcendentals=0)
def slow(work):
    return pl.CostEstimate(flops=int(work * 1e9), bytes_accessed=int(work * 2e6), transcendentals=0)


LARGE = slow(2)
GATES = (slow(3), slow(1), slow(0))
CUTS = (640, 640, 640)


def core_index():
    return lax.axis_index("dp") % 2


def line_bit():
    return lax.axis_index("dp") // 2 % 2


def swap(array, axis, mask):
    return lax.ppermute(array, axis, [(i, i ^ mask) for i in range(lax.axis_size(axis))])


def halves_kernel(x_ref, top_ref, bottom_ref):
    half = top_ref.shape[0]
    top_ref[...] = x_ref[:half]
    bottom_ref[...] = x_ref[half:]


def halves(block):
    rows, model = block.shape
    return pl.pallas_call(
        halves_kernel,
        out_shape=[jax.ShapeDtypeStruct((rows // 2, model), BF16)] * 2,
        in_specs=[VMEM],
        out_specs=[VMEM] * 2,
        compiler_params=LIMIT,
        cost_estimate=SMALL,
        name="halves",
    )(block)


def gate(arrays, after, cost=SMALL):
    return pl.pallas_call(
        lambda *refs: None,
        out_shape=[jax.ShapeDtypeStruct(a.shape, a.dtype) for a in arrays],
        in_specs=[VMEM] * len(arrays) + [ANY] * len(after),
        out_specs=[VMEM] * len(arrays),
        input_output_aliases={i: i for i in range(len(arrays))},
        compiler_params=LIMIT,
        cost_estimate=cost,
        name="gate",
    )(*arrays, *after)


def gather_blocks(block, axis, meanwhile):
    n = lax.axis_size(axis)
    if n != 4:
        return [[block]] + [[swap(block, axis, k)] for k in range(1, n)], meanwhile([block])
    top, bottom = halves(block)
    made = meanwhile([top, bottom])
    top_x, bottom_y = swap(top, axis, 1), swap(bottom, axis, 2)
    (top_x,), (bottom_y,) = gate([top_x], made), gate([bottom_y], made)
    bottom_x, top_y = swap(bottom, axis, 1), swap(top, axis, 2)
    top_xy, bottom_xy = swap(top_x, axis, 2), swap(bottom_y, axis, 1)
    return [[top, bottom], [top_x, bottom_x], [top_y, bottom_y], [top_xy, bottom_xy]], made


def padded_head(rows, h):
    own = rows[h * HEAD : (h + 1) * HEAD]
    zeros = jnp.zeros((PADDED - HEAD, rows.shape[1]), F32)
    return jnp.concatenate([own, zeros], axis=0).astype(BF16)


def shares_kernel(cot_ref, *refs):
    outs, turned = refs[:-1], refs[-1]
    turned[...] = cot_ref[...].astype(F32).T
    width, me = outs[0].shape[0], lax.axis_index("seq")
    for k, out in enumerate(outs):
        start = pl.multiple_of((me ^ k) * width, 8)
        out[...] = turned[pl.ds(start, width), :].astype(BF16)


def cotangent_shares(cotangent, n):
    rows, model = cotangent.shape
    return pl.pallas_call(
        shares_kernel,
        out_shape=[jax.ShapeDtypeStruct((model // n, rows), BF16)] * n,
        in_specs=[VMEM],
        out_specs=[VMEM] * n,
        scratch_shapes=[pltpu.VMEM((model, rows), F32)],
        compiler_params=LIMIT,
        cost_estimate=SMALL,
        name="cotangent_shares",
    )(cotangent)


def project_into(w_ref, first, frames, out_ref):
    count, heads = out_ref.shape[:2]

    def one(t, carry):
        rows = lax.dot_general(
            w_ref[first + t], frames, (((1,), (1,)), ((), ())), preferred_element_type=F32
        )
        for h in range(heads):
            out_ref[t, h] = padded_head(rows, h)
        return carry

    lax.fori_loop(0, count, one, 0)


def project_kernel(w_ref, *refs):
    project_into(w_ref, 0, jnp.concatenate([r[...] for r in refs[:-1]], axis=0), refs[-1])


def project(weights, blocks):
    rows = sum(b.shape[0] for b in blocks)
    heads = weights.shape[1] // HEAD
    return pl.pallas_call(
        project_kernel,
        out_shape=jax.ShapeDtypeStruct((2, heads, PADDED, rows), BF16),
        in_specs=[VMEM] * (1 + len(blocks)),
        out_specs=VMEM,
        compiler_params=LIMIT,
        cost_estimate=SMALL,
        name="project",
    )(weights, *blocks)


def block_spots(n, rows):
    me = lax.axis_index("seq")
    return [pl.ds(pl.multiple_of((me ^ k) * rows, PADDED), rows) for k in range(n)]


def arrange_kernel(n, ids_ref, *refs):
    pieces, (queries, keys, column) = refs[:-3], refs[-3:]
    heads, rows = queries.shape[0], ids_ref.shape[1] // n
    spot = block_spots(n, rows)
    for b in range(n):
        row = ids_ref[:, b * rows : (b + 1) * rows].astype(F32)
        column[b * rows : (b + 1) * rows, :] = jnp.broadcast_to(row, (PADDED, rows)).T
    k = 0
    for piece in pieces:
        for at in range(0, piece.shape[3], rows):
            for h in range(heads):
                queries[h, :, spot[k]] = piece[0, h, :, at : at + rows]
                keys[h, spot[k], :] = piece[1, h, :, at : at + rows].astype(F32).T.astype(BF16)
            k += 1


def arrange(ids, pieces, n):
    heads, total = pieces[0].shape[1], ids.shape[1]
    return pl.pallas_call(
        functools.partial(arrange_kernel, n),
        out_shape=[
            jax.ShapeDtypeStruct((heads, PADDED, total), BF16),
            jax.ShapeDtypeStruct((heads, total, PADDED), BF16),
            jax.ShapeDtypeStruct((total, PADDED), F32),
        ],
        in_specs=[VMEM] * (1 + len(pieces)),
        out_specs=[VMEM] * 3,
        compiler_params=LIMIT,
        cost_estimate=SMALL,
        name="arrange",
    )(ids, *pieces)


def attention_kernel(n, ids_ref, w_ref, column, *refs):
    last, (out_ref, queries, keys) = refs[:-5], refs[-3:]
    heads, total = out_ref.shape[:2]
    rows = total // n
    reach = total // 4 // rows
    frames = jnp.concatenate([r[...] for r in last], axis=0)
    spot = block_spots(n, rows)
    group = 2 if heads % 2 == 0 else 1
    for first in range(0, heads, group):
        own = [
            lax.dot_general(
                w_ref[t, first * HEAD : (first + group) * HEAD, :],
                frames,
                (((1,), (1,)), ((), ())),
                preferred_element_type=F32,
            )
            for t in range(2)
        ]
        for h in range(group):
            queries[first + h, :, spot[n - 1]] = padded_head(own[0], h)
            keys[first + h, spot[n - 1], :] = padded_head(own[1], h).astype(F32).T.astype(BF16)
        for h in range(first, first + group):
            for b in range(n):
                low, high = max(0, b - reach), min(n, b + reach + 1)
                scores = jnp.dot(
                    keys[h, low * rows : high * rows, :],
                    queries[h, :, b * rows : (b + 1) * rows],
                    preferred_element_type=F32,
                )
                same = column[low * rows : high * rows, :] == ids_ref[:, b * rows : (b + 1) * rows].astype(F32)
                scores = jnp.where(same, scores * HEAD**-0.5, -1e30)
                exponent = jnp.exp(scores - jnp.max(scores, axis=0, keepdims=True))
                inverse = 1.0 / jnp.sum(exponent, axis=0, keepdims=True)
                weights = (exponent * inverse).astype(BF16)
                for c in range(n):
                    if low <= c < high:
                        value = weights[(c - low) * rows : (c - low + 1) * rows]
                    else:
                        value = jnp.zeros((rows, rows), BF16)
                    out_ref[h, spot[c], spot[b]] = value


def attention_weights(ids, weights, pieces, last, n):
    heads, total = weights.shape[1] // HEAD, ids.shape[1]
    queries, keys, column = arrange(ids, pieces, n)
    out, _, _ = pl.pallas_call(
        functools.partial(attention_kernel, n),
        out_shape=[
            jax.ShapeDtypeStruct((heads, total, total), BF16),
            jax.ShapeDtypeStruct(queries.shape, BF16),
            jax.ShapeDtypeStruct(keys.shape, BF16),
        ],
        in_specs=[VMEM] * (5 + len(last)),
        out_specs=[VMEM] * 3,
        input_output_aliases={3 + len(last): 1, 4 + len(last): 2},
        compiler_params=LIMIT,
        cost_estimate=SMALL,
        name="attention_weights",
    )(ids, weights, column, *last, queries, keys)
    return out


def rows_times(values_ref, mine, blocks, start, cut):
    half = values_ref.shape[0] // 2
    core = core_index()
    at = half * (core if mine else 1 - core)
    if half % 16 == 0:
        values = values_ref[pl.ds(pl.multiple_of(at, 16), half), :]
    else:
        values = values_ref[...].astype(F32)
        values = jnp.where(at == 0, values[:half], values[half:]).astype(BF16)
    frames = jnp.concatenate([b[:, start : start + cut] for b in blocks], axis=0)
    return jnp.dot(values, frames, preferred_element_type=F32).astype(BF16)


def first_gradient_kernel(n, cut, weights_ref, *refs):
    cots, blocks, (values_ref, theirs) = refs[:n], refs[n:-2], refs[-2:]
    upstream = jnp.concatenate([c[...] for c in cots], axis=1).astype(F32)
    rows = []
    for h in range(weights_ref.shape[0]):
        rows.append(
            lax.dot_general(
                padded_head(upstream, h), weights_ref[h], (((1,), (1,)), ((), ())), preferred_element_type=F32
            )[:HEAD]
        )
    values_ref[...] = jnp.concatenate(rows, axis=0).astype(BF16)
    theirs[...] = rows_times(values_ref, False, blocks, 0, cut)


def next_gradient_kernel(values_ref, *refs):
    outs, blocks = refs[1 - 2 * len(CUTS) :], refs[: 1 - 2 * len(CUTS)]
    start = 0
    for i, cut in enumerate(CUTS):
        for mine in (False, True) if i else (True,):
            outs[2 * i - 1 + mine][...] = rows_times(values_ref, mine, blocks, start, cut)
        start += cut


def gradient(weights, cots, blocks):
    width, total, model = cots[0].shape[0], weights.shape[1], blocks[0].shape[1]

    def shape(cut):
        return jax.ShapeDtypeStruct((width // 2, cut), BF16)

    values, first = pl.pallas_call(
        functools.partial(first_gradient_kernel, len(cots), CUTS[0]),
        out_shape=[jax.ShapeDtypeStruct((width, total), BF16), shape(CUTS[0])],
        in_specs=[VMEM] * (1 + len(cots) + len(blocks)),
        out_specs=[VMEM] * 2,
        compiler_params=LIMIT,
        cost_estimate=SMALL,
        name="first_gradient",
    )(weights, *cots, *blocks)
    outs = pl.pallas_call(
        next_gradient_kernel,
        out_shape=[shape(CUTS[0])] + [shape(cut) for cut in CUTS[1:] for _ in range(2)],
        in_specs=[VMEM] * (1 + len(blocks)),
        out_specs=[VMEM] * (2 * len(CUTS) - 1),
        compiler_params=LIMIT,
        cost_estimate=pl.CostEstimate(
            flops=4 * width * total * model, bytes_accessed=2 * total * model, transcendentals=0
        ),
        name="next_gradient",
    )(values, *blocks)
    outs = [first] + list(outs)
    return list(zip(outs[::2], outs[1::2]))


def context_kernel(n, weights_ref, w_ref, *refs):
    blocks, outs, values = refs[: -n - 1], refs[-n - 1 : -1], refs[-1]
    project_into(w_ref, 2, jnp.concatenate([r[...] for r in blocks], axis=0), values)
    rows = outs[0].shape[1]
    found = [
        jnp.dot(values[0, h], weights_ref[h], preferred_element_type=F32)[:HEAD]
        for h in range(weights_ref.shape[0])
    ]
    stacked = jnp.concatenate(found, axis=0)
    for k, out in enumerate(outs):
        out[...] = stacked[:, k * rows : (k + 1) * rows].astype(BF16)


def contexts_of(weights, projections, blocks, n):
    heads, total = weights.shape[:2]
    return pl.pallas_call(
        functools.partial(context_kernel, n),
        out_shape=[jax.ShapeDtypeStruct((heads * HEAD, total // n), BF16)] * n,
        in_specs=[VMEM] * (2 + len(blocks)),
        out_specs=[VMEM] * n,
        scratch_shapes=[pltpu.VMEM((1, heads, PADDED, total), BF16)],
        compiler_params=LIMIT,
        cost_estimate=SMALL,
        name="contexts",
    )(weights, projections, *blocks)


def assemble_kernel(*refs):
    n = len(refs) - 3
    out, token, turned = refs[n:]
    width, me = refs[0].shape[0], lax.axis_index("seq")
    for k in range(n):
        start = pl.multiple_of((me ^ k) * width, 8)
        turned[pl.ds(start, width), :] = refs[k][...].astype(F32)
    out[...] = turned[...].T.astype(BF16)
    token[...] = jnp.zeros_like(token)


def assemble_context(pieces):
    n, (width, rows) = len(pieces), pieces[0].shape
    return pl.pallas_call(
        assemble_kernel,
        out_shape=[jax.ShapeDtypeStruct((rows, n * width), BF16), jax.ShapeDtypeStruct((8, PADDED), F32)],
        in_specs=[VMEM] * n,
        out_specs=[VMEM] * 2,
        scratch_shapes=[pltpu.VMEM((n * width, rows), F32)],
        compiler_params=LIMIT,
        cost_estimate=LARGE,
        name="assemble_context",
    )(*pieces)


def final_kernel(places, start, scale, marked, *refs):
    pieces, (scratch, sems) = refs[: len(places)], refs[-2:]
    out_ref = refs[-4] if marked else refs[-3]
    rows, cut = pieces[0].shape
    place = 2 * core_index() + line_bit()
    copies = []
    for i, (k, piece) in enumerate(zip(places, pieces)):
        at = pl.multiple_of((place ^ k) * rows, 8)
        if len(places) == 4:
            scratch[pl.ds(at, rows), :] = piece[...].astype(F32) * scale
        else:
            scratch[i * rows : (i + 1) * rows, :] = piece[...].astype(F32) * scale
            copies.append(
                pltpu.make_async_copy(
                    scratch.at[pl.ds(i * rows, rows)],
                    out_ref.at[pl.ds(at, rows), pl.ds(start, cut)],
                    sems.at[i],
                )
            )
            copies[-1].start()
    if not copies:
        copies = [pltpu.make_async_copy(scratch, out_ref.at[:, pl.ds(start, cut)], sems.at[0])]
        copies[0].start()
    if marked:
        refs[-3][...] = jnp.zeros_like(refs[-3])
    for copy in copies:
        copy.wait()


def final(places, pieces, start, scale, model, out, marked):
    rows, cut = pieces[0].shape
    earlier = [] if out is None else [out]
    return pl.pallas_call(
        functools.partial(final_kernel, places, start, scale, marked),
        out_shape=[jax.ShapeDtypeStruct((4 * rows, model), F32)] + [jax.ShapeDtypeStruct((8, PADDED), F32)] * marked,
        in_specs=[VMEM] * len(pieces) + [HBM] * len(earlier),
        out_specs=[HBM] + [VMEM] * marked,
        scratch_shapes=[pltpu.VMEM((len(pieces) * rows, cut), F32), pltpu.SemaphoreType.DMA((len(pieces),))],
        input_output_aliases={len(pieces): 0} if earlier else {},
        compiler_params=LIMIT,
        cost_estimate=SMALL,
        name="final",
    )(*pieces, *earlier)


def add_kernel(a_ref, b_ref, *refs):
    refs[-1][...] = (a_ref[...].astype(F32) + b_ref[...].astype(F32)).astype(BF16)


def add(a, b, *after):
    return pl.pallas_call(
        add_kernel,
        out_shape=jax.ShapeDtypeStruct(a.shape, BF16),
        in_specs=[VMEM, VMEM] + [ANY] * len(after),
        out_specs=VMEM,
        compiler_params=LIMIT,
        cost_estimate=SMALL,
        name="add",
    )(a, b, *after)


def split_sum_kernel(a_ref, b_ref, *refs):
    sent, kept = refs[-2:]
    total = a_ref[...].astype(F32) + b_ref[...].astype(F32)
    half = sent.shape[0]
    low = line_bit() == 0
    sent[...] = jnp.where(low, total[half:], total[:half]).astype(BF16)
    kept[...] = jnp.where(low, total[:half], total[half:]).astype(BF16)


def split_sum(a, b, *after):
    rows, columns = a.shape
    return pl.pallas_call(
        split_sum_kernel,
        out_shape=[jax.ShapeDtypeStruct((rows // 2, columns), BF16)] * 2,
        in_specs=[VMEM, VMEM] + [ANY] * len(after),
        out_specs=[VMEM] * 2,
        compiler_params=LIMIT,
        cost_estimate=SMALL,
        name="split_sum",
    )(a, b, *after)


def body(features, segment_ids, projections, cotangent):
    n, count = lax.axis_size("seq"), lax.axis_size("dp")
    model, width = features.shape[2], projections.shape[1]
    scale = 1.0 / count
    shares = cotangent_shares(cotangent[0], n)

    def meanwhile(own):
        return [project(projections, own), shares[0]]

    blocks, (own_piece, _) = gather_blocks(features[0], "seq", meanwhile)

    def flat(some):
        return [part for block in some for part in block]

    pieces = [own_piece]
    if n > 2:
        pieces.append(project(projections, flat(blocks[1 : n - 1])))
    sent = gate(shares[1:], flat(blocks[1:3])[1:3])
    cots = [shares[0]] + [swap(share, "seq", k + 1) for k, share in enumerate(sent)]
    weights = attention_weights(segment_ids, projections, pieces, flat(blocks[n - 1 :]), n)
    contexts = contexts_of(weights, projections, flat(blocks), n)
    parts, split = [], []
    for i, (theirs, mine) in enumerate(gradient(weights, cots, flat(blocks))):
        after = [] if not split else split[0][:1] if i < 2 else parts[:1]
        split.append(split_sum(mine, swap(theirs, "dp", 1), *after))
        sent, own = split[-1]
        passed = swap(sent, "dp", 2)
        parts.append(add(own, passed, *(parts[-1:] or contexts[:1])))

    moved = gate(contexts[1:], parts[1:2])
    received = [contexts[0]] + [swap(moved[k - 1], "seq", k) for k in range(1, n)]
    context, context_token = assemble_context(received)
    masks = [1 << b for b in range(2, count.bit_length() - 1)]
    aligned = width % 32 == 0
    value_grad, start, sums, tokens = None, 0, [], []
    for i, total in enumerate(parts):
        last = i == len(parts) - 1
        for mask in masks:
            got = swap(total, "dp", mask)
            wait = []
            if mask == masks[-1]:
                (got,) = gate([got], [], GATES[i])
                wait = [sums[-1][0]] if sums else parts[-1:]
                wait += [context_token] + sums[0][1:2] if last and sums else []
            total = add(total, got, *wait)
        got = swap(total, "dp", 2)
        if last and tokens:
            (got,) = gate([got], tokens[:1])
        four = [total, got, swap(total, "dp", 1), swap(got, "dp", 1)]
        sums.append(four)
        if aligned:
            value_grad, *token = final((0, 1, 2, 3), four, start, scale, model, value_grad, not tokens)
            tokens += token
        start += total.shape[1]
    if not aligned:
        chunks = []
        for kept, got, far_kept, far_got in sums:
            low = line_bit() == 0
            near = jnp.where(low, jnp.concatenate([kept, got]), jnp.concatenate([got, kept]))
            far = jnp.where(low, jnp.concatenate([far_kept, far_got]), jnp.concatenate([far_got, far_kept]))
            chunks.append(jnp.where(core_index() == 0, jnp.concatenate([near, far]), jnp.concatenate([far, near])))
        value_grad = jnp.concatenate(chunks, axis=1).astype(F32) * scale
    return context[None], value_grad


def solution(mesh):
    in_specs = (P("dp", "seq", None), P("dp", None), P(None, "seq", None), P("dp", "seq", None))
    out_specs = (P("dp", "seq", None), P("seq", None))
    return jax.shard_map(body, mesh=mesh, in_specs=in_specs, out_specs=out_specs, check_vma=False)
```

```python
import functools

import jax
import jax.numpy as jnp
from jax import lax
from jax.experimental import pallas as pl
from jax.experimental.pallas import tpu as pltpu
from jax.sharding import PartitionSpec as P

HEAD = 120
PADDED = 128
BF16 = jnp.bfloat16
F32 = jnp.float32
VMEM = pl.BlockSpec(memory_space=pltpu.VMEM)
ANY = pl.BlockSpec(memory_space=pl.ANY)
HBM = pl.BlockSpec(memory_space=pltpu.HBM)
LIMIT = pltpu.CompilerParams(vmem_limit_bytes=12 * 1024 * 1024)
SMALL = pl.CostEstimate(flops=1000, bytes_accessed=1000, transcendentals=0)
def slow(work):
    return pl.CostEstimate(flops=int(work * 1e9), bytes_accessed=int(work * 2e6), transcendentals=0)


LARGE = slow(2)
GATES = (slow(3), slow(1), slow(0))
CUTS = (640, 640, 640)


def core_index():
    return lax.axis_index("dp") % 2


def line_bit():
    return lax.axis_index("dp") // 2 % 2


def swap(array, axis, mask):
    return lax.ppermute(array, axis, [(i, i ^ mask) for i in range(lax.axis_size(axis))])


def halves_kernel(x_ref, top_ref, bottom_ref):
    half = top_ref.shape[0]
    top_ref[...] = x_ref[:half]
    bottom_ref[...] = x_ref[half:]


def halves(block):
    rows, model = block.shape
    return pl.pallas_call(
        halves_kernel,
        out_shape=[jax.ShapeDtypeStruct((rows // 2, model), BF16)] * 2,
        in_specs=[VMEM],
        out_specs=[VMEM] * 2,
        compiler_params=LIMIT,
        cost_estimate=SMALL,
        name="halves",
    )(block)


def gate(arrays, after, cost=SMALL):
    return pl.pallas_call(
        lambda *refs: None,
        out_shape=[jax.ShapeDtypeStruct(a.shape, a.dtype) for a in arrays],
        in_specs=[VMEM] * len(arrays) + [ANY] * len(after),
        out_specs=[VMEM] * len(arrays),
        input_output_aliases={i: i for i in range(len(arrays))},
        compiler_params=LIMIT,
        cost_estimate=cost,
        name="gate",
    )(*arrays, *after)


def gather_blocks(block, axis, meanwhile):
    n = lax.axis_size(axis)
    if n != 4:
        return [[block]] + [[swap(block, axis, k)] for k in range(1, n)], meanwhile([block])
    top, bottom = halves(block)
    made = meanwhile([top, bottom])
    top_x, bottom_y = swap(top, axis, 1), swap(bottom, axis, 2)
    (top_x,), (bottom_y,) = gate([top_x], made), gate([bottom_y], made)
    bottom_x, top_y = swap(bottom, axis, 1), swap(top, axis, 2)
    top_xy, bottom_xy = swap(top_x, axis, 2), swap(bottom_y, axis, 1)
    return [[top, bottom], [top_x, bottom_x], [top_y, bottom_y], [top_xy, bottom_xy]], made


def padded_head(rows, h):
    own = rows[h * HEAD : (h + 1) * HEAD]
    zeros = jnp.zeros((PADDED - HEAD, rows.shape[1]), F32)
    return jnp.concatenate([own, zeros], axis=0).astype(BF16)


def shares_kernel(cot_ref, *refs):
    outs, turned = refs[:-1], refs[-1]
    turned[...] = cot_ref[...].astype(F32).T
    width, me = outs[0].shape[0], lax.axis_index("seq")
    for k, out in enumerate(outs):
        start = pl.multiple_of((me ^ k) * width, 8)
        out[...] = turned[pl.ds(start, width), :].astype(BF16)


def cotangent_shares(cotangent, n):
    rows, model = cotangent.shape
    return pl.pallas_call(
        shares_kernel,
        out_shape=[jax.ShapeDtypeStruct((model // n, rows), BF16)] * n,
        in_specs=[VMEM],
        out_specs=[VMEM] * n,
        scratch_shapes=[pltpu.VMEM((model, rows), F32)],
        compiler_params=LIMIT,
        cost_estimate=SMALL,
        name="cotangent_shares",
    )(cotangent)


def project_into(w_ref, first, frames, out_ref):
    count, heads = out_ref.shape[:2]

    def one(t, carry):
        rows = lax.dot_general(
            w_ref[first + t], frames, (((1,), (1,)), ((), ())), preferred_element_type=F32
        )
        for h in range(heads):
            out_ref[t, h] = padded_head(rows, h)
        return carry

    lax.fori_loop(0, count, one, 0)


def project_kernel(w_ref, *refs):
    project_into(w_ref, 0, jnp.concatenate([r[...] for r in refs[:-1]], axis=0), refs[-1])


def project(weights, blocks):
    rows = sum(b.shape[0] for b in blocks)
    heads = weights.shape[1] // HEAD
    return pl.pallas_call(
        project_kernel,
        out_shape=jax.ShapeDtypeStruct((2, heads, PADDED, rows), BF16),
        in_specs=[VMEM] * (1 + len(blocks)),
        out_specs=VMEM,
        compiler_params=LIMIT,
        cost_estimate=SMALL,
        name="project",
    )(weights, *blocks)


def block_spots(n, rows):
    me = lax.axis_index("seq")
    return [pl.ds(pl.multiple_of((me ^ k) * rows, PADDED), rows) for k in range(n)]


def arrange_kernel(n, ids_ref, *refs):
    pieces, (queries, keys, column) = refs[:-3], refs[-3:]
    heads, rows = queries.shape[0], ids_ref.shape[1] // n
    spot = block_spots(n, rows)
    for b in range(n):
        row = ids_ref[:, b * rows : (b + 1) * rows].astype(F32)
        column[b * rows : (b + 1) * rows, :] = jnp.broadcast_to(row, (PADDED, rows)).T
    k = 0
    for piece in pieces:
        for at in range(0, piece.shape[3], rows):
            for h in range(heads):
                queries[h, :, spot[k]] = piece[0, h, :, at : at + rows]
                keys[h, spot[k], :] = piece[1, h, :, at : at + rows].astype(F32).T.astype(BF16)
            k += 1


def arrange(ids, pieces, n):
    heads, total = pieces[0].shape[1], ids.shape[1]
    return pl.pallas_call(
        functools.partial(arrange_kernel, n),
        out_shape=[
            jax.ShapeDtypeStruct((heads, PADDED, total), BF16),
            jax.ShapeDtypeStruct((heads, total, PADDED), BF16),
            jax.ShapeDtypeStruct((total, PADDED), F32),
        ],
        in_specs=[VMEM] * (1 + len(pieces)),
        out_specs=[VMEM] * 3,
        compiler_params=LIMIT,
        cost_estimate=SMALL,
        name="arrange",
    )(ids, *pieces)


def attention_kernel(n, ids_ref, w_ref, column, *refs):
    last, (out_ref, queries, keys) = refs[:-5], refs[-3:]
    heads, total = out_ref.shape[:2]
    rows = total // n
    reach = total // 4 // rows
    frames = jnp.concatenate([r[...] for r in last], axis=0)
    spot = block_spots(n, rows)
    group = 2 if heads % 2 == 0 else 1
    for first in range(0, heads, group):
        own = [
            lax.dot_general(
                w_ref[t, first * HEAD : (first + group) * HEAD, :],
                frames,
                (((1,), (1,)), ((), ())),
                preferred_element_type=F32,
            )
            for t in range(2)
        ]
        for h in range(group):
            queries[first + h, :, spot[n - 1]] = padded_head(own[0], h)
            keys[first + h, spot[n - 1], :] = padded_head(own[1], h).astype(F32).T.astype(BF16)
        for h in range(first, first + group):
            for b in range(n):
                low, high = max(0, b - reach), min(n, b + reach + 1)
                scores = jnp.dot(
                    keys[h, low * rows : high * rows, :],
                    queries[h, :, b * rows : (b + 1) * rows],
                    preferred_element_type=F32,
                )
                same = column[low * rows : high * rows, :] == ids_ref[:, b * rows : (b + 1) * rows].astype(F32)
                scores = jnp.where(same, scores * HEAD**-0.5, -1e30)
                exponent = jnp.exp(scores - jnp.max(scores, axis=0, keepdims=True))
                inverse = 1.0 / jnp.sum(exponent, axis=0, keepdims=True)
                weights = (exponent * inverse).astype(BF16)
                for c in range(n):
                    if low <= c < high:
                        value = weights[(c - low) * rows : (c - low + 1) * rows]
                    else:
                        value = jnp.zeros((rows, rows), BF16)
                    out_ref[h, spot[c], spot[b]] = value


def attention_weights(ids, weights, pieces, last, n):
    heads, total = weights.shape[1] // HEAD, ids.shape[1]
    queries, keys, column = arrange(ids, pieces, n)
    out, _, _ = pl.pallas_call(
        functools.partial(attention_kernel, n),
        out_shape=[
            jax.ShapeDtypeStruct((heads, total, total), BF16),
            jax.ShapeDtypeStruct(queries.shape, BF16),
            jax.ShapeDtypeStruct(keys.shape, BF16),
        ],
        in_specs=[VMEM] * (5 + len(last)),
        out_specs=[VMEM] * 3,
        input_output_aliases={3 + len(last): 1, 4 + len(last): 2},
        compiler_params=LIMIT,
        cost_estimate=SMALL,
        name="attention_weights",
    )(ids, weights, column, *last, queries, keys)
    return out


def rows_times(values_ref, mine, blocks, start, cut):
    half = values_ref.shape[0] // 2
    core = core_index()
    at = half * (core if mine else 1 - core)
    if half % 16 == 0:
        values = values_ref[pl.ds(pl.multiple_of(at, 16), half), :]
    else:
        values = values_ref[...].astype(F32)
        values = jnp.where(at == 0, values[:half], values[half:]).astype(BF16)
    frames = jnp.concatenate([b[:, start : start + cut] for b in blocks], axis=0)
    return jnp.dot(values, frames, preferred_element_type=F32).astype(BF16)


def first_gradient_kernel(n, cut, weights_ref, *refs):
    cots, blocks, (values_ref, theirs) = refs[:n], refs[n:-2], refs[-2:]
    upstream = jnp.concatenate([c[...] for c in cots], axis=1).astype(F32)
    rows = []
    for h in range(weights_ref.shape[0]):
        rows.append(
            lax.dot_general(
                padded_head(upstream, h), weights_ref[h], (((1,), (1,)), ((), ())), preferred_element_type=F32
            )[:HEAD]
        )
    values_ref[...] = jnp.concatenate(rows, axis=0).astype(BF16)
    theirs[...] = rows_times(values_ref, False, blocks, 0, cut)


def next_gradient_kernel(values_ref, *refs):
    outs, blocks = refs[1 - 2 * len(CUTS) :], refs[: 1 - 2 * len(CUTS)]
    start = 0
    for i, cut in enumerate(CUTS):
        for mine in (False, True) if i else (True,):
            outs[2 * i - 1 + mine][...] = rows_times(values_ref, mine, blocks, start, cut)
        start += cut


def gradient(weights, cots, blocks):
    width, total, model = cots[0].shape[0], weights.shape[1], blocks[0].shape[1]

    def shape(cut):
        return jax.ShapeDtypeStruct((width // 2, cut), BF16)

    values, first = pl.pallas_call(
        functools.partial(first_gradient_kernel, len(cots), CUTS[0]),
        out_shape=[jax.ShapeDtypeStruct((width, total), BF16), shape(CUTS[0])],
        in_specs=[VMEM] * (1 + len(cots) + len(blocks)),
        out_specs=[VMEM] * 2,
        compiler_params=LIMIT,
        cost_estimate=SMALL,
        name="first_gradient",
    )(weights, *cots, *blocks)
    outs = pl.pallas_call(
        next_gradient_kernel,
        out_shape=[shape(CUTS[0])] + [shape(cut) for cut in CUTS[1:] for _ in range(2)],
        in_specs=[VMEM] * (1 + len(blocks)),
        out_specs=[VMEM] * (2 * len(CUTS) - 1),
        compiler_params=LIMIT,
        cost_estimate=pl.CostEstimate(
            flops=4 * width * total * model, bytes_accessed=2 * total * model, transcendentals=0
        ),
        name="next_gradient",
    )(values, *blocks)
    outs = [first] + list(outs)
    return list(zip(outs[::2], outs[1::2]))


def context_kernel(n, weights_ref, w_ref, *refs):
    blocks, outs, values = refs[: -n - 1], refs[-n - 1 : -1], refs[-1]
    project_into(w_ref, 2, jnp.concatenate([r[...] for r in blocks], axis=0), values)
    rows = outs[0].shape[1]
    found = [
        jnp.dot(values[0, h], weights_ref[h], preferred_element_type=F32)[:HEAD]
        for h in range(weights_ref.shape[0])
    ]
    stacked = jnp.concatenate(found, axis=0)
    for k, out in enumerate(outs):
        out[...] = stacked[:, k * rows : (k + 1) * rows].astype(BF16)


def contexts_of(weights, projections, blocks, n):
    heads, total = weights.shape[:2]
    return pl.pallas_call(
        functools.partial(context_kernel, n),
        out_shape=[jax.ShapeDtypeStruct((heads * HEAD, total // n), BF16)] * n,
        in_specs=[VMEM] * (2 + len(blocks)),
        out_specs=[VMEM] * n,
        scratch_shapes=[pltpu.VMEM((1, heads, PADDED, total), BF16)],
        compiler_params=LIMIT,
        cost_estimate=SMALL,
        name="contexts",
    )(weights, projections, *blocks)


def assemble_kernel(*refs):
    n = len(refs) - 3
    out, token, turned = refs[n:]
    width, me = refs[0].shape[0], lax.axis_index("seq")
    for k in range(n):
        start = pl.multiple_of((me ^ k) * width, 8)
        turned[pl.ds(start, width), :] = refs[k][...].astype(F32)
    out[...] = turned[...].T.astype(BF16)
    token[...] = jnp.zeros_like(token)


def assemble_context(pieces):
    n, (width, rows) = len(pieces), pieces[0].shape
    return pl.pallas_call(
        assemble_kernel,
        out_shape=[jax.ShapeDtypeStruct((rows, n * width), BF16), jax.ShapeDtypeStruct((8, PADDED), F32)],
        in_specs=[VMEM] * n,
        out_specs=[VMEM] * 2,
        scratch_shapes=[pltpu.VMEM((n * width, rows), F32)],
        compiler_params=LIMIT,
        cost_estimate=LARGE,
        name="assemble_context",
    )(*pieces)


def final_kernel(places, start, scale, marked, *refs):
    pieces, (scratch, sems) = refs[: len(places)], refs[-2:]
    out_ref = refs[-4] if marked else refs[-3]
    rows, cut = pieces[0].shape
    place = 2 * core_index() + line_bit()
    copies = []
    for i, (k, piece) in enumerate(zip(places, pieces)):
        at = pl.multiple_of((place ^ k) * rows, 8)
        if len(places) == 4:
            scratch[pl.ds(at, rows), :] = piece[...].astype(F32) * scale
        else:
            scratch[i * rows : (i + 1) * rows, :] = piece[...].astype(F32) * scale
            copies.append(
                pltpu.make_async_copy(
                    scratch.at[pl.ds(i * rows, rows)],
                    out_ref.at[pl.ds(at, rows), pl.ds(start, cut)],
                    sems.at[i],
                )
            )
            copies[-1].start()
    if not copies:
        copies = [pltpu.make_async_copy(scratch, out_ref.at[:, pl.ds(start, cut)], sems.at[0])]
        copies[0].start()
    if marked:
        refs[-3][...] = jnp.zeros_like(refs[-3])
    for copy in copies:
        copy.wait()


def final(places, pieces, start, scale, model, out, marked):
    rows, cut = pieces[0].shape
    earlier = [] if out is None else [out]
    return pl.pallas_call(
        functools.partial(final_kernel, places, start, scale, marked),
        out_shape=[jax.ShapeDtypeStruct((4 * rows, model), F32)] + [jax.ShapeDtypeStruct((8, PADDED), F32)] * marked,
        in_specs=[VMEM] * len(pieces) + [HBM] * len(earlier),
        out_specs=[HBM] + [VMEM] * marked,
        scratch_shapes=[pltpu.VMEM((len(pieces) * rows, cut), F32), pltpu.SemaphoreType.DMA((len(pieces),))],
        input_output_aliases={len(pieces): 0} if earlier else {},
        compiler_params=LIMIT,
        cost_estimate=SMALL,
        name="final",
    )(*pieces, *earlier)


def add_kernel(a_ref, b_ref, *refs):
    refs[-1][...] = (a_ref[...].astype(F32) + b_ref[...].astype(F32)).astype(BF16)


def add(a, b, *after):
    return pl.pallas_call(
        add_kernel,
        out_shape=jax.ShapeDtypeStruct(a.shape, BF16),
        in_specs=[VMEM, VMEM] + [ANY] * len(after),
        out_specs=VMEM,
        compiler_params=LIMIT,
        cost_estimate=SMALL,
        name="add",
    )(a, b, *after)


def split_sum_kernel(a_ref, b_ref, *refs):
    sent, kept = refs[-2:]
    total = a_ref[...].astype(F32) + b_ref[...].astype(F32)
    half = sent.shape[0]
    low = line_bit() == 0
    sent[...] = jnp.where(low, total[half:], total[:half]).astype(BF16)
    kept[...] = jnp.where(low, total[:half], total[half:]).astype(BF16)


def split_sum(a, b, *after):
    rows, columns = a.shape
    return pl.pallas_call(
        split_sum_kernel,
        out_shape=[jax.ShapeDtypeStruct((rows // 2, columns), BF16)] * 2,
        in_specs=[VMEM, VMEM] + [ANY] * len(after),
        out_specs=[VMEM] * 2,
        compiler_params=LIMIT,
        cost_estimate=SMALL,
        name="split_sum",
    )(a, b, *after)


def body(features, segment_ids, projections, cotangent):
    n, count = lax.axis_size("seq"), lax.axis_size("dp")
    model, width = features.shape[2], projections.shape[1]
    scale = 1.0 / count
    shares = cotangent_shares(cotangent[0], n)

    def meanwhile(own):
        return [project(projections, own), shares[0]]

    blocks, (own_piece, _) = gather_blocks(features[0], "seq", meanwhile)

    def flat(some):
        return [part for block in some for part in block]

    pieces = [own_piece]
    if n > 2:
        pieces.append(project(projections, flat(blocks[1 : n - 1])))
    sent = gate(shares[1:], flat(blocks[1:3])[1:3])
    cots = [shares[0]] + [swap(share, "seq", k + 1) for k, share in enumerate(sent)]
    weights = attention_weights(segment_ids, projections, pieces, flat(blocks[n - 1 :]), n)
    contexts = contexts_of(weights, projections, flat(blocks), n)
    parts, split = [], []
    for i, (theirs, mine) in enumerate(gradient(weights, cots, flat(blocks))):
        after = [] if not split else [split[0][0], contexts[0]] if i < 2 else parts[:1]
        split.append(split_sum(mine, swap(theirs, "dp", 1), *after))
        sent, own = split[-1]
        passed = swap(sent, "dp", 2)
        parts.append(add(own, passed, *(parts[-1:] or contexts[:1])))

    moved = gate(contexts[1:], parts[1:2])
    received = [contexts[0]] + [swap(moved[k - 1], "seq", k) for k in range(1, n)]
    context, context_token = assemble_context(received)
    masks = [1 << b for b in range(2, count.bit_length() - 1)]
    aligned = width % 32 == 0
    value_grad, start, sums, tokens = None, 0, [], []
    for i, total in enumerate(parts):
        last = i == len(parts) - 1
        for mask in masks:
            got = swap(total, "dp", mask)
            wait = []
            if mask == masks[-1]:
                (got,) = gate([got], [], GATES[i])
                wait = [sums[-1][0]] if sums else parts[-1:]
                wait += [context_token] + sums[0][1:2] if last and sums else []
            total = add(total, got, *wait)
        got = swap(total, "dp", 2)
        if last and tokens:
            (got,) = gate([got], tokens[:1])
        four = [total, got, swap(total, "dp", 1), swap(got, "dp", 1)]
        sums.append(four)
        if aligned:
            value_grad, *token = final((0, 1, 2, 3), four, start, scale, model, value_grad, not tokens)
            tokens += token
        start += total.shape[1]
    if not aligned:
        chunks = []
        for kept, got, far_kept, far_got in sums:
            low = line_bit() == 0
            near = jnp.where(low, jnp.concatenate([kept, got]), jnp.concatenate([got, kept]))
            far = jnp.where(low, jnp.concatenate([far_kept, far_got]), jnp.concatenate([far_got, far_kept]))
            chunks.append(jnp.where(core_index() == 0, jnp.concatenate([near, far]), jnp.concatenate([far, near])))
        value_grad = jnp.concatenate(chunks, axis=1).astype(F32) * scale
    return context[None], value_grad


def solution(mesh):
    in_specs = (P("dp", "seq", None), P("dp", None), P(None, "seq", None), P("dp", "seq", None))
    out_specs = (P("dp", "seq", None), P("seq", None))
    return jax.shard_map(body, mesh=mesh, in_specs=in_specs, out_specs=out_specs, check_vma=False)
```

```python
import functools

import jax
import jax.numpy as jnp
from jax import lax
from jax.experimental import pallas as pl
from jax.experimental.pallas import tpu as pltpu
from jax.sharding import PartitionSpec as P

HEAD = 120
PADDED = 128
BF16 = jnp.bfloat16
F32 = jnp.float32
VMEM = pl.BlockSpec(memory_space=pltpu.VMEM)
ANY = pl.BlockSpec(memory_space=pl.ANY)
HBM = pl.BlockSpec(memory_space=pltpu.HBM)
LIMIT = pltpu.CompilerParams(vmem_limit_bytes=12 * 1024 * 1024)
SMALL = pl.CostEstimate(flops=1000, bytes_accessed=1000, transcendentals=0)
def slow(work):
    return pl.CostEstimate(flops=int(work * 1e9), bytes_accessed=int(work * 2e6), transcendentals=0)


LARGE = slow(2)
GATES = (slow(2.6), slow(1), slow(0))
CUTS = (640, 640, 640)


def core_index():
    return lax.axis_index("dp") % 2


def line_bit():
    return lax.axis_index("dp") // 2 % 2


def swap(array, axis, mask):
    return lax.ppermute(array, axis, [(i, i ^ mask) for i in range(lax.axis_size(axis))])


def halves_kernel(x_ref, top_ref, bottom_ref):
    half = top_ref.shape[0]
    top_ref[...] = x_ref[:half]
    bottom_ref[...] = x_ref[half:]


def halves(block):
    rows, model = block.shape
    return pl.pallas_call(
        halves_kernel,
        out_shape=[jax.ShapeDtypeStruct((rows // 2, model), BF16)] * 2,
        in_specs=[VMEM],
        out_specs=[VMEM] * 2,
        compiler_params=LIMIT,
        cost_estimate=SMALL,
        name="halves",
    )(block)


def gate(arrays, after, cost=SMALL):
    return pl.pallas_call(
        lambda *refs: None,
        out_shape=[jax.ShapeDtypeStruct(a.shape, a.dtype) for a in arrays],
        in_specs=[VMEM] * len(arrays) + [ANY] * len(after),
        out_specs=[VMEM] * len(arrays),
        input_output_aliases={i: i for i in range(len(arrays))},
        compiler_params=LIMIT,
        cost_estimate=cost,
        name="gate",
    )(*arrays, *after)


def gather_blocks(block, axis, meanwhile):
    n = lax.axis_size(axis)
    if n != 4:
        return [[block]] + [[swap(block, axis, k)] for k in range(1, n)], meanwhile([block])
    top, bottom = halves(block)
    made = meanwhile([top, bottom])
    top_x, bottom_y = swap(top, axis, 1), swap(bottom, axis, 2)
    (top_x,), (bottom_y,) = gate([top_x], made), gate([bottom_y], made)
    bottom_x, top_y = swap(bottom, axis, 1), swap(top, axis, 2)
    top_xy, bottom_xy = swap(top_x, axis, 2), swap(bottom_y, axis, 1)
    return [[top, bottom], [top_x, bottom_x], [top_y, bottom_y], [top_xy, bottom_xy]], made


def padded_head(rows, h):
    own = rows[h * HEAD : (h + 1) * HEAD]
    zeros = jnp.zeros((PADDED - HEAD, rows.shape[1]), F32)
    return jnp.concatenate([own, zeros], axis=0).astype(BF16)


def shares_kernel(cot_ref, *refs):
    outs, turned = refs[:-1], refs[-1]
    turned[...] = cot_ref[...].astype(F32).T
    width, me = outs[0].shape[0], lax.axis_index("seq")
    for k, out in enumerate(outs):
        start = pl.multiple_of((me ^ k) * width, 8)
        out[...] = turned[pl.ds(start, width), :].astype(BF16)


def cotangent_shares(cotangent, n):
    rows, model = cotangent.shape
    return pl.pallas_call(
        shares_kernel,
        out_shape=[jax.ShapeDtypeStruct((model // n, rows), BF16)] * n,
        in_specs=[VMEM],
        out_specs=[VMEM] * n,
        scratch_shapes=[pltpu.VMEM((model, rows), F32)],
        compiler_params=LIMIT,
        cost_estimate=SMALL,
        name="cotangent_shares",
    )(cotangent)


def project_into(w_ref, first, frames, out_ref):
    count, heads = out_ref.shape[:2]

    def one(t, carry):
        rows = lax.dot_general(
            w_ref[first + t], frames, (((1,), (1,)), ((), ())), preferred_element_type=F32
        )
        for h in range(heads):
            out_ref[t, h] = padded_head(rows, h)
        return carry

    lax.fori_loop(0, count, one, 0)


def project_kernel(w_ref, *refs):
    project_into(w_ref, 0, jnp.concatenate([r[...] for r in refs[:-1]], axis=0), refs[-1])


def project(weights, blocks):
    rows = sum(b.shape[0] for b in blocks)
    heads = weights.shape[1] // HEAD
    return pl.pallas_call(
        project_kernel,
        out_shape=jax.ShapeDtypeStruct((2, heads, PADDED, rows), BF16),
        in_specs=[VMEM] * (1 + len(blocks)),
        out_specs=VMEM,
        compiler_params=LIMIT,
        cost_estimate=SMALL,
        name="project",
    )(weights, *blocks)


def block_spots(n, rows):
    me = lax.axis_index("seq")
    return [pl.ds(pl.multiple_of((me ^ k) * rows, PADDED), rows) for k in range(n)]


def arrange_kernel(n, ids_ref, *refs):
    pieces, (queries, keys, column) = refs[:-3], refs[-3:]
    heads, rows = queries.shape[0], ids_ref.shape[1] // n
    spot = block_spots(n, rows)
    for b in range(n):
        row = ids_ref[:, b * rows : (b + 1) * rows].astype(F32)
        column[b * rows : (b + 1) * rows, :] = jnp.broadcast_to(row, (PADDED, rows)).T
    k = 0
    for piece in pieces:
        for at in range(0, piece.shape[3], rows):
            for h in range(heads):
                queries[h, :, spot[k]] = piece[0, h, :, at : at + rows]
                keys[h, spot[k], :] = piece[1, h, :, at : at + rows].astype(F32).T.astype(BF16)
            k += 1


def arrange(ids, pieces, n):
    heads, total = pieces[0].shape[1], ids.shape[1]
    return pl.pallas_call(
        functools.partial(arrange_kernel, n),
        out_shape=[
            jax.ShapeDtypeStruct((heads, PADDED, total), BF16),
            jax.ShapeDtypeStruct((heads, total, PADDED), BF16),
            jax.ShapeDtypeStruct((total, PADDED), F32),
        ],
        in_specs=[VMEM] * (1 + len(pieces)),
        out_specs=[VMEM] * 3,
        compiler_params=LIMIT,
        cost_estimate=SMALL,
        name="arrange",
    )(ids, *pieces)


def attention_kernel(n, ids_ref, w_ref, column, *refs):
    last, (out_ref, queries, keys) = refs[:-5], refs[-3:]
    heads, total = out_ref.shape[:2]
    rows = total // n
    reach = total // 4 // rows
    frames = jnp.concatenate([r[...] for r in last], axis=0)
    spot = block_spots(n, rows)
    group = 2 if heads % 2 == 0 else 1
    for first in range(0, heads, group):
        own = [
            lax.dot_general(
                w_ref[t, first * HEAD : (first + group) * HEAD, :],
                frames,
                (((1,), (1,)), ((), ())),
                preferred_element_type=F32,
            )
            for t in range(2)
        ]
        for h in range(group):
            queries[first + h, :, spot[n - 1]] = padded_head(own[0], h)
            keys[first + h, spot[n - 1], :] = padded_head(own[1], h).astype(F32).T.astype(BF16)
        for h in range(first, first + group):
            for b in range(n):
                low, high = max(0, b - reach), min(n, b + reach + 1)
                scores = jnp.dot(
                    keys[h, low * rows : high * rows, :],
                    queries[h, :, b * rows : (b + 1) * rows],
                    preferred_element_type=F32,
                )
                same = column[low * rows : high * rows, :] == ids_ref[:, b * rows : (b + 1) * rows].astype(F32)
                scores = jnp.where(same, scores * HEAD**-0.5, -1e30)
                exponent = jnp.exp(scores - jnp.max(scores, axis=0, keepdims=True))
                inverse = 1.0 / jnp.sum(exponent, axis=0, keepdims=True)
                weights = (exponent * inverse).astype(BF16)
                for c in range(n):
                    if low <= c < high:
                        value = weights[(c - low) * rows : (c - low + 1) * rows]
                    else:
                        value = jnp.zeros((rows, rows), BF16)
                    out_ref[h, spot[c], spot[b]] = value


def attention_weights(ids, weights, pieces, last, n):
    heads, total = weights.shape[1] // HEAD, ids.shape[1]
    queries, keys, column = arrange(ids, pieces, n)
    out, _, _ = pl.pallas_call(
        functools.partial(attention_kernel, n),
        out_shape=[
            jax.ShapeDtypeStruct((heads, total, total), BF16),
            jax.ShapeDtypeStruct(queries.shape, BF16),
            jax.ShapeDtypeStruct(keys.shape, BF16),
        ],
        in_specs=[VMEM] * (5 + len(last)),
        out_specs=[VMEM] * 3,
        input_output_aliases={3 + len(last): 1, 4 + len(last): 2},
        compiler_params=LIMIT,
        cost_estimate=SMALL,
        name="attention_weights",
    )(ids, weights, column, *last, queries, keys)
    return out


def rows_times(values_ref, mine, blocks, start, cut):
    half = values_ref.shape[0] // 2
    core = core_index()
    at = half * (core if mine else 1 - core)
    if half % 16 == 0:
        values = values_ref[pl.ds(pl.multiple_of(at, 16), half), :]
    else:
        values = values_ref[...].astype(F32)
        values = jnp.where(at == 0, values[:half], values[half:]).astype(BF16)
    frames = jnp.concatenate([b[:, start : start + cut] for b in blocks], axis=0)
    return jnp.dot(values, frames, preferred_element_type=F32).astype(BF16)


def first_gradient_kernel(n, cut, weights_ref, *refs):
    cots, blocks, (values_ref, theirs) = refs[:n], refs[n:-2], refs[-2:]
    upstream = jnp.concatenate([c[...] for c in cots], axis=1).astype(F32)
    rows = []
    for h in range(weights_ref.shape[0]):
        rows.append(
            lax.dot_general(
                padded_head(upstream, h), weights_ref[h], (((1,), (1,)), ((), ())), preferred_element_type=F32
            )[:HEAD]
        )
    values_ref[...] = jnp.concatenate(rows, axis=0).astype(BF16)
    theirs[...] = rows_times(values_ref, False, blocks, 0, cut)


def next_gradient_kernel(values_ref, *refs):
    outs, blocks = refs[1 - 2 * len(CUTS) :], refs[: 1 - 2 * len(CUTS)]
    start = 0
    for i, cut in enumerate(CUTS):
        for mine in (False, True) if i else (True,):
            outs[2 * i - 1 + mine][...] = rows_times(values_ref, mine, blocks, start, cut)
        start += cut


def gradient(weights, cots, blocks):
    width, total, model = cots[0].shape[0], weights.shape[1], blocks[0].shape[1]

    def shape(cut):
        return jax.ShapeDtypeStruct((width // 2, cut), BF16)

    values, first = pl.pallas_call(
        functools.partial(first_gradient_kernel, len(cots), CUTS[0]),
        out_shape=[jax.ShapeDtypeStruct((width, total), BF16), shape(CUTS[0])],
        in_specs=[VMEM] * (1 + len(cots) + len(blocks)),
        out_specs=[VMEM] * 2,
        compiler_params=LIMIT,
        cost_estimate=SMALL,
        name="first_gradient",
    )(weights, *cots, *blocks)
    outs = pl.pallas_call(
        next_gradient_kernel,
        out_shape=[shape(CUTS[0])] + [shape(cut) for cut in CUTS[1:] for _ in range(2)],
        in_specs=[VMEM] * (1 + len(blocks)),
        out_specs=[VMEM] * (2 * len(CUTS) - 1),
        compiler_params=LIMIT,
        cost_estimate=pl.CostEstimate(
            flops=4 * width * total * model, bytes_accessed=2 * total * model, transcendentals=0
        ),
        name="next_gradient",
    )(values, *blocks)
    outs = [first] + list(outs)
    return list(zip(outs[::2], outs[1::2]))


def context_kernel(n, weights_ref, w_ref, *refs):
    blocks, outs, values = refs[: -n - 1], refs[-n - 1 : -1], refs[-1]
    project_into(w_ref, 2, jnp.concatenate([r[...] for r in blocks], axis=0), values)
    rows = outs[0].shape[1]
    found = [
        jnp.dot(values[0, h], weights_ref[h], preferred_element_type=F32)[:HEAD]
        for h in range(weights_ref.shape[0])
    ]
    stacked = jnp.concatenate(found, axis=0)
    for k, out in enumerate(outs):
        out[...] = stacked[:, k * rows : (k + 1) * rows].astype(BF16)


def contexts_of(weights, projections, blocks, n):
    heads, total = weights.shape[:2]
    return pl.pallas_call(
        functools.partial(context_kernel, n),
        out_shape=[jax.ShapeDtypeStruct((heads * HEAD, total // n), BF16)] * n,
        in_specs=[VMEM] * (2 + len(blocks)),
        out_specs=[VMEM] * n,
        scratch_shapes=[pltpu.VMEM((1, heads, PADDED, total), BF16)],
        compiler_params=LIMIT,
        cost_estimate=SMALL,
        name="contexts",
    )(weights, projections, *blocks)


def assemble_kernel(*refs):
    n = len(refs) - 3
    out, token, turned = refs[n:]
    width, me = refs[0].shape[0], lax.axis_index("seq")
    for k in range(n):
        start = pl.multiple_of((me ^ k) * width, 8)
        turned[pl.ds(start, width), :] = refs[k][...].astype(F32)
    out[...] = turned[...].T.astype(BF16)
    token[...] = jnp.zeros_like(token)


def assemble_context(pieces):
    n, (width, rows) = len(pieces), pieces[0].shape
    return pl.pallas_call(
        assemble_kernel,
        out_shape=[jax.ShapeDtypeStruct((rows, n * width), BF16), jax.ShapeDtypeStruct((8, PADDED), F32)],
        in_specs=[VMEM] * n,
        out_specs=[VMEM] * 2,
        scratch_shapes=[pltpu.VMEM((n * width, rows), F32)],
        compiler_params=LIMIT,
        cost_estimate=LARGE,
        name="assemble_context",
    )(*pieces)


def final_kernel(spots, scale, marked, *refs):
    count = sum(len(places) for places, _ in spots)
    pieces, scratches, sems = list(refs[:count]), refs[-1 - len(spots) : -1], refs[-1]
    out_ref = refs[-3 - len(spots)] if marked else refs[-2 - len(spots)]
    place = 2 * core_index() + line_bit()
    copies = []

    def write(source, target):
        copies.append(pltpu.make_async_copy(source, target, sems.at[len(copies)]))
        copies[-1].start()

    for (places, start), scratch in zip(spots, scratches):
        rows, cut = scratch.shape[0] // len(places), scratch.shape[1]
        columns = pl.ds(start, cut)
        for i, k in enumerate(places):
            at = pl.multiple_of((place ^ k) * rows, 8)
            value = pieces.pop(0)[...].astype(F32) * scale
            if len(places) == 4:
                scratch[pl.ds(at, rows), :] = value
            else:
                scratch[i * rows : (i + 1) * rows, :] = value
                write(scratch.at[pl.ds(i * rows, rows)], out_ref.at[pl.ds(at, rows), columns])
        if len(places) == 4:
            write(scratch, out_ref.at[:, columns])
    if marked:
        token = refs[-2 - len(spots)]
        token[...] = jnp.zeros_like(token)
    for copy in copies:
        copy.wait()


def final(parts, scale, model, out, marked):
    spots = [(places, start) for places, start, _ in parts]
    pieces = [piece for _, _, some in parts for piece in some]
    rows = pieces[0].shape[0]
    earlier = [] if out is None else [out]
    return pl.pallas_call(
        functools.partial(final_kernel, spots, scale, marked),
        out_shape=[jax.ShapeDtypeStruct((4 * rows, model), F32)] + [jax.ShapeDtypeStruct((8, PADDED), F32)] * marked,
        in_specs=[VMEM] * len(pieces) + [HBM] * len(earlier),
        out_specs=[HBM] + [VMEM] * marked,
        scratch_shapes=[pltpu.VMEM((len(some) * rows, some[0].shape[1]), F32) for _, _, some in parts]
        + [pltpu.SemaphoreType.DMA((len(pieces),))],
        input_output_aliases={len(pieces): 0} if earlier else {},
        compiler_params=LIMIT,
        cost_estimate=SMALL,
        name="final",
    )(*pieces, *earlier)


def add_kernel(a_ref, b_ref, *refs):
    refs[-1][...] = (a_ref[...].astype(F32) + b_ref[...].astype(F32)).astype(BF16)


def add(a, b, *after):
    return pl.pallas_call(
        add_kernel,
        out_shape=jax.ShapeDtypeStruct(a.shape, BF16),
        in_specs=[VMEM, VMEM] + [ANY] * len(after),
        out_specs=VMEM,
        compiler_params=LIMIT,
        cost_estimate=SMALL,
        name="add",
    )(a, b, *after)


def split_sum_kernel(a_ref, b_ref, *refs):
    sent, kept = refs[-2:]
    total = a_ref[...].astype(F32) + b_ref[...].astype(F32)
    half = sent.shape[0]
    low = line_bit() == 0
    sent[...] = jnp.where(low, total[half:], total[:half]).astype(BF16)
    kept[...] = jnp.where(low, total[:half], total[half:]).astype(BF16)


def split_sum(a, b, *after):
    rows, columns = a.shape
    return pl.pallas_call(
        split_sum_kernel,
        out_shape=[jax.ShapeDtypeStruct((rows // 2, columns), BF16)] * 2,
        in_specs=[VMEM, VMEM] + [ANY] * len(after),
        out_specs=[VMEM] * 2,
        compiler_params=LIMIT,
        cost_estimate=SMALL,
        name="split_sum",
    )(a, b, *after)


def body(features, segment_ids, projections, cotangent):
    n, count = lax.axis_size("seq"), lax.axis_size("dp")
    model, width = features.shape[2], projections.shape[1]
    scale = 1.0 / count
    shares = cotangent_shares(cotangent[0], n)

    def meanwhile(own):
        return [project(projections, own), shares[0]]

    blocks, (own_piece, _) = gather_blocks(features[0], "seq", meanwhile)

    def flat(some):
        return [part for block in some for part in block]

    pieces = [own_piece]
    if n > 2:
        pieces.append(project(projections, flat(blocks[1 : n - 1])))
    sent = gate(shares[1:], flat(blocks[1:3])[1:3])
    cots = [shares[0]] + [swap(share, "seq", k + 1) for k, share in enumerate(sent)]
    weights = attention_weights(segment_ids, projections, pieces, flat(blocks[n - 1 :]), n)
    contexts = contexts_of(weights, projections, flat(blocks), n)
    parts, split = [], []
    for i, (theirs, mine) in enumerate(gradient(weights, cots, flat(blocks))):
        after = [] if not split else [split[0][0], contexts[0]] if i < 2 else parts[:1]
        split.append(split_sum(mine, swap(theirs, "dp", 1), *after))
        sent, own = split[-1]
        passed = swap(sent, "dp", 2)
        parts.append(add(own, passed, *(parts[-1:] or contexts[:1])))

    moved = gate(contexts[1:], parts[1:2])
    received = [contexts[0]] + [swap(moved[k - 1], "seq", k) for k in range(1, n)]
    context, context_token = assemble_context(received)
    masks = [1 << b for b in range(2, count.bit_length() - 1)]
    aligned = width % 32 == 0
    value_grad, start, sums, tokens, left = None, 0, [], [], []
    for i, total in enumerate(parts):
        last = i == len(parts) - 1
        for mask in masks:
            got = swap(total, "dp", mask)
            wait = []
            if mask == masks[-1]:
                (got,) = gate([got], [], GATES[i])
                wait = [sums[-1][0]] if sums else parts[-1:]
                wait += [context_token] + sums[0][1:2] if last and sums else []
            total = add(total, got, *wait)
        got = swap(total, "dp", 2)
        if last and tokens:
            (got,) = gate([got], tokens[:1])
        four = [total, got, swap(total, "dp", 1), swap(got, "dp", 1)]
        sums.append(four)
        if aligned:
            whole = ((0, 1, 2, 3), start, four)
            if not tokens:
                value_grad, *tokens = final([whole], scale, model, value_grad, True)
            elif not last:
                left.append(whole)
            else:
                near = left + [((0, 1, 2), start, four[:3])]
                (value_grad,) = final(near, scale, model, value_grad, False)
                (value_grad,) = final([((3,), start, four[3:])], scale, model, value_grad, False)
        start += total.shape[1]
    if not aligned:
        chunks = []
        for kept, got, far_kept, far_got in sums:
            low = line_bit() == 0
            near = jnp.where(low, jnp.concatenate([kept, got]), jnp.concatenate([got, kept]))
            far = jnp.where(low, jnp.concatenate([far_kept, far_got]), jnp.concatenate([far_got, far_kept]))
            chunks.append(jnp.where(core_index() == 0, jnp.concatenate([near, far]), jnp.concatenate([far, near])))
        value_grad = jnp.concatenate(chunks, axis=1).astype(F32) * scale
    return context[None], value_grad


def solution(mesh):
    in_specs = (P("dp", "seq", None), P("dp", None), P(None, "seq", None), P("dp", "seq", None))
    out_specs = (P("dp", "seq", None), P("seq", None))
    return jax.shard_map(body, mesh=mesh, in_specs=in_specs, out_specs=out_specs, check_vma=False)
```
